512 devices in a mesh: tm: 8 (over y_hi, x), vox: 32 (over z, y_lo), feat: 2 (over core).
Axes of the slice: x: 4, y: 4 (y_hi: 2, y_lo: 2; y = y_hi * 2 + y_lo), z: 16, core: 2. Of those that a mesh axis runs over, the one named last changes fastest.
Arguments:
- design_matrix: bfloat16 [1024, 4096], P(None, ('tm', 'feat')), may hold values from -6 to 6
- measured_signals: bfloat16 [1024, 16384], P('tm', 'vox'), may hold values from -6 to 6
- predictor_group_label: int32 [4096], P('vox'), may hold values from 0 to 3
- shrinkage_weights: float32 [2, 4], replicated, may hold values from 0.1 to 10
- target_shrink_choice: int32 [256], P('vox'), may hold values from 0 to 1
Outputs:
- trailing: float32 [2, 4096, 4096], P(None, ('tm', 'feat'), 'vox')
- right_sides: float32 [4096, 16384], P(('tm', 'feat'), 'vox')
The draws below stay inside these ranges and needn't reach their ends.
All inputs are finite; a program needn't handle non-finite values.
Results may differ from the reference program's by a relative error of at most 0.0003.
Values may be sent and summed in bfloat16 or wider, within the bound.
A program may use at most 64 MiB of HBM per device.

```python
import math
import jax
import jax.numpy as jnp
from jax import lax

P_SIZE = 4096
V = 16384
PREDICTOR_GROUPS = 4
SHRINK_OPTIONS = 2
GROUP = 64
STEPS = 1
TIME = 1024
CB = 128


def plant(values, stream_key, least, top_value):
    extent = values.shape
    index_at = [jax.random.randint(jax.random.fold_in(stream_key, axis), (), 0, extent[axis]) for axis in range(len(extent))]
    values = values.at[tuple(index_at)].set(least)
    longest = extent.index(max(extent))
    index_at[longest] = (index_at[longest] + 1) % extent[longest]
    return values.at[tuple(index_at)].set(top_value)


def block_levels(key, shape, shards, low, largest):
    loudness, own = 1.0, jax.random.fold_in(key, 6)
    for position, parts in shards:
        draws = jnp.exp(jax.random.uniform(jax.random.fold_in(own, position), (parts,), jnp.float32, low / len(shards), largest / len(shards)))
        loudness = loudness * jnp.repeat(draws, shape[position] // parts).reshape([-1 if axis == position else 1 for axis in range(len(shape))])
    return loudness


def bell_draw(stream_key, shape, spread, most, shards=(), held_as=jnp.bfloat16):
    gain = block_levels(stream_key, shape, shards, -0.22, 0.18) if shards else 1.0
    entries = jax.random.normal(stream_key, shape, jnp.float32) * spread * gain
    return jnp.minimum(jnp.maximum(entries, -most), most).astype(held_as)


def setup_inputs(seed: int = 0) -> dict:
    key_list = jax.random.split(jax.random.key(seed), 6)
    return {
        "design_matrix": bell_draw(key_list[0], (TIME, P_SIZE), 1.0, 6.0, ((1, 16),)),
        "measured_signals": bell_draw(key_list[1], (TIME, V), 1.0, 6.0, ((0, 8), (1, 32))),
        "predictor_group_label": plant(jax.random.randint(key_list[2], (P_SIZE,), 0, PREDICTOR_GROUPS), jax.random.fold_in(key_list[2], 1), 0, PREDICTOR_GROUPS - 1).astype(jnp.int32),
        "shrinkage_weights": jnp.clip(jnp.exp(jax.random.uniform(key_list[3], (SHRINK_OPTIONS, PREDICTOR_GROUPS), jnp.float32, math.log(0.1), math.log(10.0))), 0.1, 10.0),
        "target_shrink_choice": plant(jax.random.randint(key_list[4], (V // GROUP,), 0, SHRINK_OPTIONS), jax.random.fold_in(key_list[4], 1), 0, SHRINK_OPTIONS - 1).astype(jnp.int32),
    }


def reference(design_matrix, measured_signals, predictor_group_label, shrinkage_weights, target_shrink_choice):
    gram = jnp.dot(design_matrix.T.astype(jnp.float32), design_matrix.astype(jnp.float32), preferred_element_type=jnp.float32) / TIME
    predictor_shrinkage = shrinkage_weights[:, predictor_group_label]
    system = gram[None, :, :] + jax.vmap(jnp.diag)(predictor_shrinkage)
    sides = jnp.dot(design_matrix.T.astype(jnp.float32), measured_signals.astype(jnp.float32), preferred_element_type=jnp.float32) / math.sqrt(TIME)
    first_ridge = jnp.repeat(target_shrink_choice, GROUP) == 0
    global_rows = jnp.arange(P_SIZE)
    for panel_step in range(STEPS):
        block_start = panel_step * CB
        factor = jnp.linalg.cholesky(system[:, block_start:block_start + CB, block_start:block_start + CB])
        solved = lax.linalg.triangular_solve(factor, system[:, :, block_start:block_start + CB], left_side=False, lower=True, transpose_a=True)
        panel = jnp.where((global_rows >= block_start)[None, :, None], solved, 0.0)
        block_sides = jnp.broadcast_to(sides[block_start:block_start + CB], (SHRINK_OPTIONS, CB, V))
        solutions = lax.linalg.triangular_solve(factor, block_sides, left_side=True, lower=True)
        solved_sides = jnp.where(first_ridge[None, :], solutions[0], solutions[1])
        system = system - jnp.einsum('brk,bck->brc', panel, panel, precision=lax.Precision.HIGHEST)
        update_first = jnp.dot(panel[0], solved_sides, precision=lax.Precision.HIGHEST)
        update_second = jnp.dot(panel[1], solved_sides, precision=lax.Precision.HIGHEST)
        sides = sides - jnp.where(first_ridge[None, :], update_first, update_second)
        sides = sides.at[block_start:block_start + CB].set(solved_sides)
    return (system, sides)
```

```python
import math

import jax
import jax.numpy as jnp
from jax import lax
from jax.experimental import pallas as pl
from jax.experimental.pallas import tpu as pltpu
from jax.sharding import PartitionSpec as P

TIME = 1024
GROUPS = 4
CB = 128
GROUP = 64
CHIPS = 8
OFFSETS = [(dy, dx) for dy in range(2) for dx in range(4)][1:]
MESH = pl.DeviceIdType.MESH


def peer(t, dy, dx):
    y, x = t // 4, t % 4
    return ((y + dy) % 2) * 4 + (x + dx) % 4


def remote(src, dst, send, recv, **where):
    return pltpu.make_async_remote_copy(
        src_ref=src, dst_ref=dst, send_sem=send, recv_sem=recv, device_id=where, device_id_type=MESH
    )


class Spread:
    def __init__(self, buf, t, f, to, fo, sem):
        self.buf, self.t, self.f, self.to, self.fo = buf, t, f, to, fo
        self.scatter, self.scatter_r, self.own, self.own_r, self.ag, self.ag_r, self.sib, self.sib_r = sem
        self.owner = (t == to) & (f == fo)
        self.relay = (t != to) & (f == fo)
        self.side = (t != to) & (f != fo)
        self.owner_side = (t == to) & (f != fo)

    def chunk(self, t):
        return self.buf.at[pl.ds(pl.multiple_of(t * 128, 128), 128), :]

    def c_scatter(self, k):
        p = peer(self.t, *OFFSETS[k])
        c = self.chunk(p)
        return remote(c, c, self.scatter.at[k], self.scatter_r, tm=p)

    def c_scatter_in(self):
        c = self.chunk(self.t)
        return remote(c, c, self.scatter.at[0], self.scatter_r, tm=self.to)

    def c_own(self, k):
        p = peer(self.t, *OFFSETS[k])
        c = self.chunk(self.t)
        return remote(c, c, self.own.at[k], self.own_r, tm=p)

    def c_own_in(self):
        c = self.chunk(self.to)
        return remote(c, c, self.own.at[0], self.own_r, tm=self.to)

    def c_ag(self, k):
        p = peer(self.t, *OFFSETS[k])
        c = self.chunk(self.t)
        return p, remote(c, c, self.ag.at[k], self.ag_r.at[k], tm=p)

    def c_ag_in(self, k):
        dy, dx = OFFSETS[k]
        p = peer(self.t, dy, 4 - dx)
        c = self.chunk(p)
        return p, remote(c, c, self.ag.at[k], self.ag_r.at[k], tm=p)

    def c_sib(self, k, p):
        c = self.chunk(p)
        return remote(c, c, self.sib.at[k], self.sib_r.at[k], feat=1 - self.f)

    def c_whole(self):
        return remote(self.buf, self.buf, self.sib.at[0], self.sib_r.at[0], feat=1 - self.f)

    def start(self):
        @pl.when(self.owner)
        def _():
            for k in range(7):
                self.c_scatter(k).start()
            for k in range(7):
                self.c_own(k).start()
            self.c_whole().start()

    def forward(self):
        @pl.when(self.relay)
        def _():
            self.c_scatter_in().wait_recv()
            for k in range(7):
                p, c = self.c_ag(k)

                @pl.when(p != self.to)
                def _():
                    c.start()

            self.c_sib(7, self.t).start()

    def collect(self):
        @pl.when(self.relay)
        def _():
            for k in range(7):
                p, c = self.c_ag_in(k)

                @pl.when(p != self.to)
                def _():
                    c.wait_recv()

                @pl.when(p == self.to)
                def _():
                    self.c_own_in().wait_recv()

                self.c_sib(k, p).start()

    def finish(self):
        @pl.when(self.owner)
        def _():
            for k in range(7):
                self.c_scatter(k).wait_send()
                self.c_own(k).wait_send()
            self.c_whole().wait_send()

        @pl.when(self.owner_side)
        def _():
            self.c_whole().wait_recv()

        @pl.when(self.relay)
        def _():
            for k in range(7):
                p, c = self.c_ag(k)

                @pl.when(p != self.to)
                def _():
                    c.wait_send()

                q, _c = self.c_ag_in(k)
                self.c_sib(k, q).wait_send()
            self.c_sib(7, self.t).wait_send()

        @pl.when(self.side)
        def _():
            for k in range(7):
                dy, dx = OFFSETS[k]
                self.c_sib(k, peer(self.t, dy, 4 - dx)).wait_recv()
            self.c_sib(7, self.t).wait_recv()


def spread_sems():
    dma = pltpu.SemaphoreType.DMA
    return [dma((7,)), dma, dma((7,)), dma, dma((7,)), dma((7,)), dma((8,)), dma((8,))]


def gather_kernel(a_ref, y_ref, lab_ref, s_ref, c_ref, yall_ref, labs_ref, *sems):
    s_sem, c_sem, rest = sems[:8], sems[8:16], sems[16:]
    ysend, yrecv, bsend, brecv, l1s, l1r, l2s, l2r, l3s, l3r = rest
    t, f, v = lax.axis_index("tm"), lax.axis_index("feat"), lax.axis_index("vox")
    row = t * 2 + f
    first_row, first_vox = row == 0, v == 0

    barrier = pltpu.get_barrier_semaphore()
    for dy, dx in OFFSETS:
        pl.semaphore_signal(barrier, inc=1, device_id={"tm": peer(t, dy, dx)}, device_id_type=MESH)
    pl.semaphore_signal(barrier, inc=1, device_id={"feat": 1 - f}, device_id_type=MESH)

    @pl.when(first_row & (v != 0))
    def _():
        pl.semaphore_signal(
            barrier, inc=1, device_id={"tm": v // 4, "feat": (v // 2) % 2, "vox": 0}, device_id_type=MESH
        )

    @pl.when(first_row)
    def _():
        s_ref[...] = a_ref[:, 0:128]

    to, fo = v // 4, (v // 2) % 2

    @pl.when((t == to) & (f == fo))
    def _():
        c_ref[...] = a_ref[:, pl.ds(pl.multiple_of((v % 2) * 128, 128), 128)]

    yall_ref[pl.ds(pl.multiple_of(t * 128, 128), 128), :] = y_ref[...]

    @pl.when(first_row & first_vox)
    def _():
        labs_ref[...] = lab_ref[...]

    @pl.when(v != 0)
    def _():
        pl.semaphore_wait(barrier, 8)

    @pl.when(first_vox & (row != 0))
    def _():
        pl.semaphore_wait(barrier, 10)

    @pl.when(first_vox & (row == 0))
    def _():
        pl.semaphore_wait(barrier, 9)

    def c_l1(i):
        return remote(lab_ref, labs_ref, l1s.at[i], l1r, tm=0, feat=0, vox=row * 2 + i)

    @pl.when(first_vox)
    def _():
        @pl.when(row != 0)
        def _():
            c_l1(0).start()

        c_l1(1).start()

    spread_s = Spread(s_ref, t, f, 0, 0, s_sem)
    spread_c = Spread(c_ref, t, f, to, fo, c_sem)
    spread_s.start()
    spread_c.start()

    def yblock(q, g):
        return yall_ref.at[pl.ds(pl.multiple_of(q * 128 + g * 64, 64), 64), :]

    def c_y(k):
        b = yblock(t, f)
        return remote(b, b, ysend.at[k], yrecv.at[k], tm=peer(t, *OFFSETS[k]))

    def source(k):
        dy, dx = OFFSETS[k]
        return peer(t, dy, 4 - dx)

    def c_yin(k):
        b = yblock(source(k), f)
        return remote(b, b, ysend.at[k], yrecv.at[k], tm=source(k))

    def c_yout(k):
        b = yblock(source(k), f)
        return remote(b, b, bsend.at[k], brecv.at[k], feat=1 - f)

    def c_yside(k):
        b = yblock(source(k), 1 - f)
        return remote(b, b, bsend.at[k], brecv.at[k], feat=1 - f)

    for k in range(7):
        c_y(k).start()

    def c_l2(k):
        return remote(labs_ref, labs_ref, l2s.at[k], l2r, tm=peer(t, *OFFSETS[k]))

    def c_l2in():
        return remote(labs_ref, labs_ref, l2s.at[0], l2r, tm=0)

    def c_l3():
        return remote(labs_ref, labs_ref, l3s, l3r, feat=1 - f)

    spread_s.forward()
    spread_c.forward()

    @pl.when(first_row)
    def _():
        @pl.when(v != 0)
        def _():
            remote(lab_ref, labs_ref, l1s.at[0], l1r, tm=0, feat=0, vox=0).wait_recv()

        for k in range(7):
            c_l2(k).start()

    @pl.when((f == 0) & (t != 0))
    def _():
        c_l2in().wait_recv()

    @pl.when(f == 0)
    def _():
        c_l3().start()

    spread_s.collect()
    spread_c.collect()
    for k in range(7):
        c_yin(k).wait_recv()
        c_yout(k).start()
    spread_s.finish()
    spread_c.finish()

    @pl.when(f == 1)
    def _():
        c_l3().wait_recv()

    @pl.when(f == 0)
    def _():
        c_l3().wait_send()

    @pl.when(first_row)
    def _():
        for k in range(7):
            c_l2(k).wait_send()

    @pl.when(first_vox)
    def _():
        @pl.when(row != 0)
        def _():
            c_l1(0).wait_send()

        c_l1(1).wait_send()

    for k in range(7):
        c_y(k).wait_send()
        c_yout(k).wait_send()
        c_yside(k).wait_recv()


def gather(a, y, lab):
    dma = pltpu.SemaphoreType.DMA
    vmem = pl.BlockSpec(memory_space=pltpu.VMEM)
    voxels = y.shape[1]
    return pl.pallas_call(
        gather_kernel,
        out_shape=[
            jax.ShapeDtypeStruct((TIME, CB), jnp.bfloat16),
            jax.ShapeDtypeStruct((TIME, CB), jnp.bfloat16),
            jax.ShapeDtypeStruct((TIME, voxels), jnp.bfloat16),
            jax.ShapeDtypeStruct((1, CB), jnp.int32),
        ],
        in_specs=[vmem] * 3,
        out_specs=[vmem] * 4,
        scratch_shapes=spread_sems()
        + spread_sems()
        + [dma((7,)), dma((7,)), dma((7,)), dma((7,)), dma((2,)), dma, dma((7,)), dma, dma, dma],
        compiler_params=pltpu.CompilerParams(
            collective_id=0, has_side_effects=True, vmem_limit_bytes=16 << 20
        ),
        name="gather",
    )(a, y, lab)


def inverse_factor(matrix):
    n = matrix.shape[0]
    count = n // 8
    sub = lax.broadcasted_iota(jnp.int32, (8, n), 0)
    lane = lax.broadcasted_iota(jnp.int32, (8, n), 1)
    rows = [matrix[8 * i : 8 * i + 8, :] for i in range(count)]
    out = []
    for j in range(count):
        inside = (lane >= 8 * j) & (lane < 8 * j + 8)
        eye = jnp.where(lane == 8 * j + sub, 1.0, 0.0)
        cols = {}
        for i in range(j, count):
            r = rows[i]
            cols[i] = [jnp.broadcast_to(r[:, 8 * j + p : 8 * j + p + 1], (8, n)) for p in range(8)]
            rows[i] = jnp.where(inside, eye if i == j else 0.0, r)
        scale = jnp.zeros((8, n), jnp.float32)
        for p in range(8):
            crow = [jnp.broadcast_to(cols[j][k][p : p + 1, :], (8, n)) if k >= p else None for k in range(8)]
            rrow = jnp.broadcast_to(rows[j][p : p + 1, :], (8, n))
            inv = 1.0 / crow[p]
            scale = jnp.where(sub == p, lax.rsqrt(crow[p]), scale)
            for i in range(j, count):
                factor = cols[i][p] * inv
                if i == j:
                    factor = jnp.where(sub > p, factor, 0.0)
                rows[i] = rows[i] - factor * rrow
                for k in range(p + 1, 8):
                    cols[i][k] = cols[i][k] - factor * crow[k]
        out.append(jnp.where(lane <= 8 * j + sub, rows[j] * scale, 0.0))
    return out


def tdot(a, b):
    return lax.dot_general(a, b, (((0,), (0,)), ((), ())), preferred_element_type=jnp.float32)


def fdot(a, b):
    return jnp.dot(a, b, precision=lax.Precision.HIGHEST, preferred_element_type=jnp.float32)


def solve_kernel(
    weights_ref, choice_ref, a_ref, s_ref, c_ref, y_ref, labs_ref, labc_ref, trail_ref, sides_ref, inv_ref
):
    t, f, v = lax.axis_index("tm"), lax.axis_index("feat"), lax.axis_index("vox")
    row = t * 2 + f
    rows, voxels = sides_ref.shape
    s = s_ref[...]
    c = c_ref[...]
    y = y_ref[...]
    a = a_ref[...]

    def penalty(r, lab):
        total = jnp.zeros(lab.shape, jnp.float32)
        for g in range(GROUPS):
            total = jnp.where(lab == g, weights_ref[r, g], total)
        return total

    i_sub = lax.broadcasted_iota(jnp.int32, (CB, CB), 0)
    i_lane = lax.broadcasted_iota(jnp.int32, (CB, CB), 1)
    eye = i_sub == i_lane
    gss = tdot(s, s) * (1.0 / TIME)
    for r in range(2):
        pen = jnp.broadcast_to(penalty(r, labs_ref[...]), (CB, CB))
        for j, block in enumerate(inverse_factor(gss + jnp.where(eye, pen, 0.0))):
            inv_ref[r, 8 * j : 8 * j + 8, :] = block

    r_sub = lax.broadcasted_iota(jnp.int32, (rows, CB), 0) + row * rows
    r_lane = lax.broadcasted_iota(jnp.int32, (rows, CB), 1)
    grs = tdot(a, s) * (1.0 / TIME)
    grc = tdot(a, c) * (1.0 / TIME)
    gsc = tdot(s, c) * (1.0 / TIME)
    side = tdot(a, y) * (1.0 / math.sqrt(TIME))
    sside = tdot(s, y) * (1.0 / math.sqrt(TIME))

    group = lax.broadcasted_iota(jnp.int32, (1, voxels), 1) // GROUP
    ridge = jnp.zeros((1, voxels), jnp.int32)
    for g in range(voxels // GROUP):
        ridge = jnp.where(group == g, choice_ref[g], ridge)

    panels, solved = [], []
    for r in range(2):
        inv = inv_ref[r]
        pen_s = jnp.broadcast_to(penalty(r, labs_ref[...]), (rows, CB))
        pen_c = jnp.broadcast_to(penalty(r, labc_ref[...]), (rows, CB))
        grs_r = grs + jnp.where(r_sub == r_lane, pen_s, 0.0)
        gsc_r = gsc + jnp.where(eye & (v == 0), pen_c[:CB], 0.0)
        panel = lax.dot_general(
            grs_r, inv, (((1,), (1,)), ((), ())), precision=lax.Precision.HIGHEST,
            preferred_element_type=jnp.float32,
        )
        partner = fdot(inv, gsc_r)
        system = grc + jnp.where(r_sub == r_lane + v * CB, pen_c, 0.0)
        trail_ref[r] = system - fdot(panel, partner)
        panels.append(panel)
        solved.append(jnp.where(ridge == r, fdot(inv, sside), 0.0))
    update = fdot(panels[0], solved[0]) + fdot(panels[1], solved[1])
    sides_ref[...] = side - update

    @pl.when(row == 0)
    def _():
        sides_ref[0:CB, :] = solved[0] + solved[1]


def solve(weights, choice, a, s, c, y, labs, labc):
    vmem = pl.BlockSpec(memory_space=pltpu.VMEM)
    smem = pl.BlockSpec(memory_space=pltpu.SMEM)
    rows, voxels = a.shape[1], y.shape[1]
    return pl.pallas_call(
        solve_kernel,
        out_shape=[
            jax.ShapeDtypeStruct((2, rows, CB), jnp.float32),
            jax.ShapeDtypeStruct((rows, voxels), jnp.float32),
        ],
        in_specs=[smem, smem] + [vmem] * 6,
        out_specs=[vmem] * 2,
        scratch_shapes=[pltpu.VMEM((2, CB, CB), jnp.float32)],
        compiler_params=pltpu.CompilerParams(vmem_limit_bytes=32 << 20),
        name="solve",
    )(weights, choice, a, s, c, y, labs, labc)


def local(design, signals, label, weights, choice):
    lab = label.reshape(1, CB)
    s, c, y, labs = gather(design, signals, lab)
    trail, sides = solve(weights, choice, design, s, c, y, labs, lab)
    return trail, sides


def solution(mesh):
    return jax.shard_map(
        local,
        mesh=mesh,
        in_specs=(P(None, ("tm", "feat")), P("tm", "vox"), P("vox"), P(), P("vox")),
        out_specs=(P(None, ("tm", "feat"), "vox"), P(("tm", "feat"), "vox")),
        check_vma=False,
    )
```

```python
import math

import jax
import jax.numpy as jnp
from jax import lax
from jax.experimental import pallas as pl
from jax.experimental.pallas import tpu as pltpu
from jax.sharding import PartitionSpec as P

TIME = 1024
GROUPS = 4
CB = 128
GROUP = 64
CHIPS = 8
OFFSETS = [(dy, dx) for dy in range(2) for dx in range(4)][1:]
MESH = pl.DeviceIdType.MESH


def peer(t, dy, dx):
    y, x = t // 4, t % 4
    return ((y + dy) % 2) * 4 + (x + dx) % 4


def remote(src, dst, send, recv, **where):
    return pltpu.make_async_remote_copy(
        src_ref=src, dst_ref=dst, send_sem=send, recv_sem=recv, device_id=where, device_id_type=MESH
    )


class Spread:
    def __init__(self, buf, t, f, to, fo, sem):
        self.buf, self.t, self.f, self.to, self.fo = buf, t, f, to, fo
        self.scatter, self.scatter_r, self.own, self.own_r, self.ag, self.ag_r, self.sib, self.sib_r = sem
        self.owner = (t == to) & (f == fo)
        self.relay = (t != to) & (f == fo)
        self.side = (t != to) & (f != fo)
        self.owner_side = (t == to) & (f != fo)

    def chunk(self, t):
        return self.buf.at[pl.ds(pl.multiple_of(t * 128, 128), 128), :]

    def c_scatter(self, k):
        p = peer(self.t, *OFFSETS[k])
        c = self.chunk(p)
        return remote(c, c, self.scatter.at[k], self.scatter_r, tm=p)

    def c_scatter_in(self):
        c = self.chunk(self.t)
        return remote(c, c, self.scatter.at[0], self.scatter_r, tm=self.to)

    def c_own(self, k):
        p = peer(self.t, *OFFSETS[k])
        c = self.chunk(self.t)
        return remote(c, c, self.own.at[k], self.own_r, tm=p)

    def c_own_in(self):
        c = self.chunk(self.to)
        return remote(c, c, self.own.at[0], self.own_r, tm=self.to)

    def c_ag(self, k):
        p = peer(self.t, *OFFSETS[k])
        c = self.chunk(self.t)
        return p, remote(c, c, self.ag.at[k], self.ag_r.at[k], tm=p)

    def c_ag_in(self, k):
        dy, dx = OFFSETS[k]
        p = peer(self.t, dy, 4 - dx)
        c = self.chunk(p)
        return p, remote(c, c, self.ag.at[k], self.ag_r.at[k], tm=p)

    def c_sib(self, k, p):
        c = self.chunk(p)
        return remote(c, c, self.sib.at[k], self.sib_r.at[k], feat=1 - self.f)

    def c_whole(self):
        return remote(self.buf, self.buf, self.sib.at[0], self.sib_r.at[0], feat=1 - self.f)

    def start(self):
        @pl.when(self.owner)
        def _():
            for k in range(7):
                self.c_scatter(k).start()
            for k in range(7):
                self.c_own(k).start()
            self.c_whole().start()

    def forward(self):
        @pl.when(self.relay)
        def _():
            self.c_scatter_in().wait_recv()
            for k in range(7):
                p, c = self.c_ag(k)

                @pl.when(p != self.to)
                def _():
                    c.start()

            self.c_sib(7, self.t).start()

    def collect(self):
        @pl.when(self.relay)
        def _():
            for k in range(7):
                p, c = self.c_ag_in(k)

                @pl.when(p != self.to)
                def _():
                    c.wait_recv()

                @pl.when(p == self.to)
                def _():
                    self.c_own_in().wait_recv()

                self.c_sib(k, p).start()

    def finish(self):
        @pl.when(self.owner)
        def _():
            for k in range(7):
                self.c_scatter(k).wait_send()
                self.c_own(k).wait_send()
            self.c_whole().wait_send()

        @pl.when(self.owner_side)
        def _():
            self.c_whole().wait_recv()

        @pl.when(self.relay)
        def _():
            for k in range(7):
                p, c = self.c_ag(k)

                @pl.when(p != self.to)
                def _():
                    c.wait_send()

                q, _c = self.c_ag_in(k)
                self.c_sib(k, q).wait_send()
            self.c_sib(7, self.t).wait_send()

        @pl.when(self.side)
        def _():
            for k in range(7):
                dy, dx = OFFSETS[k]
                self.c_sib(k, peer(self.t, dy, 4 - dx)).wait_recv()
            self.c_sib(7, self.t).wait_recv()


def spread_sems():
    dma = pltpu.SemaphoreType.DMA
    return [dma((7,)), dma, dma((7,)), dma, dma((7,)), dma((7,)), dma((8,)), dma((8,))]


def gather_kernel(a_ref, y_ref, lab_ref, s_ref, c_ref, yall_ref, labs_ref, *sems):
    s_sem, c_sem, rest = sems[:8], sems[8:16], sems[16:]
    ysend, yrecv, bsend, brecv, lsend, lrecv, copy_sem = rest
    t, f, v = lax.axis_index("tm"), lax.axis_index("feat"), lax.axis_index("vox")
    row = t * 2 + f
    to, fo = v // 4, (v // 2) % 2
    owner_s, owner_c = row == 0, (t == to) & (f == fo)
    plain, server, single = v != 0, (v == 0) & (f == 1), (v == 0) & (f == 0)
    barrier = pltpu.get_barrier_semaphore()

    def signal(**where):
        pl.semaphore_signal(barrier, inc=1, device_id=where, device_id_type=MESH)

    @pl.when(plain)
    def _():
        signal(tm=v // 4, feat=1, vox=0)

    @pl.when(plain | single)
    def _():
        for dy, dx in OFFSETS:
            signal(tm=peer(t, dy, dx))

    @pl.when(plain | server)
    def _():
        signal(feat=1 - f)

    get_s = pltpu.make_async_copy(a_ref.at[:, pl.ds(0, CB)], s_ref, copy_sem.at[0])
    get_c = pltpu.make_async_copy(
        a_ref.at[:, pl.ds(pl.multiple_of((v % 2) * CB, CB), CB)], c_ref, copy_sem.at[1]
    )
    get_y = pltpu.make_async_copy(
        y_ref, yall_ref.at[pl.ds(pl.multiple_of(t * 128, 128), 128), :], copy_sem.at[2]
    )
    get_lab = pltpu.make_async_copy(lab_ref, labs_ref, copy_sem.at[3])

    @pl.when(owner_s)
    def _():
        get_s.start()

    @pl.when(owner_c)
    def _():
        get_c.start()

    get_y.start()

    @pl.when(v == 0)
    def _():
        get_lab.start()

    @pl.when(owner_s)
    def _():
        get_s.wait()

    @pl.when(owner_c)
    def _():
        get_c.wait()

    get_y.wait()

    @pl.when(v == 0)
    def _():
        get_lab.wait()

    @pl.when(plain | single)
    def _():
        pl.semaphore_wait(barrier, 8)

    @pl.when(server & (t != 0))
    def _():
        pl.semaphore_wait(barrier, 64)

    @pl.when(server & (t == 0))
    def _():
        pl.semaphore_wait(barrier, 48)

    first = jnp.where(t == 0, 16, 0)

    def c_lab(i):
        where = dict(tm=i // 2 % 8, feat=i % 2, vox=t * 4 + i // 16)
        return remote(labs_ref, labs_ref, lsend.at[i], lrecv, **where)

    @pl.when(server)
    def _():
        @pl.loop(first, 64)
        def _(i):
            c_lab(i).start()

    spread_s = Spread(s_ref, t, f, 0, 0, s_sem)
    spread_c = Spread(c_ref, t, f, to, fo, c_sem)
    spread_s.start()
    spread_c.start()

    def yblock(q, g):
        return yall_ref.at[pl.ds(pl.multiple_of(q * 128 + g * 64, 64), 64), :]

    def yslab(q):
        return yall_ref.at[pl.ds(pl.multiple_of(q * 128, 128), 128), :]

    def source(k):
        dy, dx = OFFSETS[k]
        return peer(t, dy, 4 - dx)

    def c_y(k, b):
        return remote(b, b, ysend.at[k], yrecv.at[k], tm=peer(t, *OFFSETS[k]))

    def c_yout(k, b):
        return remote(b, b, bsend.at[k], brecv.at[k], feat=1 - f)

    @pl.when(plain)
    def _():
        for k in range(7):
            c_y(k, yblock(t, f)).start()

    @pl.when(single)
    def _():
        for k in range(7):
            c_y(k, yslab(t)).start()

    spread_s.forward()
    spread_c.forward()
    spread_s.collect()
    spread_c.collect()

    @pl.when(plain)
    def _():
        for k in range(7):
            b = yblock(source(k), f)
            c_y(k, b).wait_recv()
            c_yout(k, b).start()

    @pl.when(single)
    def _():
        for k in range(7):
            b = yslab(source(k))
            c_y(k, b).wait_recv()
            c_yout(k, b).start()

    spread_s.finish()
    spread_c.finish()

    @pl.when(plain)
    def _():
        for k in range(7):
            c_y(k, yblock(t, f)).wait_send()
            c_yout(k, yblock(source(k), f)).wait_send()
            c_yout(k, yblock(source(k), 1 - f)).wait_recv()
        c_lab(0).wait_recv()

    @pl.when(single)
    def _():
        for k in range(7):
            c_y(k, yslab(t)).wait_send()
            c_yout(k, yslab(source(k))).wait_send()

    @pl.when(server)
    def _():
        for k in range(7):
            c_yout(k, yslab(source(k))).wait_recv()

        @pl.loop(first, 64)
        def _(i):
            c_lab(i).wait_send()


def in_hbm(*arrays):
    return [pltpu.with_memory_space_constraint(x, pltpu.HBM) for x in arrays]


def gather(a, y, lab):
    dma = pltpu.SemaphoreType.DMA
    vmem = pl.BlockSpec(memory_space=pltpu.VMEM)
    hbm = pl.BlockSpec(memory_space=pltpu.HBM)
    voxels = y.shape[1]
    return pl.pallas_call(
        gather_kernel,
        out_shape=[
            jax.ShapeDtypeStruct((TIME, CB), jnp.bfloat16),
            jax.ShapeDtypeStruct((TIME, CB), jnp.bfloat16),
            jax.ShapeDtypeStruct((TIME, voxels), jnp.bfloat16),
            jax.ShapeDtypeStruct((1, CB), jnp.int32),
        ],
        in_specs=[hbm] * 3,
        out_specs=[vmem] * 4,
        scratch_shapes=spread_sems()
        + spread_sems()
        + [dma((7,)), dma((7,)), dma((7,)), dma((7,)), dma((64,)), dma, dma((4,))],
        compiler_params=pltpu.CompilerParams(
            collective_id=0, has_side_effects=True, vmem_limit_bytes=16 << 20
        ),
        name="gather",
    )(*in_hbm(a, y, lab))


def inverse_factor(matrix):
    n = matrix.shape[0]
    count = n // 8
    sub = lax.broadcasted_iota(jnp.int32, (8, n), 0)
    lane = lax.broadcasted_iota(jnp.int32, (8, n), 1)
    rows = [matrix[8 * i : 8 * i + 8, :] for i in range(count)]
    out = []
    for j in range(count):
        inside = (lane >= 8 * j) & (lane < 8 * j + 8)
        eye = jnp.where(lane == 8 * j + sub, 1.0, 0.0)
        cols = {}
        for i in range(j, count):
            r = rows[i]
            cols[i] = [jnp.broadcast_to(r[:, 8 * j + p : 8 * j + p + 1], (8, n)) for p in range(8)]
            rows[i] = jnp.where(inside, eye if i == j else 0.0, r)
        scale = jnp.zeros((8, n), jnp.float32)
        for p in range(8):
            crow = [jnp.broadcast_to(cols[j][k][p : p + 1, :], (8, n)) if k >= p else None for k in range(8)]
            rrow = jnp.broadcast_to(rows[j][p : p + 1, :], (8, n))
            inv = 1.0 / crow[p]
            scale = jnp.where(sub == p, lax.rsqrt(crow[p]), scale)
            for i in range(j, count):
                factor = cols[i][p] * inv
                if i == j:
                    factor = jnp.where(sub > p, factor, 0.0)
                rows[i] = rows[i] - factor * rrow
                for k in range(p + 1, 8):
                    cols[i][k] = cols[i][k] - factor * crow[k]
        out.append(jnp.where(lane <= 8 * j + sub, rows[j] * scale, 0.0))
    return out


def tdot(a, b):
    return lax.dot_general(a, b, (((0,), (0,)), ((), ())), preferred_element_type=jnp.float32)


def fdot(a, b):
    return jnp.dot(a, b, precision=lax.Precision.HIGHEST, preferred_element_type=jnp.float32)


def solve_kernel(
    weights_hbm, choice_hbm, labc_hbm, a_ref, s_ref, c_ref, y_ref, labs_ref, trail_ref, sides_ref,
    inv_ref, weights_ref, choice_ref, labc_ref, sem
):
    small = [
        pltpu.make_async_copy(weights_hbm, weights_ref, sem.at[0]),
        pltpu.make_async_copy(choice_hbm, choice_ref, sem.at[1]),
        pltpu.make_async_copy(labc_hbm, labc_ref, sem.at[2]),
    ]
    for copy in small:
        copy.start()
    t, f, v = lax.axis_index("tm"), lax.axis_index("feat"), lax.axis_index("vox")
    row = t * 2 + f
    rows, voxels = sides_ref.shape
    s = s_ref[...]
    c = c_ref[...]
    y = y_ref[...]
    a = a_ref[...]

    def penalty(r, lab):
        total = jnp.zeros(lab.shape, jnp.float32)
        for g in range(GROUPS):
            total = jnp.where(lab == g, weights_ref[r, g], total)
        return total

    i_sub = lax.broadcasted_iota(jnp.int32, (CB, CB), 0)
    i_lane = lax.broadcasted_iota(jnp.int32, (CB, CB), 1)
    eye = i_sub == i_lane
    gss = tdot(s, s) * (1.0 / TIME)
    for copy in small:
        copy.wait()
    for r in range(2):
        pen = jnp.broadcast_to(penalty(r, labs_ref[...]), (CB, CB))
        for j, block in enumerate(inverse_factor(gss + jnp.where(eye, pen, 0.0))):
            inv_ref[r, 8 * j : 8 * j + 8, :] = block

    r_sub = lax.broadcasted_iota(jnp.int32, (rows, CB), 0) + row * rows
    r_lane = lax.broadcasted_iota(jnp.int32, (rows, CB), 1)
    grs = tdot(a, s) * (1.0 / TIME)
    grc = tdot(a, c) * (1.0 / TIME)
    gsc = tdot(s, c) * (1.0 / TIME)
    side = tdot(a, y) * (1.0 / math.sqrt(TIME))
    sside = tdot(s, y) * (1.0 / math.sqrt(TIME))

    group = lax.broadcasted_iota(jnp.int32, (1, voxels), 1) // GROUP
    ridge = jnp.zeros((1, voxels), jnp.int32)
    for g in range(voxels // GROUP):
        ridge = jnp.where(group == g, choice_ref[g], ridge)

    panels, solved = [], []
    for r in range(2):
        inv = inv_ref[r]
        pen_s = jnp.broadcast_to(penalty(r, labs_ref[...]), (rows, CB))
        pen_c = jnp.broadcast_to(penalty(r, labc_ref[...]), (rows, CB))
        grs_r = grs + jnp.where(r_sub == r_lane, pen_s, 0.0)
        gsc_r = gsc + jnp.where(eye & (v == 0), pen_c[:CB], 0.0)
        panel = lax.dot_general(
            grs_r, inv, (((1,), (1,)), ((), ())), precision=lax.Precision.HIGHEST,
            preferred_element_type=jnp.float32,
        )
        partner = fdot(inv, gsc_r)
        system = grc + jnp.where(r_sub == r_lane + v * CB, pen_c, 0.0)
        trail_ref[r] = system - fdot(panel, partner)
        panels.append(panel)
        solved.append(jnp.where(ridge == r, fdot(inv, sside), 0.0))
    update = fdot(panels[0], solved[0]) + fdot(panels[1], solved[1])
    sides_ref[...] = side - update

    @pl.when(row == 0)
    def _():
        sides_ref[0:CB, :] = solved[0] + solved[1]


def solve(weights, choice, labc, a, s, c, y, labs):
    vmem = pl.BlockSpec(memory_space=pltpu.VMEM)
    hbm = pl.BlockSpec(memory_space=pltpu.HBM)
    rows, voxels = a.shape[1], y.shape[1]
    return pl.pallas_call(
        solve_kernel,
        out_shape=[
            jax.ShapeDtypeStruct((2, rows, CB), jnp.float32),
            jax.ShapeDtypeStruct((rows, voxels), jnp.float32),
        ],
        in_specs=[hbm] * 3 + [vmem] * 5,
        out_specs=[vmem] * 2,
        scratch_shapes=[
            pltpu.VMEM((2, CB, CB), jnp.float32),
            pltpu.SMEM(weights.shape, jnp.float32),
            pltpu.SMEM(choice.shape, jnp.int32),
            pltpu.VMEM((1, CB), jnp.int32),
            pltpu.SemaphoreType.DMA((3,)),
        ],
        compiler_params=pltpu.CompilerParams(vmem_limit_bytes=32 << 20),
        name="solve",
    )(*in_hbm(weights, choice, labc), a, s, c, y, labs)


def local(design, signals, label, weights, choice):
    lab = label.reshape(1, CB)
    s, c, y, labs = gather(design, signals, lab)
    trail, sides = solve(weights, choice, lab, design, s, c, y, labs)
    return trail, sides


def solution(mesh):
    return jax.shard_map(
        local,
        mesh=mesh,
        in_specs=(P(None, ("tm", "feat")), P("tm", "vox"), P("vox"), P(), P("vox")),
        out_specs=(P(None, ("tm", "feat"), "vox"), P(("tm", "feat"), "vox")),
        check_vma=False,
    )
```

```python
import math

import jax
import jax.numpy as jnp
from jax import lax
from jax.experimental import pallas as pl
from jax.experimental.pallas import tpu as pltpu
from jax.sharding import PartitionSpec as P

TIME = 1024
GROUPS = 4
CB = 128
GROUP = 64
CHIPS = 8
OFFSETS = [(dy, dx) for dy in range(2) for dx in range(4)][1:]
MESH = pl.DeviceIdType.MESH


def peer(t, dy, dx):
    y, x = t // 4, t % 4
    return ((y + dy) % 2) * 4 + (x + dx) % 4


def remote(src, dst, send, recv, **where):
    return pltpu.make_async_remote_copy(
        src_ref=src, dst_ref=dst, send_sem=send, recv_sem=recv, device_id=where, device_id_type=MESH
    )


class Spread:
    def __init__(self, buf, t, f, to, fo, sem):
        self.buf, self.t, self.f, self.to, self.fo = buf, t, f, to, fo
        self.scatter, self.scatter_r, self.own, self.own_r, self.ag, self.ag_r, self.sib, self.sib_r = sem
        self.owner = (t == to) & (f == fo)
        self.relay = (t != to) & (f == fo)
        self.side = (t != to) & (f != fo)
        self.owner_side = (t == to) & (f != fo)

    def chunk(self, t):
        return self.buf.at[pl.ds(pl.multiple_of(t * 128, 128), 128), :]

    def c_scatter(self, k):
        p = peer(self.t, *OFFSETS[k])
        c = self.chunk(p)
        return remote(c, c, self.scatter.at[k], self.scatter_r, tm=p)

    def c_scatter_in(self):
        c = self.chunk(self.t)
        return remote(c, c, self.scatter.at[0], self.scatter_r, tm=self.to)

    def c_own(self, k):
        p = peer(self.t, *OFFSETS[k])
        c = self.chunk(self.t)
        return remote(c, c, self.own.at[k], self.own_r, tm=p)

    def c_own_in(self):
        c = self.chunk(self.to)
        return remote(c, c, self.own.at[0], self.own_r, tm=self.to)

    def c_ag(self, k):
        p = peer(self.t, *OFFSETS[k])
        c = self.chunk(self.t)
        return p, remote(c, c, self.ag.at[k], self.ag_r.at[k], tm=p)

    def c_ag_in(self, k):
        dy, dx = OFFSETS[k]
        p = peer(self.t, dy, 4 - dx)
        c = self.chunk(p)
        return p, remote(c, c, self.ag.at[k], self.ag_r.at[k], tm=p)

    def c_sib(self, k, p):
        c = self.chunk(p)
        return remote(c, c, self.sib.at[k], self.sib_r.at[k], feat=1 - self.f)

    def c_whole(self):
        return remote(self.buf, self.buf, self.sib.at[0], self.sib_r.at[0], feat=1 - self.f)

    def start(self):
        @pl.when(self.owner)
        def _():
            for k in range(7):
                self.c_scatter(k).start()
            for k in range(7):
                self.c_own(k).start()
            self.c_whole().start()

    def forward(self):
        @pl.when(self.relay)
        def _():
            self.c_scatter_in().wait_recv()
            for k in range(7):
                p, c = self.c_ag(k)

                @pl.when(p != self.to)
                def _():
                    c.start()

            self.c_sib(7, self.t).start()

    def collect(self):
        @pl.when(self.relay)
        def _():
            for k in range(7):
                p, c = self.c_ag_in(k)

                @pl.when(p != self.to)
                def _():
                    c.wait_recv()

                @pl.when(p == self.to)
                def _():
                    self.c_own_in().wait_recv()

                self.c_sib(k, p).start()

    def arrive(self):
        @pl.when(self.owner_side)
        def _():
            self.c_whole().wait_recv()

        @pl.when(self.side)
        def _():
            for k in range(7):
                dy, dx = OFFSETS[k]
                self.c_sib(k, peer(self.t, dy, 4 - dx)).wait_recv()
            self.c_sib(7, self.t).wait_recv()

    def finish(self):
        @pl.when(self.owner)
        def _():
            for k in range(7):
                self.c_scatter(k).wait_send()
                self.c_own(k).wait_send()
            self.c_whole().wait_send()

        @pl.when(self.relay)
        def _():
            for k in range(7):
                p, c = self.c_ag(k)

                @pl.when(p != self.to)
                def _():
                    c.wait_send()

                q, _c = self.c_ag_in(k)
                self.c_sib(k, q).wait_send()
            self.c_sib(7, self.t).wait_send()


def spread_sems():
    dma = pltpu.SemaphoreType.DMA
    return [dma((7,)), dma, dma((7,)), dma, dma((7,)), dma((7,)), dma((8,)), dma((8,))]


def gather_kernel(
    a_ref, y_ref, lab_ref, w_hbm, s_ref, c_ref, yall_ref, labs_ref, inv_ref, w_ref, *sems
):
    s_sem, c_sem, rest = sems[:8], sems[8:16], sems[16:]
    ysend, yrecv, bsend, brecv, lsend, lrecv, copy_sem = rest
    t, f, v = lax.axis_index("tm"), lax.axis_index("feat"), lax.axis_index("vox")
    row = t * 2 + f
    to, fo = v // 4, (v // 2) % 2
    owner_s, owner_c = row == 0, (t == to) & (f == fo)
    plain, server, single = v != 0, (v == 0) & (f == 1), (v == 0) & (f == 0)
    barrier = pltpu.get_barrier_semaphore()

    def signal(**where):
        pl.semaphore_signal(barrier, inc=1, device_id=where, device_id_type=MESH)

    @pl.when(plain)
    def _():
        signal(tm=v // 4, feat=1, vox=0)

    @pl.when(plain | single)
    def _():
        for dy, dx in OFFSETS:
            signal(tm=peer(t, dy, dx))

    @pl.when(plain | server)
    def _():
        signal(feat=1 - f)

    get_s = pltpu.make_async_copy(a_ref.at[:, pl.ds(0, CB)], s_ref, copy_sem.at[0])
    get_c = pltpu.make_async_copy(
        a_ref.at[:, pl.ds(pl.multiple_of((v % 2) * CB, CB), CB)], c_ref, copy_sem.at[1]
    )
    get_y = pltpu.make_async_copy(
        y_ref, yall_ref.at[pl.ds(pl.multiple_of(t * 128, 128), 128), :], copy_sem.at[2]
    )
    get_lab = pltpu.make_async_copy(lab_ref, labs_ref, copy_sem.at[3])

    @pl.when(owner_s)
    def _():
        get_s.start()

    @pl.when(owner_c)
    def _():
        get_c.start()

    get_y.start()
    get_w = pltpu.make_async_copy(w_hbm, w_ref, copy_sem.at[4])
    get_w.start()

    @pl.when(v == 0)
    def _():
        get_lab.start()

    @pl.when(owner_s)
    def _():
        get_s.wait()

    @pl.when(owner_c)
    def _():
        get_c.wait()

    get_y.wait()
    get_w.wait()

    @pl.when(v == 0)
    def _():
        get_lab.wait()

    @pl.when(plain | single)
    def _():
        pl.semaphore_wait(barrier, 8)

    @pl.when(server & (t != 0))
    def _():
        pl.semaphore_wait(barrier, 64)

    @pl.when(server & (t == 0))
    def _():
        pl.semaphore_wait(barrier, 48)

    first = jnp.where(t == 0, 16, 0)

    def c_lab(i):
        where = dict(tm=i // 2 % 8, feat=i % 2, vox=t * 4 + i // 16)
        return remote(labs_ref, labs_ref, lsend.at[i], lrecv, **where)

    @pl.when(server)
    def _():
        @pl.loop(first, 64)
        def _(i):
            c_lab(i).start()

    spread_s = Spread(s_ref, t, f, 0, 0, s_sem)
    spread_c = Spread(c_ref, t, f, to, fo, c_sem)
    spread_s.start()
    spread_c.start()

    def yblock(q, g):
        return yall_ref.at[pl.ds(pl.multiple_of(q * 128 + g * 64, 64), 64), :]

    def yslab(q):
        return yall_ref.at[pl.ds(pl.multiple_of(q * 128, 128), 128), :]

    def source(k):
        dy, dx = OFFSETS[k]
        return peer(t, dy, 4 - dx)

    def c_y(k, b):
        return remote(b, b, ysend.at[k], yrecv.at[k], tm=peer(t, *OFFSETS[k]))

    def c_yout(k, b):
        return remote(b, b, bsend.at[k], brecv.at[k], feat=1 - f)

    def y_start(ks):
        @pl.when(plain)
        def _():
            for k in ks:
                c_y(k, yblock(t, f)).start()

        @pl.when(single)
        def _():
            for k in ks:
                c_y(k, yslab(t)).start()

    def y_collect(ks):
        @pl.when(plain)
        def _():
            for k in ks:
                b = yblock(source(k), f)
                c_y(k, b).wait_recv()
                c_yout(k, b).start()

        @pl.when(single)
        def _():
            for k in ks:
                b = yslab(source(k))
                c_y(k, b).wait_recv()
                c_yout(k, b).start()

    y_start((0, 2))
    spread_s.forward()
    spread_c.forward()
    y_start((3, 1, 4, 6, 5))
    spread_s.collect()
    spread_s.arrive()

    @pl.when(plain)
    def _():
        c_lab(0).wait_recv()

    s_all = s_ref[...]
    gram = tdot(s_all, s_all) * (1.0 / TIME)
    eye = lax.broadcasted_iota(jnp.int32, (CB, CB), 0) == lax.broadcasted_iota(jnp.int32, (CB, CB), 1)
    matrices = []
    for r in range(2):
        pen = jnp.broadcast_to(penalty(w_ref, r, labs_ref[...]), (CB, CB))
        matrices.append(gram + jnp.where(eye, pen, 0.0))

    def between(panel):
        if panel == 0:
            spread_c.collect()
        elif panel == 1:
            y_collect((0, 2, 3))
        elif panel == 2:
            y_collect((1, 4, 6, 5))

    inverse_factor(jnp.stack(matrices), inv_ref, between)
    spread_c.arrive()
    spread_s.finish()
    spread_c.finish()

    @pl.when(plain)
    def _():
        for k in range(7):
            c_y(k, yblock(t, f)).wait_send()
            c_yout(k, yblock(source(k), f)).wait_send()
            c_yout(k, yblock(source(k), 1 - f)).wait_recv()

    @pl.when(single)
    def _():
        for k in range(7):
            c_y(k, yslab(t)).wait_send()
            c_yout(k, yslab(source(k))).wait_send()

    @pl.when(server)
    def _():
        for k in range(7):
            c_yout(k, yslab(source(k))).wait_recv()

        @pl.loop(first, 64)
        def _(i):
            c_lab(i).wait_send()


def in_hbm(*arrays):
    return [pltpu.with_memory_space_constraint(x, pltpu.HBM) for x in arrays]


def gather(a, y, lab, w):
    dma = pltpu.SemaphoreType.DMA
    vmem = pl.BlockSpec(memory_space=pltpu.VMEM)
    hbm = pl.BlockSpec(memory_space=pltpu.HBM)
    voxels = y.shape[1]
    return pl.pallas_call(
        gather_kernel,
        out_shape=[
            jax.ShapeDtypeStruct((TIME, CB), jnp.bfloat16),
            jax.ShapeDtypeStruct((TIME, CB), jnp.bfloat16),
            jax.ShapeDtypeStruct((TIME, voxels), jnp.bfloat16),
            jax.ShapeDtypeStruct((1, CB), jnp.int32),
            jax.ShapeDtypeStruct((2, CB, CB), jnp.float32),
        ],
        in_specs=[hbm] * 4,
        out_specs=[vmem] * 5,
        scratch_shapes=[pltpu.SMEM(w.shape, jnp.float32)]
        + spread_sems()
        + spread_sems()
        + [dma((7,)), dma((7,)), dma((7,)), dma((7,)), dma((64,)), dma, dma((5,))],
        compiler_params=pltpu.CompilerParams(
            collective_id=0, has_side_effects=True, vmem_limit_bytes=24 << 20
        ),
        name="gather",
    )(*in_hbm(a, y, lab, w))


PANEL = 32


def eliminate(t, base):
    q, height, n = t.shape
    lane8 = lax.broadcasted_iota(jnp.int32, (q, 8, n), 2)
    sub8 = lax.broadcasted_iota(jnp.int32, (q, 8, n), 1)
    out = []
    for step in range(height // 8):
        o = base + 8 * step
        block = t[:, :8, :]
        cols = [jnp.broadcast_to(block[:, :, o + p : o + p + 1], (q, 8, n)) for p in range(8)]
        inside = (lane8 >= o) & (lane8 < o + 8)
        block = jnp.where(inside, jnp.where(lane8 == o + sub8, 1.0, 0.0), block)
        invs, rrows, crows = [], [], []
        scale = jnp.zeros((q, 8, n), jnp.float32)
        for p in range(8):
            crow = {k: jnp.broadcast_to(cols[k][:, p : p + 1, :], (q, 8, n)) for k in range(p, 8)}
            rrow = jnp.broadcast_to(block[:, p : p + 1, :], (q, 8, n))
            inv = 1.0 / crow[p]
            scale = jnp.where(sub8 == p, lax.rsqrt(crow[p]), scale)
            factor = jnp.where(sub8 > p, cols[p] * inv, 0.0)
            block = block - factor * rrow
            for k in range(p + 1, 8):
                cols[k] = cols[k] - factor * crow[k]
            invs.append(inv)
            rrows.append(rrow)
            crows.append(crow)
        out.append(block * scale)
        rest = t.shape[1] - 8
        if rest:
            low = t[:, 8:, :].reshape(q, rest // 8, 8, n)
            cols = [
                jnp.broadcast_to(low[:, :, :, o + p : o + p + 1], (q, rest // 8, 8, n)) for p in range(8)
            ]
            lane = lax.broadcasted_iota(jnp.int32, low.shape, 3)
            low = jnp.where((lane >= o) & (lane < o + 8), 0.0, low)
            for p in range(8):
                factor = cols[p] * invs[p][:, None]
                low = low - factor * rrows[p][:, None]
                for k in range(p + 1, 8):
                    cols[k] = cols[k] - factor * crows[p][k][:, None]
            t = low.reshape(q, rest, n)
    return jnp.concatenate(out, axis=1)


def parts(x):
    high = x.astype(jnp.bfloat16)
    rest = x - high.astype(jnp.float32)
    mid = rest.astype(jnp.bfloat16)
    low = (rest - mid.astype(jnp.float32)).astype(jnp.bfloat16)
    return high, mid, low


def inverse_factor(t, out_ref, between):
    q, n, _ = t.shape
    lane = lax.broadcasted_iota(jnp.int32, (PANEL, n), 1)
    sub = lax.broadcasted_iota(jnp.int32, (PANEL, n), 0)
    for panel in range(n // PANEL):
        base, end = panel * PANEL, (panel + 1) * PANEL
        scaled = eliminate(t[:, :PANEL, :], base)
        for r in range(q):
            out_ref[r, base:end, :] = jnp.where(lane <= sub + base, scaled[r], 0.0)
        if end < n:
            rest = []
            for r in range(q):
                row = jnp.where((lane >= end) | (lane <= sub + base), scaled[r], 0.0)
                h, m, l = parts(row)
                update = tdot(
                    jnp.concatenate([h, h, h, m, m, l], 0), jnp.concatenate([h, m, l, h, m, h], 0)
                )[end:, :]
                low = t[r, PANEL:, :]
                lanes = lax.broadcasted_iota(jnp.int32, low.shape, 1)
                rest.append(jnp.where((lanes >= base) & (lanes < end), 0.0, low) - update)
            t = jnp.stack(rest)
            between(panel)


def penalty(w_ref, r, lab):
    total = jnp.zeros(lab.shape, jnp.float32)
    for g in range(GROUPS):
        total = jnp.where(lab == g, w_ref[r, g], total)
    return total


def tdot(a, b):
    return lax.dot_general(a, b, (((0,), (0,)), ((), ())), preferred_element_type=jnp.float32)


def fdot(a, b):
    return jnp.dot(a, b, precision=lax.Precision.HIGHEST, preferred_element_type=jnp.float32)


def solve_kernel(
    weights_hbm, choice_hbm, labc_hbm, a_ref, s_ref, c_ref, y_ref, labs_ref, inv_ref, trail_ref, sides_ref,
    weights_ref, choice_ref, labc_ref, sem
):
    small = [
        pltpu.make_async_copy(weights_hbm, weights_ref, sem.at[0]),
        pltpu.make_async_copy(choice_hbm, choice_ref, sem.at[1]),
        pltpu.make_async_copy(labc_hbm, labc_ref, sem.at[2]),
    ]
    for copy in small:
        copy.start()
    t, f, v = lax.axis_index("tm"), lax.axis_index("feat"), lax.axis_index("vox")
    row = t * 2 + f
    rows, voxels = sides_ref.shape
    s = s_ref[...]
    c = c_ref[...]
    y = y_ref[...]
    a = a_ref[...]

    i_sub = lax.broadcasted_iota(jnp.int32, (CB, CB), 0)
    i_lane = lax.broadcasted_iota(jnp.int32, (CB, CB), 1)
    eye = i_sub == i_lane
    for copy in small:
        copy.wait()
    r_sub = lax.broadcasted_iota(jnp.int32, (rows, CB), 0) + row * rows
    r_lane = lax.broadcasted_iota(jnp.int32, (rows, CB), 1)
    grs = tdot(a, s) * (1.0 / TIME)
    grc = tdot(a, c) * (1.0 / TIME)
    gsc = tdot(s, c) * (1.0 / TIME)
    side = tdot(a, y) * (1.0 / math.sqrt(TIME))
    sside = tdot(s, y) * (1.0 / math.sqrt(TIME))

    group = lax.broadcasted_iota(jnp.int32, (1, voxels), 1) // GROUP
    ridge = jnp.zeros((1, voxels), jnp.int32)
    for g in range(voxels // GROUP):
        ridge = jnp.where(group == g, choice_ref[g], ridge)

    panels, solved = [], []
    for r in range(2):
        inv = inv_ref[r]
        pen_s = jnp.broadcast_to(penalty(weights_ref, r, labs_ref[...]), (rows, CB))
        pen_c = jnp.broadcast_to(penalty(weights_ref, r, labc_ref[...]), (rows, CB))
        grs_r = grs + jnp.where(r_sub == r_lane, pen_s, 0.0)
        gsc_r = gsc + jnp.where(eye & (v == 0), pen_c[:CB], 0.0)
        panel = lax.dot_general(
            grs_r, inv, (((1,), (1,)), ((), ())), precision=lax.Precision.HIGHEST,
            preferred_element_type=jnp.float32,
        )
        partner = fdot(inv, gsc_r)
        system = grc + jnp.where(r_sub == r_lane + v * CB, pen_c, 0.0)
        trail_ref[r] = system - fdot(panel, partner)
        panels.append(panel)
        solved.append(jnp.where(ridge == r, fdot(inv, sside), 0.0))
    update = fdot(panels[0], solved[0]) + fdot(panels[1], solved[1])
    sides_ref[...] = side - update

    @pl.when(row == 0)
    def _():
        sides_ref[0:CB, :] = solved[0] + solved[1]


def solve(weights, choice, labc, a, s, c, y, labs, inv):
    vmem = pl.BlockSpec(memory_space=pltpu.VMEM)
    hbm = pl.BlockSpec(memory_space=pltpu.HBM)
    rows, voxels = a.shape[1], y.shape[1]
    return pl.pallas_call(
        solve_kernel,
        out_shape=[
            jax.ShapeDtypeStruct((2, rows, CB), jnp.float32),
            jax.ShapeDtypeStruct((rows, voxels), jnp.float32),
        ],
        in_specs=[hbm] * 3 + [vmem] * 6,
        out_specs=[vmem] * 2,
        scratch_shapes=[
            pltpu.SMEM(weights.shape, jnp.float32),
            pltpu.SMEM(choice.shape, jnp.int32),
            pltpu.VMEM((1, CB), jnp.int32),
            pltpu.SemaphoreType.DMA((3,)),
        ],
        compiler_params=pltpu.CompilerParams(vmem_limit_bytes=32 << 20),
        name="solve",
    )(*in_hbm(weights, choice, labc), a, s, c, y, labs, inv)


def local(design, signals, label, weights, choice):
    lab = label.reshape(1, CB)
    s, c, y, labs, inv = gather(design, signals, lab, weights)
    trail, sides = solve(weights, choice, lab, design, s, c, y, labs, inv)
    return trail, sides


def solution(mesh):
    return jax.shard_map(
        local,
        mesh=mesh,
        in_specs=(P(None, ("tm", "feat")), P("tm", "vox"), P("vox"), P(), P("vox")),
        out_specs=(P(None, ("tm", "feat"), "vox"), P(("tm", "feat"), "vox")),
        check_vma=False,
    )
```

```python
import math

import jax
import jax.numpy as jnp
from jax import lax
from jax.experimental import pallas as pl
from jax.experimental.pallas import tpu as pltpu
from jax.sharding import PartitionSpec as P

TIME = 1024
GROUPS = 4
CB = 128
GROUP = 64
MESH = pl.DeviceIdType.MESH
NEAR = [(0, 1), (0, 3), (1, 0)]
CHUNKS = 4
CHUNK = TIME // CHUNKS


def peer(t, dy, dx):
    y, x = t // 4, t % 4
    return ((y + dy) % 2) * 4 + (x + dx) % 4


def remote(src, dst, send, recv, **where):
    return pltpu.make_async_remote_copy(
        src_ref=src, dst_ref=dst, send_sem=send, recv_sem=recv, device_id=where, device_id_type=MESH
    )


class Place:
    def __init__(self):
        self.t, self.f, self.v = lax.axis_index("tm"), lax.axis_index("feat"), lax.axis_index("vox")
        self.zero = self.v == 0
        self.mover = self.f == jnp.where(self.t == 0, 1, 0)
        self.plain = self.v != 0
        self.single = self.zero & self.mover
        self.server = self.zero & jnp.logical_not(self.mover)

    def core(self, t, own):
        return jnp.where(self.zero, jnp.where(t == 0, 1, 0), own)

    def near(self, k):
        p = peer(self.t, *NEAR[k])
        return dict(tm=p, feat=self.core(p, self.f))


class Tree:
    def __init__(self, here, buf, to, fo, plane, sem, extra=None):
        self.here, self.buf, self.extra = here, buf, extra
        self.send, self.recv, self.sib_send, self.sib_recv = sem
        t = here.t
        self.dx = (t % 4 - to % 4 + 4) % 4
        self.dy = (t // 4 - to // 4 + 2) % 2
        self.on = here.f == here.core(t, plane)
        self.off = jnp.logical_not(self.on)
        self.root = (self.dx == 0) & (self.dy == 0)
        self.aside = self.root & here.plain & (fo != plane)
        self.owner = self.on & self.root & here.plain & (fo == plane)
        self.waits = jnp.logical_not(self.owner)

    def chunk(self, i):
        return self.buf.at[pl.ds(i * CHUNK, CHUNK), :]

    def near(self, k, i):
        c = self.chunk(i)
        return remote(c, c, self.send.at[k * CHUNKS + i], self.recv.at[i], **self.here.near(k))

    def sib(self, i):
        c = self.chunk(i)
        return remote(c, c, self.sib_send.at[i], self.sib_recv.at[i], feat=1 - self.here.f)

    def sends(self, i, act):
        out_right = (self.dx == 0) | (self.dx == 1) if i < CHUNKS // 2 else self.dx == 0
        out_left = self.dx == 0 if i < CHUNKS // 2 else (self.dx == 0) | (self.dx == 3)

        @pl.when(out_right)
        def _():
            act(self.near(0, i))

        @pl.when(out_left)
        def _():
            act(self.near(1, i))

        @pl.when(self.root & self.here.plain)
        def _():
            act(self.near(2, i))

        @pl.when(jnp.logical_not(self.aside))
        def _():
            act(self.sib(i))

    def across(self, i):
        c = self.chunk(i)
        return remote(c, c, self.sib_send.at[i], self.recv.at[i], feat=1 - self.here.f)

    def ext(self, i, act):
        c = self.chunk(i)
        if self.extra is not None:

            @pl.when(self.here.v == 1)
            def _():
                for n, (tm, feat) in enumerate(((0, 1), (4, 0))):
                    act(remote(c, c, self.extra.at[n * CHUNKS + i], self.recv.at[i], tm=tm, feat=feat, vox=0))

    def kick(self):
        @pl.when(self.owner)
        def _():
            for i in range(CHUNKS):
                self.ext(i, lambda c: c.start())
                self.sends(i, lambda c: c.start())

        @pl.when(self.off & self.aside)
        def _():
            for i in range(CHUNKS):
                self.across(i).start()

    def step(self, i):
        @pl.when(self.on & self.waits)
        def _():
            self.near(0, i).wait_recv()
            self.sends(i, lambda c: c.start())

    def arrive(self):
        @pl.when(self.off & jnp.logical_not(self.aside))
        def _():
            for i in range(CHUNKS):
                self.sib(i).wait_recv()

    def finish(self):
        @pl.when(self.owner)
        def _():
            for i in range(CHUNKS):
                self.ext(i, lambda c: c.wait_send())

        @pl.when(self.off & self.aside)
        def _():
            for i in range(CHUNKS):
                self.across(i).wait_send()

        @pl.when(self.on)
        def _():
            for i in range(CHUNKS):
                self.sends(i, lambda c: c.wait_send())


def tree_sems():
    dma = pltpu.SemaphoreType.DMA
    return [dma((3 * CHUNKS,)), dma((CHUNKS,)), dma((CHUNKS,)), dma((CHUNKS,))]


class Ring:
    PIECES = [
        ((1, 0), 0), ((0, 3), 0), ((0, 1), 0), ((1, 3), 0), ((1, 1), 0),
        ((0, 2), 1), ((0, 2), 2), ((1, 2), 1), ((1, 2), 2),
    ]
    COPIES = [(-1, 0, 2), (-1, 0, 0), (-1, 0, 1), (0, 0, 0), (0, 0, 1), (1, 1, 0), (2, 2, 1), (3, 1, 0), (4, 2, 1)]
    NEXT = {0: (3, 4), 1: (5,), 2: (6,), 3: (7,), 4: (8,)}

    def __init__(self, here, buf, rows, start, other, sem):
        self.here, self.buf, self.rows, self.start_row, self.other_row = here, buf, rows, start, other
        self.send, self.recv, self.sib_send, self.sib_recv = sem

    def block(self, offset, part, first):
        q = peer(self.here.t, *offset)
        row = q * 128 + first
        rows = self.rows
        if part:
            rows = rows // 2
            row = row + (part - 1) * rows
        return self.buf.at[pl.ds(pl.multiple_of(row, rows), rows), :]

    def copy(self, n):
        piece, part, k = self.COPIES[n]
        offset = (0, 0) if piece < 0 else self.PIECES[piece][0]
        b = self.block(offset, part, self.start_row)
        return remote(b, b, self.send.at[n], self.recv.at[n], **self.here.near(k))

    def incoming(self, n):
        b = self.block(*self.PIECES[n], self.start_row)
        return remote(b, b, self.send.at[n], self.recv.at[n], **self.here.near(0))

    def sib(self, n, row):
        b = self.block(*self.PIECES[n], row)
        return remote(b, b, self.sib_send.at[n], self.sib_recv.at[n], feat=1 - self.here.f)

    def begin(self):
        for n in (0, 1, 2):
            self.copy(n).start()

    def step(self, n):
        self.incoming(n).wait_recv()
        for m in self.NEXT.get(n, ()):
            self.copy(m).start()
        self.sib(n, self.start_row).start()

    def finish(self):
        for n in range(9):
            self.copy(n).wait_send()
            self.sib(n, self.start_row).wait_send()

    def arrive(self):
        for n in range(9):
            self.sib(n, self.other_row).wait_recv()


def gather_kernel(
    a_ref, y_ref, lab_ref, w_hbm, s_ref, c_ref, yall_ref, labs_ref, inv_ref, w_ref, *sems
):
    s_sem, c_sem, y_sem, rest = sems[:4], sems[4:8], sems[8:12], sems[12:]
    ext_sem, lsend, lrecv, copy_sem, ready = rest
    here = Place()
    t, f, v = here.t, here.f, here.v
    plain, single, server = here.plain, here.single, here.server
    row = t * 2 + f
    to, fo = v // 4, (v // 2) % 2
    owner_s, owner_c = plain & (row == 0), plain & (t == to) & (f == fo)
    barrier = pltpu.get_barrier_semaphore()

    def signal(**where):
        pl.semaphore_signal(barrier, inc=1, device_id=where, device_id_type=MESH)

    @pl.when(plain)
    def _():
        signal(tm=v // 4, feat=jnp.where(v // 4 == 0, 0, 1), vox=0)

    @pl.when(plain | single)
    def _():
        for k in range(3):
            signal(**here.near(k))

    @pl.when(plain | (server & (t != 0)) | (single & (t == 0)))
    def _():
        signal(feat=1 - f)

    @pl.when(single & (t % 4 == 0))
    def _():
        signal(tm=0, feat=0, vox=1)

    get_s = pltpu.make_async_copy(a_ref.at[:, pl.ds(0, CB)], s_ref, copy_sem.at[0])
    get_c = pltpu.make_async_copy(
        a_ref.at[:, pl.ds(pl.multiple_of((v % 2) * CB, CB), CB)], c_ref, copy_sem.at[1]
    )
    get_y = pltpu.make_async_copy(
        y_ref, yall_ref.at[pl.ds(pl.multiple_of(t * 128, 128), 128), :], copy_sem.at[2]
    )
    get_lab = pltpu.make_async_copy(lab_ref, labs_ref, copy_sem.at[3])
    get_w = pltpu.make_async_copy(w_hbm, w_ref, copy_sem.at[4])

    @pl.when(owner_s)
    def _():
        get_s.start()

    @pl.when(owner_c)
    def _():
        get_c.start()

    get_y.start()
    get_w.start()

    @pl.when(v == 0)
    def _():
        get_lab.start()
        get_lab.wait()

    @pl.when(owner_s)
    def _():
        get_s.wait()

    @pl.when(owner_c)
    def _():
        get_c.wait()

    get_y.wait()
    get_w.wait()

    extra = (v == 1) & (row == 0)

    @pl.when(extra)
    def _():
        pl.semaphore_wait(barrier, 6)

    @pl.when((plain & jnp.logical_not(extra)) | (single & (t != 0)))
    def _():
        pl.semaphore_wait(barrier, 4)

    @pl.when(single & (t == 0))
    def _():
        pl.semaphore_wait(barrier, 3)

    @pl.when(server & (t != 0))
    def _():
        pl.semaphore_wait(barrier, 64)

    @pl.when(server & (t == 0))
    def _():
        pl.semaphore_wait(barrier, 49)
        pl.semaphore_signal(ready, inc=1, device_id={"feat": 1}, device_id_type=MESH)

    first = jnp.where(t == 0, 16, 0)

    def c_lab(i):
        where = dict(tm=i // 2 % 8, feat=i % 2, vox=t * 4 + i // 16)
        return remote(labs_ref, labs_ref, lsend.at[i], lrecv, **where)

    @pl.when(server)
    def _():
        @pl.loop(first, 64)
        def _(i):
            c_lab(i).start()

    tree_s = Tree(here, s_ref, 0, 0, 0, s_sem, ext_sem)
    tree_c = Tree(here, c_ref, to, fo, 1, c_sem)
    halves = Ring(here, yall_ref, 64, f * 64, (1 - f) * 64, y_sem)
    whole = Ring(here, yall_ref, 128, 0, 0, y_sem)

    def y_do(name, *steps):
        @pl.when(plain)
        def _():
            for n in steps or (None,):
                getattr(halves, name)(*(() if n is None else (n,)))

        @pl.when(single)
        def _():
            for n in steps or (None,):
                getattr(whole, name)(*(() if n is None else (n,)))

    def c_do(name, *args):
        @pl.when(plain)
        def _():
            getattr(tree_c, name)(*args)

    tree_s.kick()
    c_do("kick")
    y_do("begin")

    @pl.when(single & (t == 0))
    def _():
        pl.semaphore_wait(ready, 1)

    tree_s.step(0)
    c_do("step", 0)
    tree_s.step(1)
    c_do("step", 1)
    y_do("step", 0)
    tree_s.step(2)
    c_do("step", 2)
    y_do("step", 1, 2)
    tree_s.step(3)
    c_do("step", 3)
    y_do("step", 3, 4)
    tree_s.arrive()

    @pl.when(plain)
    def _():
        c_lab(0).wait_recv()

    s_all = s_ref[...]
    gram = tdot(s_all, s_all) * (1.0 / TIME)
    eye = lax.broadcasted_iota(jnp.int32, (CB, CB), 0) == lax.broadcasted_iota(jnp.int32, (CB, CB), 1)
    matrices = []
    for r in range(2):
        pen = jnp.broadcast_to(penalty(w_ref, r, labs_ref[...]), (CB, CB))
        matrices.append(gram + jnp.where(eye, pen, 0.0))

    def between(panel):
        if panel == 0:
            y_do("step", 5, 6)
        elif panel == 1:
            y_do("step", 7, 8)

    inverse_factor(jnp.stack(matrices), inv_ref, between)
    c_do("arrive")

    @pl.when(here.zero)
    def _():
        c_ref[...] = s_ref[...]

    tree_s.finish()
    c_do("finish")
    y_do("finish")

    @pl.when(plain)
    def _():
        halves.arrive()

    @pl.when(server)
    def _():
        whole.arrive()

        @pl.loop(first, 64)
        def _(i):
            c_lab(i).wait_send()


def in_hbm(*arrays):
    return [pltpu.with_memory_space_constraint(x, pltpu.HBM) for x in arrays]


def gather(a, y, lab, w):
    dma = pltpu.SemaphoreType.DMA
    vmem = pl.BlockSpec(memory_space=pltpu.VMEM)
    hbm = pl.BlockSpec(memory_space=pltpu.HBM)
    voxels = y.shape[1]
    return pl.pallas_call(
        gather_kernel,
        out_shape=[
            jax.ShapeDtypeStruct((TIME, CB), jnp.bfloat16),
            jax.ShapeDtypeStruct((TIME, CB), jnp.bfloat16),
            jax.ShapeDtypeStruct((TIME, voxels), jnp.bfloat16),
            jax.ShapeDtypeStruct((1, CB), jnp.int32),
            jax.ShapeDtypeStruct((2, CB, CB), jnp.float32),
        ],
        in_specs=[hbm] * 4,
        out_specs=[vmem] * 5,
        scratch_shapes=[pltpu.SMEM(w.shape, jnp.float32)]
        + tree_sems()
        + tree_sems()
        + [dma((9,)), dma((9,)), dma((9,)), dma((9,))]
        + [dma((2 * CHUNKS,)), dma((64,)), dma, dma((5,)), pltpu.SemaphoreType.REGULAR],
        compiler_params=pltpu.CompilerParams(
            collective_id=0, has_side_effects=True, vmem_limit_bytes=24 << 20
        ),
        name="gather",
    )(*in_hbm(a, y, lab, w))


PANEL = 32


def eliminate(t, base):
    q, height, n = t.shape
    lane8 = lax.broadcasted_iota(jnp.int32, (q, 8, n), 2)
    sub8 = lax.broadcasted_iota(jnp.int32, (q, 8, n), 1)
    out = []
    for step in range(height // 8):
        o = base + 8 * step
        block = t[:, :8, :]
        cols = [jnp.broadcast_to(block[:, :, o + p : o + p + 1], (q, 8, n)) for p in range(8)]
        inside = (lane8 >= o) & (lane8 < o + 8)
        block = jnp.where(inside, jnp.where(lane8 == o + sub8, 1.0, 0.0), block)
        invs, rrows, crows = [], [], []
        scale = jnp.zeros((q, 8, n), jnp.float32)
        for p in range(8):
            crow = {k: jnp.broadcast_to(cols[k][:, p : p + 1, :], (q, 8, n)) for k in range(p, 8)}
            rrow = jnp.broadcast_to(block[:, p : p + 1, :], (q, 8, n))
            inv = 1.0 / crow[p]
            scale = jnp.where(sub8 == p, lax.rsqrt(crow[p]), scale)
            factor = jnp.where(sub8 > p, cols[p] * inv, 0.0)
            block = block - factor * rrow
            for k in range(p + 1, 8):
                cols[k] = cols[k] - factor * crow[k]
            invs.append(inv)
            rrows.append(rrow)
            crows.append(crow)
        out.append(block * scale)
        rest = t.shape[1] - 8
        if rest:
            low = t[:, 8:, :].reshape(q, rest // 8, 8, n)
            cols = [
                jnp.broadcast_to(low[:, :, :, o + p : o + p + 1], (q, rest // 8, 8, n)) for p in range(8)
            ]
            lane = lax.broadcasted_iota(jnp.int32, low.shape, 3)
            low = jnp.where((lane >= o) & (lane < o + 8), 0.0, low)
            for p in range(8):
                factor = cols[p] * invs[p][:, None]
                low = low - factor * rrows[p][:, None]
                for k in range(p + 1, 8):
                    cols[k] = cols[k] - factor * crows[p][k][:, None]
            t = low.reshape(q, rest, n)
    return jnp.concatenate(out, axis=1)


def parts(x):
    high = x.astype(jnp.bfloat16)
    rest = x - high.astype(jnp.float32)
    mid = rest.astype(jnp.bfloat16)
    low = (rest - mid.astype(jnp.float32)).astype(jnp.bfloat16)
    return high, mid, low


def inverse_factor(t, out_ref, between):
    q, n, _ = t.shape
    lane = lax.broadcasted_iota(jnp.int32, (PANEL, n), 1)
    sub = lax.broadcasted_iota(jnp.int32, (PANEL, n), 0)
    for panel in range(n // PANEL):
        base, end = panel * PANEL, (panel + 1) * PANEL
        scaled = eliminate(t[:, :PANEL, :], base)
        for r in range(q):
            out_ref[r, base:end, :] = jnp.where(lane <= sub + base, scaled[r], 0.0)
        if end < n:
            rest = []
            for r in range(q):
                row = jnp.where((lane >= end) | (lane <= sub + base), scaled[r], 0.0)
                h, m, l = parts(row)
                update = tdot(
                    jnp.concatenate([h, h, h, m, m, l], 0), jnp.concatenate([h, m, l, h, m, h], 0)
                )[end:, :]
                low = t[r, PANEL:, :]
                lanes = lax.broadcasted_iota(jnp.int32, low.shape, 1)
                rest.append(jnp.where((lanes >= base) & (lanes < end), 0.0, low) - update)
            t = jnp.stack(rest)
            between(panel)


def penalty(w_ref, r, lab):
    total = jnp.zeros(lab.shape, jnp.float32)
    for g in range(GROUPS):
        total = jnp.where(lab == g, w_ref[r, g], total)
    return total


def tdot(a, b):
    return lax.dot_general(a, b, (((0,), (0,)), ((), ())), preferred_element_type=jnp.float32)


def fdot(a, b):
    return jnp.dot(a, b, precision=lax.Precision.HIGHEST, preferred_element_type=jnp.float32)


def solve_kernel(
    weights_hbm, choice_hbm, labc_hbm, a_ref, s_ref, c_ref, y_ref, labs_ref, inv_ref, trail_ref, sides_ref,
    weights_ref, choice_ref, labc_ref, sem
):
    small = [
        pltpu.make_async_copy(weights_hbm, weights_ref, sem.at[0]),
        pltpu.make_async_copy(choice_hbm, choice_ref, sem.at[1]),
        pltpu.make_async_copy(labc_hbm, labc_ref, sem.at[2]),
    ]
    for copy in small:
        copy.start()
    t, f, v = lax.axis_index("tm"), lax.axis_index("feat"), lax.axis_index("vox")
    row = t * 2 + f
    rows, voxels = sides_ref.shape
    s = s_ref[...]
    c = c_ref[...]
    y = y_ref[...]
    a = a_ref[...]

    i_sub = lax.broadcasted_iota(jnp.int32, (CB, CB), 0)
    i_lane = lax.broadcasted_iota(jnp.int32, (CB, CB), 1)
    eye = i_sub == i_lane
    for copy in small:
        copy.wait()
    r_sub = lax.broadcasted_iota(jnp.int32, (rows, CB), 0) + row * rows
    r_lane = lax.broadcasted_iota(jnp.int32, (rows, CB), 1)
    grs = tdot(a, s) * (1.0 / TIME)
    grc = tdot(a, c) * (1.0 / TIME)
    gsc = tdot(s, c) * (1.0 / TIME)
    side = tdot(a, y) * (1.0 / math.sqrt(TIME))
    sside = tdot(s, y) * (1.0 / math.sqrt(TIME))

    group = lax.broadcasted_iota(jnp.int32, (1, voxels), 1) // GROUP
    ridge = jnp.zeros((1, voxels), jnp.int32)
    for g in range(voxels // GROUP):
        ridge = jnp.where(group == g, choice_ref[g], ridge)

    panels, solved = [], []
    for r in range(2):
        inv = inv_ref[r]
        pen_s = jnp.broadcast_to(penalty(weights_ref, r, labs_ref[...]), (rows, CB))
        pen_c = jnp.broadcast_to(penalty(weights_ref, r, labc_ref[...]), (rows, CB))
        grs_r = grs + jnp.where(r_sub == r_lane, pen_s, 0.0)
        gsc_r = gsc + jnp.where(eye & (v == 0), pen_c[:CB], 0.0)
        panel = lax.dot_general(
            grs_r, inv, (((1,), (1,)), ((), ())), precision=lax.Precision.HIGHEST,
            preferred_element_type=jnp.float32,
        )
        partner = fdot(inv, gsc_r)
        system = grc + jnp.where(r_sub == r_lane + v * CB, pen_c, 0.0)
        trail_ref[r] = system - fdot(panel, partner)
        panels.append(panel)
        solved.append(jnp.where(ridge == r, fdot(inv, sside), 0.0))
    update = fdot(panels[0], solved[0]) + fdot(panels[1], solved[1])
    sides_ref[...] = side - update

    @pl.when(row == 0)
    def _():
        sides_ref[0:CB, :] = solved[0] + solved[1]


def solve(weights, choice, labc, a, s, c, y, labs, inv):
    vmem = pl.BlockSpec(memory_space=pltpu.VMEM)
    hbm = pl.BlockSpec(memory_space=pltpu.HBM)
    rows, voxels = a.shape[1], y.shape[1]
    return pl.pallas_call(
        solve_kernel,
        out_shape=[
            jax.ShapeDtypeStruct((2, rows, CB), jnp.float32),
            jax.ShapeDtypeStruct((rows, voxels), jnp.float32),
        ],
        in_specs=[hbm] * 3 + [vmem] * 6,
        out_specs=[vmem] * 2,
        scratch_shapes=[
            pltpu.SMEM(weights.shape, jnp.float32),
            pltpu.SMEM(choice.shape, jnp.int32),
            pltpu.VMEM((1, CB), jnp.int32),
            pltpu.SemaphoreType.DMA((3,)),
        ],
        compiler_params=pltpu.CompilerParams(vmem_limit_bytes=32 << 20),
        name="solve",
    )(*in_hbm(weights, choice, labc), a, s, c, y, labs, inv)


def local(design, signals, label, weights, choice):
    lab = label.reshape(1, CB)
    s, c, y, labs, inv = gather(design, signals, lab, weights)
    trail, sides = solve(weights, choice, lab, design, s, c, y, labs, inv)
    return trail, sides


def solution(mesh):
    return jax.shard_map(
        local,
        mesh=mesh,
        in_specs=(P(None, ("tm", "feat")), P("tm", "vox"), P("vox"), P(), P("vox")),
        out_specs=(P(None, ("tm", "feat"), "vox"), P(("tm", "feat"), "vox")),
        check_vma=False,
    )
```

```python
import math

import jax
import jax.numpy as jnp
from jax import lax
from jax.experimental import pallas as pl
from jax.experimental.pallas import tpu as pltpu
from jax.sharding import PartitionSpec as P

TIME = 1024
GROUPS = 4
CB = 128
GROUP = 64
OFFSETS = [(dy, dx) for dy in range(2) for dx in range(4)][1:]
MESH = pl.DeviceIdType.MESH


def peer(t, dy, dx):
    y, x = t // 4, t % 4
    return ((y + dy) % 2) * 4 + (x + dx) % 4


def remote(src, dst, send, recv, **where):
    return pltpu.make_async_remote_copy(
        src_ref=src, dst_ref=dst, send_sem=send, recv_sem=recv, device_id=where, device_id_type=MESH
    )


class Place:
    def __init__(self):
        self.t, self.f, self.v = lax.axis_index("tm"), lax.axis_index("feat"), lax.axis_index("vox")
        self.zero = self.v == 0
        self.mover = self.f == jnp.where(self.t == 0, 1, 0)
        self.plain = self.v != 0
        self.single = self.zero & self.mover
        self.server = self.zero & jnp.logical_not(self.mover)

    def core(self, t, own):
        return jnp.where(self.zero, jnp.where(t == 0, 1, 0), own)

    def chip(self, p):
        return dict(tm=p, feat=self.core(p, self.f))


class Spread:
    def __init__(self, here, buf, to, fo, sem):
        self.here, self.buf, self.t, self.f, self.to = here, buf, here.t, here.f, to
        self.scatter, self.scatter_r, self.own, self.own_r, self.ag, self.ag_r, self.sib, self.sib_r = sem
        on = self.f == here.core(self.t, fo)
        self.owner = (self.t == to) & on
        self.relay = (self.t != to) & on
        self.side = (self.t != to) & jnp.logical_not(on)
        self.owner_side = (self.t == to) & jnp.logical_not(on)

    def chunk(self, t):
        return self.buf.at[pl.ds(pl.multiple_of(t * 128, 128), 128), :]

    def c_scatter(self, k):
        p = peer(self.t, *OFFSETS[k])
        c = self.chunk(p)
        return remote(c, c, self.scatter.at[k], self.scatter_r, **self.here.chip(p))

    def c_scatter_in(self):
        c = self.chunk(self.t)
        return remote(c, c, self.scatter.at[0], self.scatter_r, **self.here.chip(self.to))

    def c_own(self, k):
        p = peer(self.t, *OFFSETS[k])
        c = self.chunk(self.t)
        return remote(c, c, self.own.at[k], self.own_r, **self.here.chip(p))

    def c_own_in(self):
        c = self.chunk(self.to)
        return remote(c, c, self.own.at[0], self.own_r, **self.here.chip(self.to))

    def c_ag(self, k):
        p = peer(self.t, *OFFSETS[k])
        c = self.chunk(self.t)
        return p, remote(c, c, self.ag.at[k], self.ag_r.at[k], **self.here.chip(p))

    def c_ag_in(self, k):
        dy, dx = OFFSETS[k]
        p = peer(self.t, dy, 4 - dx)
        c = self.chunk(p)
        return p, remote(c, c, self.ag.at[k], self.ag_r.at[k], **self.here.chip(p))

    def c_sib(self, k, p):
        c = self.chunk(p)
        return remote(c, c, self.sib.at[k], self.sib_r.at[k], feat=1 - self.f)

    def c_whole(self):
        return remote(self.buf, self.buf, self.sib.at[0], self.sib_r.at[0], feat=1 - self.f)

    def start(self):
        @pl.when(self.owner)
        def _():
            for k in range(7):
                self.c_scatter(k).start()
            for k in range(7):
                self.c_own(k).start()

            @pl.when(self.here.plain)
            def _():
                self.c_whole().start()

    def forward(self):
        @pl.when(self.relay)
        def _():
            self.c_scatter_in().wait_recv()
            for k in range(7):
                p, c = self.c_ag(k)

                @pl.when(p != self.to)
                def _():
                    c.start()

            self.c_sib(7, self.t).start()

    def collect(self):
        @pl.when(self.relay)
        def _():
            for k in range(7):
                p, c = self.c_ag_in(k)

                @pl.when(p != self.to)
                def _():
                    c.wait_recv()

                @pl.when(p == self.to)
                def _():
                    self.c_own_in().wait_recv()

                self.c_sib(k, p).start()

    def arrive(self):
        @pl.when(self.owner_side & self.here.plain)
        def _():
            self.c_whole().wait_recv()

        @pl.when(self.side)
        def _():
            for k in range(7):
                dy, dx = OFFSETS[k]
                self.c_sib(k, peer(self.t, dy, 4 - dx)).wait_recv()
            self.c_sib(7, self.t).wait_recv()

    def finish(self):
        @pl.when(self.owner)
        def _():
            for k in range(7):
                self.c_scatter(k).wait_send()
                self.c_own(k).wait_send()

            @pl.when(self.here.plain)
            def _():
                self.c_whole().wait_send()

        @pl.when(self.relay)
        def _():
            for k in range(7):
                p, c = self.c_ag(k)

                @pl.when(p != self.to)
                def _():
                    c.wait_send()

                q, _c = self.c_ag_in(k)
                self.c_sib(k, q).wait_send()
            self.c_sib(7, self.t).wait_send()


def spread_sems():
    dma = pltpu.SemaphoreType.DMA
    return [dma((7,)), dma, dma((7,)), dma, dma((7,)), dma((7,)), dma((8,)), dma((8,))]


def gather_kernel(
    a_hbm, y_ref, lab_ref, w_hbm,
    at_ref, st_ref, grs_ref, grc_ref, gsc_ref, yall_ref, labs_ref, inv_ref,
    w_ref, a_ref, s_ref, c_ref, *sems,
):
    s_sem, c_sem, rest = sems[:8], sems[8:16], sems[16:]
    ysend, yrecv, bsend, brecv, lsend, lrecv, copy_sem, over_send, over_recv, ready = rest
    here = Place()
    t, f, v = here.t, here.f, here.v
    plain, single, server = here.plain, here.single, here.server
    row = t * 2 + f
    to, fo = v // 4, (v // 2) % 2
    owner_s, owner_c = row == 0, plain & (t == to) & (f == fo)
    first_single, first_server = single & (t == 0), server & (t == 0)
    barrier = pltpu.get_barrier_semaphore()

    def signal(**where):
        pl.semaphore_signal(barrier, inc=1, device_id=where, device_id_type=MESH)

    @pl.when(plain)
    def _():
        signal(tm=v // 4, feat=jnp.where(v // 4 == 0, 0, 1), vox=0)

    @pl.when(plain | single)
    def _():
        for offset in OFFSETS:
            signal(**here.chip(peer(t, *offset)))

    @pl.when(plain | (server & (t != 0)) | first_single)
    def _():
        signal(feat=1 - f)

    get_s = pltpu.make_async_copy(a_hbm.at[:, pl.ds(0, CB)], s_ref, copy_sem.at[0])
    get_c = pltpu.make_async_copy(
        a_hbm.at[:, pl.ds(pl.multiple_of((v % 2) * CB, CB), CB)], c_ref, copy_sem.at[1]
    )
    get_y = pltpu.make_async_copy(
        y_ref, yall_ref.at[pl.ds(pl.multiple_of(t * 128, 128), 128), :], copy_sem.at[2]
    )
    get_lab = pltpu.make_async_copy(lab_ref, labs_ref, copy_sem.at[3])
    get_w = pltpu.make_async_copy(w_hbm, w_ref, copy_sem.at[4])
    get_a = pltpu.make_async_copy(a_hbm, a_ref, copy_sem.at[5])

    @pl.when(owner_s)
    def _():
        get_s.start()

    @pl.when(owner_c)
    def _():
        get_c.start()

    get_y.start()
    get_w.start()
    get_a.start()

    @pl.when(v == 0)
    def _():
        get_lab.start()
        get_lab.wait()

    @pl.when(owner_s)
    def _():
        get_s.wait()

    @pl.when(owner_c)
    def _():
        get_c.wait()

    get_y.wait()
    get_w.wait()
    get_a.wait()
    at_ref[...] = a_ref[...].T

    @pl.when(plain | (single & (t != 0)))
    def _():
        pl.semaphore_wait(barrier, 8)

    @pl.when(first_single)
    def _():
        pl.semaphore_wait(barrier, 7)

    @pl.when(server & (t != 0))
    def _():
        pl.semaphore_wait(barrier, 64)

    over = remote(s_ref, s_ref, over_send, over_recv, feat=1 - f)

    @pl.when(first_server)
    def _():
        pl.semaphore_wait(barrier, 49)
        pl.semaphore_signal(ready, inc=1, device_id={"feat": 1}, device_id_type=MESH)
        over.start()

    first = jnp.where(t == 0, 16, 0)

    def c_lab(i):
        where = dict(tm=i // 2 % 8, feat=i % 2, vox=t * 4 + i // 16)
        return remote(labs_ref, labs_ref, lsend.at[i], lrecv, **where)

    @pl.when(server)
    def _():
        @pl.loop(first, 64)
        def _(i):
            c_lab(i).start()

    spread_s = Spread(here, s_ref, 0, 0, s_sem)
    spread_c = Spread(here, c_ref, to, fo, c_sem)

    def c_do(name):
        @pl.when(plain)
        def _():
            getattr(spread_c, name)()

    @pl.when(plain)
    def _():
        spread_s.start()

    c_do("start")

    def yblock(q, g):
        return yall_ref.at[pl.ds(pl.multiple_of(q * 128 + g * 64, 64), 64), :]

    def yslab(q):
        return yall_ref.at[pl.ds(pl.multiple_of(q * 128, 128), 128), :]

    def source(k):
        dy, dx = OFFSETS[k]
        return peer(t, dy, 4 - dx)

    def c_y(k, b):
        return remote(b, b, ysend.at[k], yrecv.at[k], **here.chip(peer(t, *OFFSETS[k])))

    def c_yout(k, b):
        return remote(b, b, bsend.at[k], brecv.at[k], feat=1 - f)

    def y_start(ks):
        @pl.when(plain)
        def _():
            for k in ks:
                c_y(k, yblock(t, f)).start()

        @pl.when(single)
        def _():
            for k in ks:
                c_y(k, yslab(t)).start()

    def y_collect(ks):
        @pl.when(plain)
        def _():
            for k in ks:
                b = yblock(source(k), f)
                c_y(k, b).wait_recv()
                c_yout(k, b).start()

        @pl.when(single)
        def _():
            for k in ks:
                b = yslab(source(k))
                c_y(k, b).wait_recv()
                c_yout(k, b).start()

    y_start((0, 2))

    @pl.when(first_single)
    def _():
        y_start((3, 1, 4, 6, 5))
        pl.semaphore_wait(ready, 1)
        over.wait_recv()
        spread_s.start()

    spread_s.forward()
    c_do("forward")

    @pl.when(jnp.logical_not(first_single))
    def _():
        y_start((3, 1, 4, 6, 5))

    spread_s.collect()
    spread_s.arrive()

    @pl.when(plain)
    def _():
        c_lab(0).wait_recv()

    s_all = s_ref[...]
    st_ref[...] = s_all.T
    gram = dot(st_ref[...], s_all) * (1.0 / TIME)
    eye = lax.broadcasted_iota(jnp.int32, (CB, CB), 0) == lax.broadcasted_iota(jnp.int32, (CB, CB), 1)
    matrices = []
    for r in range(2):
        pen = jnp.broadcast_to(penalty(w_ref, r, labs_ref[...]), (CB, CB))
        matrices.append(gram + jnp.where(eye, pen, 0.0))

    def between(panel):
        if panel == 0:
            c_do("collect")
        elif panel == 1:
            y_collect((0, 2, 3))
        elif panel == 2:
            y_collect((1, 4, 6, 5))

    inverse_factor(jnp.stack(matrices), inv_ref, between)
    grs_ref[...] = dot(at_ref[...], s_all) * (1.0 / TIME)
    c_do("arrive")

    @pl.when(here.zero)
    def _():
        c_ref[...] = s_ref[...]

    c_all = c_ref[...]
    grc_ref[...] = dot(at_ref[...], c_all) * (1.0 / TIME)
    gsc_ref[...] = dot(st_ref[...], c_all) * (1.0 / TIME)
    spread_s.finish()
    c_do("finish")

    @pl.when(first_server)
    def _():
        over.wait_send()

    @pl.when(plain)
    def _():
        for k in range(7):
            c_y(k, yblock(t, f)).wait_send()
            c_yout(k, yblock(source(k), f)).wait_send()
            c_yout(k, yblock(source(k), 1 - f)).wait_recv()

    @pl.when(single)
    def _():
        for k in range(7):
            c_y(k, yslab(t)).wait_send()
            c_yout(k, yslab(source(k))).wait_send()

    @pl.when(server)
    def _():
        for k in range(7):
            c_yout(k, yslab(source(k))).wait_recv()

        @pl.loop(first, 64)
        def _(i):
            c_lab(i).wait_send()


def in_hbm(*arrays):
    return [pltpu.with_memory_space_constraint(x, pltpu.HBM) for x in arrays]


def gather(a, y, lab, w):
    dma = pltpu.SemaphoreType.DMA
    vmem = pl.BlockSpec(memory_space=pltpu.VMEM)
    hbm = pl.BlockSpec(memory_space=pltpu.HBM)
    rows, voxels = a.shape[1], y.shape[1]
    return pl.pallas_call(
        gather_kernel,
        out_shape=[
            jax.ShapeDtypeStruct((rows, TIME), jnp.bfloat16),
            jax.ShapeDtypeStruct((CB, TIME), jnp.bfloat16),
            jax.ShapeDtypeStruct((rows, CB), jnp.float32),
            jax.ShapeDtypeStruct((rows, CB), jnp.float32),
            jax.ShapeDtypeStruct((CB, CB), jnp.float32),
            jax.ShapeDtypeStruct((TIME, voxels), jnp.bfloat16),
            jax.ShapeDtypeStruct((1, CB), jnp.int32),
            jax.ShapeDtypeStruct((2, CB, CB), jnp.float32),
        ],
        in_specs=[hbm] * 4,
        out_specs=[vmem] * 8,
        scratch_shapes=[
            pltpu.SMEM(w.shape, jnp.float32),
            pltpu.VMEM(a.shape, jnp.bfloat16),
            pltpu.VMEM((TIME, CB), jnp.bfloat16),
            pltpu.VMEM((TIME, CB), jnp.bfloat16),
        ]
        + spread_sems()
        + spread_sems()
        + [dma((7,)), dma((7,)), dma((7,)), dma((7,)), dma((64,)), dma, dma((6,))]
        + [dma, dma, pltpu.SemaphoreType.REGULAR],
        compiler_params=pltpu.CompilerParams(
            collective_id=0, has_side_effects=True, vmem_limit_bytes=24 << 20
        ),
        name="gather",
    )(*in_hbm(a, y, lab, w))


PANEL = 32


def eliminate(t, base):
    q, height, n = t.shape
    lane8 = lax.broadcasted_iota(jnp.int32, (q, 8, n), 2)
    sub8 = lax.broadcasted_iota(jnp.int32, (q, 8, n), 1)
    out = []
    for step in range(height // 8):
        o = base + 8 * step
        block = t[:, :8, :]
        cols = [jnp.broadcast_to(block[:, :, o + p : o + p + 1], (q, 8, n)) for p in range(8)]
        inside = (lane8 >= o) & (lane8 < o + 8)
        block = jnp.where(inside, jnp.where(lane8 == o + sub8, 1.0, 0.0), block)
        invs, rrows, crows = [], [], []
        scale = jnp.zeros((q, 8, n), jnp.float32)
        for p in range(8):
            crow = {k: jnp.broadcast_to(cols[k][:, p : p + 1, :], (q, 8, n)) for k in range(p, 8)}
            rrow = jnp.broadcast_to(block[:, p : p + 1, :], (q, 8, n))
            inv = 1.0 / crow[p]
            scale = jnp.where(sub8 == p, lax.rsqrt(crow[p]), scale)
            factor = jnp.where(sub8 > p, cols[p] * inv, 0.0)
            block = block - factor * rrow
            for k in range(p + 1, 8):
                cols[k] = cols[k] - factor * crow[k]
            invs.append(inv)
            rrows.append(rrow)
            crows.append(crow)
        out.append(block * scale)
        rest = t.shape[1] - 8
        if rest:
            low = t[:, 8:, :].reshape(q, rest // 8, 8, n)
            cols = [
                jnp.broadcast_to(low[:, :, :, o + p : o + p + 1], (q, rest // 8, 8, n)) for p in range(8)
            ]
            lane = lax.broadcasted_iota(jnp.int32, low.shape, 3)
            low = jnp.where((lane >= o) & (lane < o + 8), 0.0, low)
            for p in range(8):
                factor = cols[p] * invs[p][:, None]
                low = low - factor * rrows[p][:, None]
                for k in range(p + 1, 8):
                    cols[k] = cols[k] - factor * crows[p][k][:, None]
            t = low.reshape(q, rest, n)
    return jnp.concatenate(out, axis=1)


def parts(x):
    high = x.astype(jnp.bfloat16)
    rest = x - high.astype(jnp.float32)
    mid = rest.astype(jnp.bfloat16)
    low = (rest - mid.astype(jnp.float32)).astype(jnp.bfloat16)
    return high, mid, low


def inverse_factor(t, out_ref, between):
    q, n, _ = t.shape
    lane = lax.broadcasted_iota(jnp.int32, (PANEL, n), 1)
    sub = lax.broadcasted_iota(jnp.int32, (PANEL, n), 0)
    for panel in range(n // PANEL):
        base, end = panel * PANEL, (panel + 1) * PANEL
        scaled = eliminate(t[:, :PANEL, :], base)
        for r in range(q):
            out_ref[r, base:end, :] = jnp.where(lane <= sub + base, scaled[r], 0.0)
        if end < n:
            rest = []
            for r in range(q):
                row = jnp.where((lane >= end) | (lane <= sub + base), scaled[r], 0.0)
                h, m, l = parts(row)
                update = tdot(
                    jnp.concatenate([h, h, h, m, m, l], 0), jnp.concatenate([h, m, l, h, m, h], 0)
                )[end:, :]
                low = t[r, PANEL:, :]
                lanes = lax.broadcasted_iota(jnp.int32, low.shape, 1)
                rest.append(jnp.where((lanes >= base) & (lanes < end), 0.0, low) - update)
            t = jnp.stack(rest)
            between(panel)


def penalty(w_ref, r, lab):
    total = jnp.zeros(lab.shape, jnp.float32)
    for g in range(GROUPS):
        total = jnp.where(lab == g, w_ref[r, g], total)
    return total


def tdot(a, b):
    return lax.dot_general(a, b, (((0,), (0,)), ((), ())), preferred_element_type=jnp.float32)


def stack_left(x):
    h, m, l = parts(x)
    return jnp.concatenate([h, h, h, m, m, l], axis=1)


def stack_right(x, axis):
    h, m, l = parts(x)
    return jnp.concatenate([h, m, l, h, m, h], axis=axis)


def dot(a, b):
    return jnp.dot(a, b, preferred_element_type=jnp.float32)


def dot_nt(a, b):
    return lax.dot_general(a, b, (((1,), (1,)), ((), ())), preferred_element_type=jnp.float32)


def solve_kernel(
    weights_hbm, choice_hbm, labc_hbm, at_ref, st_ref, grs_ref, grc_ref, gsc_ref, y_ref, labs_ref, inv_ref,
    trail_ref, sides_ref, weights_ref, choice_ref, labc_ref, sem,
):
    small = [
        pltpu.make_async_copy(weights_hbm, weights_ref, sem.at[0]),
        pltpu.make_async_copy(choice_hbm, choice_ref, sem.at[1]),
        pltpu.make_async_copy(labc_hbm, labc_ref, sem.at[2]),
    ]
    for copy in small:
        copy.start()
    t, f, v = lax.axis_index("tm"), lax.axis_index("feat"), lax.axis_index("vox")
    row = t * 2 + f
    rows, voxels = sides_ref.shape
    y = y_ref[...]
    sside = dot(st_ref[...], y) * (1.0 / math.sqrt(TIME))
    sside6 = stack_right(sside, 0)
    for copy in small:
        copy.wait()

    eye = lax.broadcasted_iota(jnp.int32, (CB, CB), 0) == lax.broadcasted_iota(jnp.int32, (CB, CB), 1)
    r_sub = lax.broadcasted_iota(jnp.int32, (rows, CB), 0) + row * rows
    r_lane = lax.broadcasted_iota(jnp.int32, (rows, CB), 1)
    group = lax.broadcasted_iota(jnp.int32, (1, voxels), 1) // GROUP
    ridge = jnp.zeros((1, voxels), jnp.int32)
    for g in range(voxels // GROUP):
        ridge = jnp.where(group == g, choice_ref[g], ridge)

    panels, solved = [], []
    for r in range(2):
        inv = inv_ref[r]
        left = stack_left(inv)
        pen_s = jnp.broadcast_to(penalty(weights_ref, r, labs_ref[...]), (rows, CB))
        pen_c = jnp.broadcast_to(penalty(weights_ref, r, labc_ref[...]), (rows, CB))
        grs_r = grs_ref[...] + jnp.where(r_sub == r_lane, pen_s, 0.0)
        gsc_r = gsc_ref[...] + jnp.where(eye & (v == 0), pen_c[:CB], 0.0)
        panel = stack_left(dot_nt(stack_left(grs_r), stack_right(inv, 1)))
        partner = dot(left, stack_right(gsc_r, 0))
        system = grc_ref[...] + jnp.where(r_sub == r_lane + v * CB, pen_c, 0.0)
        trail_ref[r] = system - dot(panel, stack_right(partner, 0))
        panels.append(panel)
        solved.append(jnp.where(ridge == r, dot(left, sside6), 0.0))
    update = dot(
        jnp.concatenate(panels, 1), jnp.concatenate([stack_right(solved[0], 0), stack_right(solved[1], 0)], 0)
    )
    sides_ref[...] = dot(at_ref[...], y) * (1.0 / math.sqrt(TIME)) - update

    @pl.when(row == 0)
    def _():
        sides_ref[0:CB, :] = solved[0] + solved[1]


def solve(weights, choice, labc, at, st, grs, grc, gsc, y, labs, inv):
    vmem = pl.BlockSpec(memory_space=pltpu.VMEM)
    hbm = pl.BlockSpec(memory_space=pltpu.HBM)
    rows, voxels = at.shape[0], y.shape[1]
    return pl.pallas_call(
        solve_kernel,
        out_shape=[
            jax.ShapeDtypeStruct((2, rows, CB), jnp.float32),
            jax.ShapeDtypeStruct((rows, voxels), jnp.float32),
        ],
        in_specs=[hbm] * 3 + [vmem] * 8,
        out_specs=[vmem] * 2,
        scratch_shapes=[
            pltpu.SMEM(weights.shape, jnp.float32),
            pltpu.SMEM(choice.shape, jnp.int32),
            pltpu.VMEM((1, CB), jnp.int32),
            pltpu.SemaphoreType.DMA((3,)),
        ],
        compiler_params=pltpu.CompilerParams(vmem_limit_bytes=32 << 20),
        name="solve",
    )(*in_hbm(weights, choice, labc), at, st, grs, grc, gsc, y, labs, inv)


def local(design, signals, label, weights, choice):
    lab = label.reshape(1, CB)
    at, st, grs, grc, gsc, y, labs, inv = gather(design, signals, lab, weights)
    return solve(weights, choice, lab, at, st, grs, grc, gsc, y, labs, inv)


def solution(mesh):
    return jax.shard_map(
        local,
        mesh=mesh,
        in_specs=(P(None, ("tm", "feat")), P("tm", "vox"), P("vox"), P(), P("vox")),
        out_specs=(P(None, ("tm", "feat"), "vox"), P(("tm", "feat"), "vox")),
        check_vma=False,
    )
```

```python
import math

import jax
import jax.numpy as jnp
from jax import lax
from jax.experimental import pallas as pl
from jax.experimental.pallas import tpu as pltpu
from jax.sharding import PartitionSpec as P

TIME = 1024
GROUPS = 4
CB = 128
GROUP = 64
OFFSETS = [(dy, dx) for dy in range(2) for dx in range(4)][1:]
MESH = pl.DeviceIdType.MESH


def peer(t, dy, dx):
    y, x = t // 4, t % 4
    return ((y + dy) % 2) * 4 + (x + dx) % 4


def remote(src, dst, send, recv, **where):
    return pltpu.make_async_remote_copy(
        src_ref=src, dst_ref=dst, send_sem=send, recv_sem=recv, device_id=where, device_id_type=MESH
    )


class Place:
    def __init__(self):
        self.t, self.f, self.v = lax.axis_index("tm"), lax.axis_index("feat"), lax.axis_index("vox")
        self.zero = self.v == 0
        self.mover = self.f == jnp.where(self.t == 0, 1, 0)
        self.plain = self.v != 0
        self.single = self.zero & self.mover
        self.server = self.zero & jnp.logical_not(self.mover)

    def core(self, t, own):
        return jnp.where(self.zero, jnp.where(t == 0, 1, 0), own)

    def chip(self, p):
        return dict(tm=p, feat=self.core(p, self.f))


class Spread:
    def __init__(self, here, buf, to, fo, sem, extra=None):
        self.here, self.buf, self.t, self.f, self.extra = here, buf, here.t, here.f, extra
        to = jnp.where(here.zero, -1, to)
        self.to = to
        self.scatter, self.scatter_r, self.own, self.own_r, self.ag, self.ag_r, self.sib, self.sib_r = sem
        on = self.f == here.core(self.t, fo)
        self.owner = (self.t == to) & on
        self.relay = (self.t != to) & on
        self.side = (self.t != to) & jnp.logical_not(on)
        self.owner_side = (self.t == to) & jnp.logical_not(on)

    def chunk(self, t):
        return self.buf.at[pl.ds(pl.multiple_of(t * 128, 128), 128), :]

    def c_scatter(self, k):
        p = peer(self.t, *OFFSETS[k])
        c = self.chunk(p)
        return remote(c, c, self.scatter.at[k], self.scatter_r, **self.here.chip(p))

    def c_scatter_in(self):
        c = self.chunk(self.t)
        return remote(c, c, self.scatter.at[0], self.scatter_r, **self.here.chip(self.to))

    def c_own(self, k):
        p = peer(self.t, *OFFSETS[k])
        c = self.chunk(self.t)
        return remote(c, c, self.own.at[k], self.own_r, **self.here.chip(p))

    def c_own_in(self):
        c = self.chunk(self.to)
        return remote(c, c, self.own.at[0], self.own_r, **self.here.chip(self.to))

    def c_ag(self, k):
        p = peer(self.t, *OFFSETS[k])
        c = self.chunk(self.t)
        return p, remote(c, c, self.ag.at[k], self.ag_r.at[k], **self.here.chip(p))

    def c_ag_in(self, k):
        dy, dx = OFFSETS[k]
        p = peer(self.t, dy, 4 - dx)
        c = self.chunk(p)
        return p, remote(c, c, self.ag.at[k], self.ag_r.at[k], **self.here.chip(p))

    def c_sib(self, k, p):
        c = self.chunk(p)
        return remote(c, c, self.sib.at[k], self.sib_r.at[k], feat=1 - self.f)

    def c_whole(self):
        return remote(self.buf, self.buf, self.sib.at[0], self.sib_r.at[0], feat=1 - self.f)

    def pass_on(self, act):
        if self.extra is not None:

            @pl.when(self.here.v == 1)
            def _():
                c = self.chunk(self.t)
                feat = jnp.where(self.t == 0, 1, 0)
                act(remote(c, c, self.extra, self.scatter_r, feat=feat, vox=0))

    def start(self):
        @pl.when(self.owner)
        def _():
            for k in range(7):
                self.c_scatter(k).start()
            for k in range(7):
                self.c_own(k).start()
            self.c_whole().start()
            self.pass_on(lambda c: c.start())

    def forward(self):
        @pl.when(self.relay)
        def _():
            self.c_scatter_in().wait_recv()
            self.pass_on(lambda c: c.start())
            for k in range(7):
                p, c = self.c_ag(k)

                @pl.when(p != self.to)
                def _():
                    c.start()

            self.c_sib(7, self.t).start()

    def collect(self):
        @pl.when(self.relay)
        def _():
            for k in range(7):
                p, c = self.c_ag_in(k)

                @pl.when(p != self.to)
                def _():
                    c.wait_recv()

                @pl.when(p == self.to)
                def _():
                    self.c_own_in().wait_recv()

                self.c_sib(k, p).start()

    def arrive(self):
        @pl.when(self.owner_side)
        def _():
            self.c_whole().wait_recv()

        @pl.when(self.side)
        def _():
            for k in range(7):
                dy, dx = OFFSETS[k]
                self.c_sib(k, peer(self.t, dy, 4 - dx)).wait_recv()
            self.c_sib(7, self.t).wait_recv()

    def finish(self):
        @pl.when(self.owner)
        def _():
            for k in range(7):
                self.c_scatter(k).wait_send()
                self.c_own(k).wait_send()
            self.c_whole().wait_send()
            self.pass_on(lambda c: c.wait_send())

        @pl.when(self.relay)
        def _():
            for k in range(7):
                p, c = self.c_ag(k)

                @pl.when(p != self.to)
                def _():
                    c.wait_send()

                q, _c = self.c_ag_in(k)
                self.c_sib(k, q).wait_send()
            self.c_sib(7, self.t).wait_send()
            self.pass_on(lambda c: c.wait_send())


def spread_sems():
    dma = pltpu.SemaphoreType.DMA
    return [dma((7,)), dma, dma((7,)), dma, dma((7,)), dma((7,)), dma((8,)), dma((8,))]


def gather_kernel(
    a_hbm, y_ref, lab_ref, w_hbm,
    at_ref, st_ref, grs_ref, grc_ref, gsc_ref, yall_ref, labs_ref, inv_ref,
    w_ref, a_ref, s_ref, c_ref, *sems,
):
    s_sem, c_sem, rest = sems[:8], sems[8:16], sems[16:]
    ysend, yrecv, bsend, brecv, lsend, lrecv, copy_sem, extra_sem, ready = rest
    here = Place()
    t, f, v = here.t, here.f, here.v
    plain, single, server = here.plain, here.single, here.server
    row = t * 2 + f
    to, fo = v // 4, (v // 2) % 2
    owner_s, owner_c = plain & (row == 0), plain & (t == to) & (f == fo)
    first_single, first_server = single & (t == 0), server & (t == 0)
    barrier = pltpu.get_barrier_semaphore()

    def signal(**where):
        pl.semaphore_signal(barrier, inc=1, device_id=where, device_id_type=MESH)

    @pl.when(plain)
    def _():
        signal(tm=v // 4, feat=jnp.where(v // 4 == 0, 0, 1), vox=0)

    @pl.when(plain | single)
    def _():
        for offset in OFFSETS:
            signal(**here.chip(peer(t, *offset)))

    @pl.when(plain | (server & (t != 0)) | first_single)
    def _():
        signal(feat=1 - f)

    extra = (v == 1) & (f == 0)

    @pl.when(single)
    def _():
        signal(feat=0, vox=1)

    get_s = pltpu.make_async_copy(a_hbm.at[:, pl.ds(0, CB)], s_ref, copy_sem.at[0])
    get_c = pltpu.make_async_copy(
        a_hbm.at[:, pl.ds(pl.multiple_of((v % 2) * CB, CB), CB)], c_ref, copy_sem.at[1]
    )
    get_y = pltpu.make_async_copy(
        y_ref, yall_ref.at[pl.ds(pl.multiple_of(t * 128, 128), 128), :], copy_sem.at[2]
    )
    get_lab = pltpu.make_async_copy(lab_ref, labs_ref, copy_sem.at[3])
    get_w = pltpu.make_async_copy(w_hbm, w_ref, copy_sem.at[4])
    get_a = pltpu.make_async_copy(a_hbm, a_ref, copy_sem.at[5])

    @pl.when(owner_s)
    def _():
        get_s.start()

    @pl.when(owner_c)
    def _():
        get_c.start()

    get_y.start()
    get_w.start()
    get_a.start()

    @pl.when(v == 0)
    def _():
        get_lab.start()
        get_lab.wait()

    @pl.when(owner_s)
    def _():
        get_s.wait()

    @pl.when(owner_c)
    def _():
        get_c.wait()

    get_y.wait()
    get_w.wait()

    def transpose():
        get_a.wait()
        at_ref[...] = a_ref[...].T

    @pl.when(plain | single)
    def _():
        transpose()

    @pl.when(extra)
    def _():
        pl.semaphore_wait(barrier, 9)

    @pl.when((plain & jnp.logical_not(extra)) | (single & (t != 0)))
    def _():
        pl.semaphore_wait(barrier, 8)

    @pl.when(first_single)
    def _():
        pl.semaphore_wait(barrier, 7)

    @pl.when(server & (t != 0))
    def _():
        pl.semaphore_wait(barrier, 64)

    @pl.when(first_server)
    def _():
        pl.semaphore_wait(barrier, 49)
        pl.semaphore_signal(ready, inc=1, device_id={"feat": 1}, device_id_type=MESH)

    first = jnp.where(t == 0, 16, 0)

    def c_lab(i):
        where = dict(tm=i // 2 % 8, feat=i % 2, vox=t * 4 + i // 16)
        return remote(labs_ref, labs_ref, lsend.at[i], lrecv, **where)

    @pl.when(server)
    def _():
        @pl.loop(first, 64)
        def _(i):
            c_lab(i).start()

        transpose()

    spread_s = Spread(here, s_ref, 0, 0, s_sem, extra_sem)
    spread_c = Spread(here, c_ref, to, fo, c_sem)

    def c_do(name):
        @pl.when(plain)
        def _():
            getattr(spread_c, name)()

    spread_s.start()
    c_do("start")

    def yblock(q, g):
        return yall_ref.at[pl.ds(pl.multiple_of(q * 128 + g * 64, 64), 64), :]

    def yslab(q):
        return yall_ref.at[pl.ds(pl.multiple_of(q * 128, 128), 128), :]

    def source(k):
        dy, dx = OFFSETS[k]
        return peer(t, dy, 4 - dx)

    def c_y(k, b):
        return remote(b, b, ysend.at[k], yrecv.at[k], **here.chip(peer(t, *OFFSETS[k])))

    def c_yout(k, b):
        return remote(b, b, bsend.at[k], brecv.at[k], feat=1 - f)

    def y_start(ks):
        @pl.when(plain)
        def _():
            for k in ks:
                c_y(k, yblock(t, f)).start()

        @pl.when(single)
        def _():
            for k in ks:
                c_y(k, yslab(t)).start()

    def y_collect(ks):
        @pl.when(plain)
        def _():
            for k in ks:
                b = yblock(source(k), f)
                c_y(k, b).wait_recv()
                c_yout(k, b).start()

        @pl.when(single)
        def _():
            for k in ks:
                b = yslab(source(k))
                c_y(k, b).wait_recv()
                c_yout(k, b).start()

    y_start((0, 2))

    @pl.when(first_single)
    def _():
        pl.semaphore_wait(ready, 1)

    spread_s.forward()
    c_do("forward")
    y_start((3, 1, 4, 6, 5))

    spread_s.collect()
    spread_s.arrive()

    @pl.when(plain)
    def _():
        c_lab(0).wait_recv()

    s_all = s_ref[...]
    st_ref[...] = s_all.T
    gram = dot(st_ref[...], s_all) * (1.0 / TIME)
    eye = lax.broadcasted_iota(jnp.int32, (CB, CB), 0) == lax.broadcasted_iota(jnp.int32, (CB, CB), 1)
    matrices = []
    for r in range(2):
        pen = jnp.broadcast_to(penalty(w_ref, r, labs_ref[...]), (CB, CB))
        matrices.append(gram + jnp.where(eye, pen, 0.0))

    def between(panel):
        if panel == 0:
            c_do("collect")
        elif panel == 1:
            y_collect((0, 2, 3))
        elif panel == 2:
            y_collect((1, 4, 6, 5))

    inverse_factor(jnp.stack(matrices), inv_ref, between)
    grs_ref[...] = dot(at_ref[...], s_all) * (1.0 / TIME)
    c_do("arrive")

    @pl.when(here.zero)
    def _():
        c_ref[...] = s_ref[...]

    c_all = c_ref[...]
    grc_ref[...] = dot(at_ref[...], c_all) * (1.0 / TIME)
    gsc_ref[...] = dot(st_ref[...], c_all) * (1.0 / TIME)
    spread_s.finish()
    c_do("finish")

    @pl.when(plain)
    def _():
        for k in range(7):
            c_y(k, yblock(t, f)).wait_send()
            c_yout(k, yblock(source(k), f)).wait_send()
            c_yout(k, yblock(source(k), 1 - f)).wait_recv()

    @pl.when(single)
    def _():
        for k in range(7):
            c_y(k, yslab(t)).wait_send()
            c_yout(k, yslab(source(k))).wait_send()

    @pl.when(server)
    def _():
        for k in range(7):
            c_yout(k, yslab(source(k))).wait_recv()

        @pl.loop(first, 64)
        def _(i):
            c_lab(i).wait_send()


def in_hbm(*arrays):
    return [pltpu.with_memory_space_constraint(x, pltpu.HBM) for x in arrays]


def gather(a, y, lab, w):
    dma = pltpu.SemaphoreType.DMA
    vmem = pl.BlockSpec(memory_space=pltpu.VMEM)
    hbm = pl.BlockSpec(memory_space=pltpu.HBM)
    rows, voxels = a.shape[1], y.shape[1]
    return pl.pallas_call(
        gather_kernel,
        out_shape=[
            jax.ShapeDtypeStruct((rows, TIME), jnp.bfloat16),
            jax.ShapeDtypeStruct((CB, TIME), jnp.bfloat16),
            jax.ShapeDtypeStruct((rows, CB), jnp.float32),
            jax.ShapeDtypeStruct((rows, CB), jnp.float32),
            jax.ShapeDtypeStruct((CB, CB), jnp.float32),
            jax.ShapeDtypeStruct((TIME, voxels), jnp.bfloat16),
            jax.ShapeDtypeStruct((1, CB), jnp.int32),
            jax.ShapeDtypeStruct((2, CB, CB), jnp.float32),
        ],
        in_specs=[hbm] * 4,
        out_specs=[vmem] * 8,
        scratch_shapes=[
            pltpu.SMEM(w.shape, jnp.float32),
            pltpu.VMEM(a.shape, jnp.bfloat16),
            pltpu.VMEM((TIME, CB), jnp.bfloat16),
            pltpu.VMEM((TIME, CB), jnp.bfloat16),
        ]
        + spread_sems()
        + spread_sems()
        + [dma((7,)), dma((7,)), dma((7,)), dma((7,)), dma((64,)), dma, dma((6,))]
        + [dma, pltpu.SemaphoreType.REGULAR],
        compiler_params=pltpu.CompilerParams(
            collective_id=0, has_side_effects=True, vmem_limit_bytes=24 << 20
        ),
        name="gather",
    )(*in_hbm(a, y, lab, w))


PANEL = 32


def eliminate(t, base):
    q, height, n = t.shape
    lane8 = lax.broadcasted_iota(jnp.int32, (q, 8, n), 2)
    sub8 = lax.broadcasted_iota(jnp.int32, (q, 8, n), 1)
    out = []
    for step in range(height // 8):
        o = base + 8 * step
        block = t[:, :8, :]
        cols = [jnp.broadcast_to(block[:, :, o + p : o + p + 1], (q, 8, n)) for p in range(8)]
        inside = (lane8 >= o) & (lane8 < o + 8)
        block = jnp.where(inside, jnp.where(lane8 == o + sub8, 1.0, 0.0), block)
        invs, rrows, crows = [], [], []
        scale = jnp.zeros((q, 8, n), jnp.float32)
        for p in range(8):
            crow = {k: jnp.broadcast_to(cols[k][:, p : p + 1, :], (q, 8, n)) for k in range(p, 8)}
            rrow = jnp.broadcast_to(block[:, p : p + 1, :], (q, 8, n))
            inv = 1.0 / crow[p]
            scale = jnp.where(sub8 == p, lax.rsqrt(crow[p]), scale)
            factor = jnp.where(sub8 > p, cols[p] * inv, 0.0)
            block = block - factor * rrow
            for k in range(p + 1, 8):
                cols[k] = cols[k] - factor * crow[k]
            invs.append(inv)
            rrows.append(rrow)
            crows.append(crow)
        out.append(block * scale)
        rest = t.shape[1] - 8
        if rest:
            low = t[:, 8:, :].reshape(q, rest // 8, 8, n)
            cols = [
                jnp.broadcast_to(low[:, :, :, o + p : o + p + 1], (q, rest // 8, 8, n)) for p in range(8)
            ]
            lane = lax.broadcasted_iota(jnp.int32, low.shape, 3)
            low = jnp.where((lane >= o) & (lane < o + 8), 0.0, low)
            for p in range(8):
                factor = cols[p] * invs[p][:, None]
                low = low - factor * rrows[p][:, None]
                for k in range(p + 1, 8):
                    cols[k] = cols[k] - factor * crows[p][k][:, None]
            t = low.reshape(q, rest, n)
    return jnp.concatenate(out, axis=1)


def parts(x):
    high = x.astype(jnp.bfloat16)
    rest = x - high.astype(jnp.float32)
    mid = rest.astype(jnp.bfloat16)
    low = (rest - mid.astype(jnp.float32)).astype(jnp.bfloat16)
    return high, mid, low


def inverse_factor(t, out_ref, between):
    q, n, _ = t.shape
    lane = lax.broadcasted_iota(jnp.int32, (PANEL, n), 1)
    sub = lax.broadcasted_iota(jnp.int32, (PANEL, n), 0)
    for panel in range(n // PANEL):
        base, end = panel * PANEL, (panel + 1) * PANEL
        scaled = eliminate(t[:, :PANEL, :], base)
        for r in range(q):
            out_ref[r, base:end, :] = jnp.where(lane <= sub + base, scaled[r], 0.0)
        if end < n:
            rest = []
            for r in range(q):
                row = jnp.where((lane >= end) | (lane <= sub + base), scaled[r], 0.0)
                h, m, l = parts(row)
                update = tdot(
                    jnp.concatenate([h, h, h, m, m, l], 0), jnp.concatenate([h, m, l, h, m, h], 0)
                )[end:, :]
                low = t[r, PANEL:, :]
                lanes = lax.broadcasted_iota(jnp.int32, low.shape, 1)
                rest.append(jnp.where((lanes >= base) & (lanes < end), 0.0, low) - update)
            t = jnp.stack(rest)
            between(panel)


def penalty(w_ref, r, lab):
    total = jnp.zeros(lab.shape, jnp.float32)
    for g in range(GROUPS):
        total = jnp.where(lab == g, w_ref[r, g], total)
    return total


def tdot(a, b):
    return lax.dot_general(a, b, (((0,), (0,)), ((), ())), preferred_element_type=jnp.float32)


def stack_left(x):
    h, m, l = parts(x)
    return jnp.concatenate([h, h, h, m, m, l], axis=1)


def stack_right(x, axis):
    h, m, l = parts(x)
    return jnp.concatenate([h, m, l, h, m, h], axis=axis)


def dot(a, b):
    return jnp.dot(a, b, preferred_element_type=jnp.float32)


def dot_nt(a, b):
    return lax.dot_general(a, b, (((1,), (1,)), ((), ())), preferred_element_type=jnp.float32)


def solve_kernel(
    weights_hbm, choice_hbm, labc_hbm, at_ref, st_ref, grs_ref, grc_ref, gsc_ref, y_ref, labs_ref, inv_ref,
    trail_ref, sides_ref, weights_ref, choice_ref, labc_ref, sem,
):
    small = [
        pltpu.make_async_copy(weights_hbm, weights_ref, sem.at[0]),
        pltpu.make_async_copy(choice_hbm, choice_ref, sem.at[1]),
        pltpu.make_async_copy(labc_hbm, labc_ref, sem.at[2]),
    ]
    for copy in small:
        copy.start()
    t, f, v = lax.axis_index("tm"), lax.axis_index("feat"), lax.axis_index("vox")
    row = t * 2 + f
    rows, voxels = sides_ref.shape
    y = y_ref[...]
    sside = dot(st_ref[...], y) * (1.0 / math.sqrt(TIME))
    sside6 = stack_right(sside, 0)
    for copy in small:
        copy.wait()

    eye = lax.broadcasted_iota(jnp.int32, (CB, CB), 0) == lax.broadcasted_iota(jnp.int32, (CB, CB), 1)
    r_sub = lax.broadcasted_iota(jnp.int32, (rows, CB), 0) + row * rows
    r_lane = lax.broadcasted_iota(jnp.int32, (rows, CB), 1)
    group = lax.broadcasted_iota(jnp.int32, (1, voxels), 1) // GROUP
    ridge = jnp.zeros((1, voxels), jnp.int32)
    for g in range(voxels // GROUP):
        ridge = jnp.where(group == g, choice_ref[g], ridge)

    panels, solved = [], []
    for r in range(2):
        inv = inv_ref[r]
        left = stack_left(inv)
        pen_s = jnp.broadcast_to(penalty(weights_ref, r, labs_ref[...]), (rows, CB))
        pen_c = jnp.broadcast_to(penalty(weights_ref, r, labc_ref[...]), (rows, CB))
        grs_r = grs_ref[...] + jnp.where(r_sub == r_lane, pen_s, 0.0)
        gsc_r = gsc_ref[...] + jnp.where(eye & (v == 0), pen_c[:CB], 0.0)
        panel = stack_left(dot_nt(stack_left(grs_r), stack_right(inv, 1)))
        partner = dot(left, stack_right(gsc_r, 0))
        system = grc_ref[...] + jnp.where(r_sub == r_lane + v * CB, pen_c, 0.0)
        trail_ref[r] = system - dot(panel, stack_right(partner, 0))
        panels.append(panel)
        solved.append(jnp.where(ridge == r, dot(left, sside6), 0.0))
    update = dot(
        jnp.concatenate(panels, 1), jnp.concatenate([stack_right(solved[0], 0), stack_right(solved[1], 0)], 0)
    )
    sides_ref[...] = dot(at_ref[...], y) * (1.0 / math.sqrt(TIME)) - update

    @pl.when(row == 0)
    def _():
        sides_ref[0:CB, :] = solved[0] + solved[1]


def solve(weights, choice, labc, at, st, grs, grc, gsc, y, labs, inv):
    vmem = pl.BlockSpec(memory_space=pltpu.VMEM)
    hbm = pl.BlockSpec(memory_space=pltpu.HBM)
    rows, voxels = at.shape[0], y.shape[1]
    return pl.pallas_call(
        solve_kernel,
        out_shape=[
            jax.ShapeDtypeStruct((2, rows, CB), jnp.float32),
            jax.ShapeDtypeStruct((rows, voxels), jnp.float32),
        ],
        in_specs=[hbm] * 3 + [vmem] * 8,
        out_specs=[vmem] * 2,
        scratch_shapes=[
            pltpu.SMEM(weights.shape, jnp.float32),
            pltpu.SMEM(choice.shape, jnp.int32),
            pltpu.VMEM((1, CB), jnp.int32),
            pltpu.SemaphoreType.DMA((3,)),
        ],
        compiler_params=pltpu.CompilerParams(vmem_limit_bytes=32 << 20),
        name="solve",
    )(*in_hbm(weights, choice, labc), at, st, grs, grc, gsc, y, labs, inv)


def local(design, signals, label, weights, choice):
    lab = label.reshape(1, CB)
    at, st, grs, grc, gsc, y, labs, inv = gather(design, signals, lab, weights)
    return solve(weights, choice, lab, at, st, grs, grc, gsc, y, labs, inv)


def solution(mesh):
    return jax.shard_map(
        local,
        mesh=mesh,
        in_specs=(P(None, ("tm", "feat")), P("tm", "vox"), P("vox"), P(), P("vox")),
        out_specs=(P(None, ("tm", "feat"), "vox"), P(("tm", "feat"), "vox")),
        check_vma=False,
    )
```

```python
import math

import jax
import jax.numpy as jnp
from jax import lax
from jax.experimental import pallas as pl
from jax.experimental.pallas import tpu as pltpu
from jax.sharding import PartitionSpec as P

TIME = 1024
GROUPS = 4
CB = 128
GROUP = 64
OFFSETS = [(dy, dx) for dy in range(2) for dx in range(4)][1:]
MESH = pl.DeviceIdType.MESH


def peer(t, dy, dx):
    y, x = t // 4, t % 4
    return ((y + dy) % 2) * 4 + (x + dx) % 4


def remote(src, dst, send, recv, **where):
    return pltpu.make_async_remote_copy(
        src_ref=src, dst_ref=dst, send_sem=send, recv_sem=recv, device_id=where, device_id_type=MESH
    )


class Spread:
    def __init__(self, buf, t, f, to, fo, sem):
        self.buf, self.t, self.f, self.to = buf, t, f, to
        self.scatter, self.scatter_r, self.own, self.own_r, self.ag, self.ag_r, self.sib, self.sib_r = sem
        on = f == fo
        self.owner = (self.t == to) & on
        self.relay = (self.t != to) & on
        self.side = (self.t != to) & jnp.logical_not(on)
        self.owner_side = (self.t == to) & jnp.logical_not(on)

    def chunk(self, t):
        return self.buf.at[pl.ds(pl.multiple_of(t * 128, 128), 128), :]

    def c_scatter(self, k):
        p = peer(self.t, *OFFSETS[k])
        c = self.chunk(p)
        return remote(c, c, self.scatter.at[k], self.scatter_r, tm=p)

    def c_scatter_in(self):
        c = self.chunk(self.t)
        return remote(c, c, self.scatter.at[0], self.scatter_r, tm=self.to)

    def c_own(self, k):
        p = peer(self.t, *OFFSETS[k])
        c = self.chunk(self.t)
        return remote(c, c, self.own.at[k], self.own_r, tm=p)

    def c_own_in(self):
        c = self.chunk(self.to)
        return remote(c, c, self.own.at[0], self.own_r, tm=self.to)

    def c_ag(self, k):
        p = peer(self.t, *OFFSETS[k])
        c = self.chunk(self.t)
        return p, remote(c, c, self.ag.at[k], self.ag_r.at[k], tm=p)

    def c_ag_in(self, k):
        dy, dx = OFFSETS[k]
        p = peer(self.t, dy, 4 - dx)
        c = self.chunk(p)
        return p, remote(c, c, self.ag.at[k], self.ag_r.at[k], tm=p)

    def c_sib(self, k, p):
        c = self.chunk(p)
        return remote(c, c, self.sib.at[k], self.sib_r.at[k], feat=1 - self.f)

    def c_whole(self):
        return remote(self.buf, self.buf, self.sib.at[0], self.sib_r.at[0], feat=1 - self.f)

    def start(self):
        @pl.when(self.owner)
        def _():
            for k in range(7):
                self.c_scatter(k).start()
            for k in range(7):
                self.c_own(k).start()
            self.c_whole().start()

    def forward(self):
        @pl.when(self.relay)
        def _():
            self.c_scatter_in().wait_recv()
            for k in range(7):
                p, c = self.c_ag(k)

                @pl.when(p != self.to)
                def _():
                    c.start()

            self.c_sib(7, self.t).start()

    def collect(self):
        @pl.when(self.relay)
        def _():
            for k in range(7):
                p, c = self.c_ag_in(k)

                @pl.when(p != self.to)
                def _():
                    c.wait_recv()

                @pl.when(p == self.to)
                def _():
                    self.c_own_in().wait_recv()

                self.c_sib(k, p).start()

    def arrive(self):
        @pl.when(self.owner_side)
        def _():
            self.c_whole().wait_recv()

        @pl.when(self.side)
        def _():
            for k in range(7):
                dy, dx = OFFSETS[k]
                self.c_sib(k, peer(self.t, dy, 4 - dx)).wait_recv()
            self.c_sib(7, self.t).wait_recv()

    def finish(self):
        @pl.when(self.owner)
        def _():
            for k in range(7):
                self.c_scatter(k).wait_send()
                self.c_own(k).wait_send()
            self.c_whole().wait_send()

        @pl.when(self.relay)
        def _():
            for k in range(7):
                p, c = self.c_ag(k)

                @pl.when(p != self.to)
                def _():
                    c.wait_send()

                q, _c = self.c_ag_in(k)
                self.c_sib(k, q).wait_send()
            self.c_sib(7, self.t).wait_send()


def spread_sems():
    dma = pltpu.SemaphoreType.DMA
    return [dma((7,)), dma, dma((7,)), dma, dma((7,)), dma((7,)), dma((8,)), dma((8,))]


def gather_kernel(
    a_hbm, y_ref, lab_ref, w_hbm,
    at_ref, st_ref, grs_ref, grc_ref, gsc_ref, yall_ref, labs_ref, inv_ref,
    w_ref, a_ref, s_ref, c_ref, *sems,
):
    s_sem, c_sem, rest = sems[:8], sems[8:16], sems[16:]
    ysend, yrecv, bsend, brecv, lsend, lrecv, copy_sem, ready = rest
    t, f, v = lax.axis_index("tm"), lax.axis_index("feat"), lax.axis_index("vox")
    row = t * 2 + f
    to, fo = v // 4, (v // 2) % 2
    other = v != 0
    server = (v == 0) & (f == 1)
    owner_s, owner_c = row == 0, other & (t == to) & (f == fo)
    last_in = (v == 0) & (row == 0)
    barrier = pltpu.get_barrier_semaphore()

    def signal(**where):
        pl.semaphore_signal(barrier, inc=1, device_id=where, device_id_type=MESH)

    for offset in OFFSETS:
        signal(tm=peer(t, *offset))
    signal(feat=1 - f)

    first = jnp.where(t == 0, 16, 0)

    def client(i):
        return dict(tm=i // 2 % 8, feat=i % 2, vox=t * 4 + i // 16)

    @pl.when(server)
    def _():
        @pl.loop(first, 64)
        def _(i):
            signal(**client(i))

    get_s = pltpu.make_async_copy(a_hbm.at[:, pl.ds(0, CB)], s_ref, copy_sem.at[0])
    get_c = pltpu.make_async_copy(
        a_hbm.at[:, pl.ds(pl.multiple_of((v % 2) * CB, CB), CB)], c_ref, copy_sem.at[1]
    )
    get_y = pltpu.make_async_copy(
        y_ref, yall_ref.at[pl.ds(pl.multiple_of(t * 128, 128), 128), :], copy_sem.at[2]
    )
    get_lab = pltpu.make_async_copy(lab_ref, labs_ref, copy_sem.at[3])
    get_w = pltpu.make_async_copy(w_hbm, w_ref, copy_sem.at[4])
    get_a = pltpu.make_async_copy(a_hbm, a_ref, copy_sem.at[5])

    @pl.when(owner_s)
    def _():
        get_s.start()

    @pl.when(owner_c)
    def _():
        get_c.start()

    get_y.start()
    get_w.start()
    get_a.start()

    @pl.when(v == 0)
    def _():
        get_lab.start()
        get_lab.wait()

    @pl.when(owner_s)
    def _():
        get_s.wait()

    @pl.when(owner_c)
    def _():
        get_c.wait()

    get_y.wait()
    get_w.wait()

    def transpose():
        get_a.wait()
        at_ref[...] = a_ref[...].T

    @pl.when(jnp.logical_not(last_in))
    def _():
        transpose()

    @pl.when(v == 0)
    def _():
        pl.semaphore_wait(barrier, 8)

    @pl.when(other)
    def _():
        pl.semaphore_wait(barrier, 9)
        pl.semaphore_signal(
            ready, inc=1, device_id={"tm": v // 4, "feat": 1, "vox": 0}, device_id_type=MESH
        )

    def c_lab(i):
        return remote(labs_ref, labs_ref, lsend.at[i], lrecv, **client(i))

    spread_s = Spread(s_ref, t, f, 0, 0, s_sem)
    spread_c = Spread(c_ref, t, f, to, fo, c_sem)

    def c_do(name):
        @pl.when(other)
        def _():
            getattr(spread_c, name)()

    spread_s.start()
    c_do("start")

    def yblock(q, g):
        return yall_ref.at[pl.ds(pl.multiple_of(q * 128 + g * 64, 64), 64), :]

    def source(k):
        dy, dx = OFFSETS[k]
        return peer(t, dy, 4 - dx)

    def c_y(k, b):
        return remote(b, b, ysend.at[k], yrecv.at[k], tm=peer(t, *OFFSETS[k]))

    def c_yout(k, b):
        return remote(b, b, bsend.at[k], brecv.at[k], feat=1 - f)

    def y_start(ks):
        for k in ks:
            c_y(k, yblock(t, f)).start()

    def y_collect(ks):
        for k in ks:
            b = yblock(source(k), f)
            c_y(k, b).wait_recv()
            c_yout(k, b).start()

    y_start((0, 2))

    @pl.when(last_in)
    def _():
        transpose()

    spread_s.forward()
    c_do("forward")
    y_start((3, 1, 4, 6, 5))

    spread_s.collect()
    spread_s.arrive()

    @pl.when(server & (t != 0))
    def _():
        pl.semaphore_wait(ready, 64)

    @pl.when(server & (t == 0))
    def _():
        pl.semaphore_wait(ready, 48)

    @pl.when(server)
    def _():
        @pl.loop(first, 64)
        def _(i):
            c_lab(i).start()

    @pl.when(other)
    def _():
        c_lab(0).wait_recv()

    s_all = s_ref[...]
    st_ref[...] = s_all.T
    gram = dot(st_ref[...], s_all) * (1.0 / TIME)
    eye = lax.broadcasted_iota(jnp.int32, (CB, CB), 0) == lax.broadcasted_iota(jnp.int32, (CB, CB), 1)
    matrices = []
    for r in range(2):
        pen = jnp.broadcast_to(penalty(w_ref, r, labs_ref[...]), (CB, CB))
        matrices.append(gram + jnp.where(eye, pen, 0.0))

    def between(panel):
        if panel == 0:
            c_do("collect")
        elif panel == 1:
            y_collect((0, 2, 3))
        elif panel == 2:
            y_collect((1, 4, 6, 5))

    inverse_factor(jnp.stack(matrices), inv_ref, between)
    grs_ref[...] = dot(at_ref[...], s_all) * (1.0 / TIME)
    c_do("arrive")

    @pl.when(v == 0)
    def _():
        c_ref[...] = s_ref[...]

    c_all = c_ref[...]
    grc_ref[...] = dot(at_ref[...], c_all) * (1.0 / TIME)
    gsc_ref[...] = dot(st_ref[...], c_all) * (1.0 / TIME)
    spread_s.finish()
    c_do("finish")

    for k in range(7):
        c_y(k, yblock(t, f)).wait_send()
        c_yout(k, yblock(source(k), f)).wait_send()
        c_yout(k, yblock(source(k), 1 - f)).wait_recv()

    @pl.when(server)
    def _():
        @pl.loop(first, 64)
        def _(i):
            c_lab(i).wait_send()


def in_hbm(*arrays):
    return [pltpu.with_memory_space_constraint(x, pltpu.HBM) for x in arrays]


def gather(a, y, lab, w):
    dma = pltpu.SemaphoreType.DMA
    vmem = pl.BlockSpec(memory_space=pltpu.VMEM)
    hbm = pl.BlockSpec(memory_space=pltpu.HBM)
    rows, voxels = a.shape[1], y.shape[1]
    return pl.pallas_call(
        gather_kernel,
        out_shape=[
            jax.ShapeDtypeStruct((rows, TIME), jnp.bfloat16),
            jax.ShapeDtypeStruct((CB, TIME), jnp.bfloat16),
            jax.ShapeDtypeStruct((rows, CB), jnp.float32),
            jax.ShapeDtypeStruct((rows, CB), jnp.float32),
            jax.ShapeDtypeStruct((CB, CB), jnp.float32),
            jax.ShapeDtypeStruct((TIME, voxels), jnp.bfloat16),
            jax.ShapeDtypeStruct((1, CB), jnp.int32),
            jax.ShapeDtypeStruct((2, CB, CB), jnp.float32),
        ],
        in_specs=[hbm] * 4,
        out_specs=[vmem] * 8,
        scratch_shapes=[
            pltpu.SMEM(w.shape, jnp.float32),
            pltpu.VMEM(a.shape, jnp.bfloat16),
            pltpu.VMEM((TIME, CB), jnp.bfloat16),
            pltpu.VMEM((TIME, CB), jnp.bfloat16),
        ]
        + spread_sems()
        + spread_sems()
        + [dma((7,)), dma((7,)), dma((7,)), dma((7,)), dma((64,)), dma, dma((6,))]
        + [pltpu.SemaphoreType.REGULAR],
        compiler_params=pltpu.CompilerParams(
            collective_id=0, has_side_effects=True, vmem_limit_bytes=24 << 20
        ),
        name="gather",
    )(*in_hbm(a, y, lab, w))


PANEL = 32


def eliminate(t, base):
    q, height, n = t.shape
    lane8 = lax.broadcasted_iota(jnp.int32, (q, 8, n), 2)
    sub8 = lax.broadcasted_iota(jnp.int32, (q, 8, n), 1)
    out = []
    for step in range(height // 8):
        o = base + 8 * step
        block = t[:, :8, :]
        cols = [jnp.broadcast_to(block[:, :, o + p : o + p + 1], (q, 8, n)) for p in range(8)]
        inside = (lane8 >= o) & (lane8 < o + 8)
        block = jnp.where(inside, jnp.where(lane8 == o + sub8, 1.0, 0.0), block)
        invs, rrows, crows = [], [], []
        scale = jnp.zeros((q, 8, n), jnp.float32)
        for p in range(8):
            crow = {k: jnp.broadcast_to(cols[k][:, p : p + 1, :], (q, 8, n)) for k in range(p, 8)}
            rrow = jnp.broadcast_to(block[:, p : p + 1, :], (q, 8, n))
            inv = 1.0 / crow[p]
            scale = jnp.where(sub8 == p, lax.rsqrt(crow[p]), scale)
            factor = jnp.where(sub8 > p, cols[p] * inv, 0.0)
            block = block - factor * rrow
            for k in range(p + 1, 8):
                cols[k] = cols[k] - factor * crow[k]
            invs.append(inv)
            rrows.append(rrow)
            crows.append(crow)
        out.append(block * scale)
        rest = t.shape[1] - 8
        if rest:
            low = t[:, 8:, :].reshape(q, rest // 8, 8, n)
            cols = [
                jnp.broadcast_to(low[:, :, :, o + p : o + p + 1], (q, rest // 8, 8, n)) for p in range(8)
            ]
            lane = lax.broadcasted_iota(jnp.int32, low.shape, 3)
            low = jnp.where((lane >= o) & (lane < o + 8), 0.0, low)
            for p in range(8):
                factor = cols[p] * invs[p][:, None]
                low = low - factor * rrows[p][:, None]
                for k in range(p + 1, 8):
                    cols[k] = cols[k] - factor * crows[p][k][:, None]
            t = low.reshape(q, rest, n)
    return jnp.concatenate(out, axis=1)


def parts(x):
    high = x.astype(jnp.bfloat16)
    rest = x - high.astype(jnp.float32)
    mid = rest.astype(jnp.bfloat16)
    low = (rest - mid.astype(jnp.float32)).astype(jnp.bfloat16)
    return high, mid, low


def inverse_factor(t, out_ref, between):
    q, n, _ = t.shape
    lane = lax.broadcasted_iota(jnp.int32, (PANEL, n), 1)
    sub = lax.broadcasted_iota(jnp.int32, (PANEL, n), 0)
    for panel in range(n // PANEL):
        base, end = panel * PANEL, (panel + 1) * PANEL
        scaled = eliminate(t[:, :PANEL, :], base)
        for r in range(q):
            out_ref[r, base:end, :] = jnp.where(lane <= sub + base, scaled[r], 0.0)
        if end < n:
            rest = []
            for r in range(q):
                row = jnp.where((lane >= end) | (lane <= sub + base), scaled[r], 0.0)
                h, m, l = parts(row)
                update = tdot(
                    jnp.concatenate([h, h, h, m, m, l], 0), jnp.concatenate([h, m, l, h, m, h], 0)
                )[end:, :]
                low = t[r, PANEL:, :]
                lanes = lax.broadcasted_iota(jnp.int32, low.shape, 1)
                rest.append(jnp.where((lanes >= base) & (lanes < end), 0.0, low) - update)
            t = jnp.stack(rest)
            between(panel)


def penalty(w_ref, r, lab):
    total = jnp.zeros(lab.shape, jnp.float32)
    for g in range(GROUPS):
        total = jnp.where(lab == g, w_ref[r, g], total)
    return total


def tdot(a, b):
    return lax.dot_general(a, b, (((0,), (0,)), ((), ())), preferred_element_type=jnp.float32)


def stack_left(x):
    h, m, l = parts(x)
    return jnp.concatenate([h, h, h, m, m, l], axis=1)


def stack_right(x, axis):
    h, m, l = parts(x)
    return jnp.concatenate([h, m, l, h, m, h], axis=axis)


def dot(a, b):
    return jnp.dot(a, b, preferred_element_type=jnp.float32)


def dot_nt(a, b):
    return lax.dot_general(a, b, (((1,), (1,)), ((), ())), preferred_element_type=jnp.float32)


def solve_kernel(
    weights_hbm, choice_hbm, labc_hbm, at_ref, st_ref, grs_ref, grc_ref, gsc_ref, y_ref, labs_ref, inv_ref,
    trail_ref, sides_ref, weights_ref, choice_ref, labc_ref, sem,
):
    small = [
        pltpu.make_async_copy(weights_hbm, weights_ref, sem.at[0]),
        pltpu.make_async_copy(choice_hbm, choice_ref, sem.at[1]),
        pltpu.make_async_copy(labc_hbm, labc_ref, sem.at[2]),
    ]
    for copy in small:
        copy.start()
    t, f, v = lax.axis_index("tm"), lax.axis_index("feat"), lax.axis_index("vox")
    row = t * 2 + f
    rows, voxels = sides_ref.shape
    y = y_ref[...]
    sside = dot(st_ref[...], y) * (1.0 / math.sqrt(TIME))
    sside6 = stack_right(sside, 0)
    for copy in small:
        copy.wait()

    eye = lax.broadcasted_iota(jnp.int32, (CB, CB), 0) == lax.broadcasted_iota(jnp.int32, (CB, CB), 1)
    r_sub = lax.broadcasted_iota(jnp.int32, (rows, CB), 0) + row * rows
    r_lane = lax.broadcasted_iota(jnp.int32, (rows, CB), 1)
    group = lax.broadcasted_iota(jnp.int32, (1, voxels), 1) // GROUP
    ridge = jnp.zeros((1, voxels), jnp.int32)
    for g in range(voxels // GROUP):
        ridge = jnp.where(group == g, choice_ref[g], ridge)

    panels, solved = [], []
    for r in range(2):
        inv = inv_ref[r]
        left = stack_left(inv)
        pen_s = jnp.broadcast_to(penalty(weights_ref, r, labs_ref[...]), (rows, CB))
        pen_c = jnp.broadcast_to(penalty(weights_ref, r, labc_ref[...]), (rows, CB))
        grs_r = grs_ref[...] + jnp.where(r_sub == r_lane, pen_s, 0.0)
        gsc_r = gsc_ref[...] + jnp.where(eye & (v == 0), pen_c[:CB], 0.0)
        panel = stack_left(dot_nt(stack_left(grs_r), stack_right(inv, 1)))
        partner = dot(left, stack_right(gsc_r, 0))
        system = grc_ref[...] + jnp.where(r_sub == r_lane + v * CB, pen_c, 0.0)
        trail_ref[r] = system - dot(panel, stack_right(partner, 0))
        panels.append(panel)
        solved.append(jnp.where(ridge == r, dot(left, sside6), 0.0))
    update = dot(
        jnp.concatenate(panels, 1), jnp.concatenate([stack_right(solved[0], 0), stack_right(solved[1], 0)], 0)
    )
    sides_ref[...] = dot(at_ref[...], y) * (1.0 / math.sqrt(TIME)) - update

    @pl.when(row == 0)
    def _():
        sides_ref[0:CB, :] = solved[0] + solved[1]


def solve(weights, choice, labc, at, st, grs, grc, gsc, y, labs, inv):
    vmem = pl.BlockSpec(memory_space=pltpu.VMEM)
    hbm = pl.BlockSpec(memory_space=pltpu.HBM)
    rows, voxels = at.shape[0], y.shape[1]
    return pl.pallas_call(
        solve_kernel,
        out_shape=[
            jax.ShapeDtypeStruct((2, rows, CB), jnp.float32),
            jax.ShapeDtypeStruct((rows, voxels), jnp.float32),
        ],
        in_specs=[hbm] * 3 + [vmem] * 8,
        out_specs=[vmem] * 2,
        scratch_shapes=[
            pltpu.SMEM(weights.shape, jnp.float32),
            pltpu.SMEM(choice.shape, jnp.int32),
            pltpu.VMEM((1, CB), jnp.int32),
            pltpu.SemaphoreType.DMA((3,)),
        ],
        compiler_params=pltpu.CompilerParams(vmem_limit_bytes=32 << 20),
        name="solve",
    )(*in_hbm(weights, choice, labc), at, st, grs, grc, gsc, y, labs, inv)


def local(design, signals, label, weights, choice):
    lab = label.reshape(1, CB)
    at, st, grs, grc, gsc, y, labs, inv = gather(design, signals, lab, weights)
    return solve(weights, choice, lab, at, st, grs, grc, gsc, y, labs, inv)


def solution(mesh):
    return jax.shard_map(
        local,
        mesh=mesh,
        in_specs=(P(None, ("tm", "feat")), P("tm", "vox"), P("vox"), P(), P("vox")),
        out_specs=(P(None, ("tm", "feat"), "vox"), P(("tm", "feat"), "vox")),
        check_vma=False,
    )
```

```python
import math

import jax
import jax.numpy as jnp
from jax import lax
from jax.experimental import pallas as pl
from jax.experimental.pallas import tpu as pltpu
from jax.sharding import PartitionSpec as P

TIME = 1024
GROUPS = 4
CB = 128
GROUP = 64
OFFSETS = [(dy, dx) for dy in range(2) for dx in range(4)][1:]
MESH = pl.DeviceIdType.MESH


def peer(t, dy, dx):
    y, x = t // 4, t % 4
    return ((y + dy) % 2) * 4 + (x + dx) % 4


def remote(src, dst, send, recv, **where):
    return pltpu.make_async_remote_copy(
        src_ref=src, dst_ref=dst, send_sem=send, recv_sem=recv, device_id=where, device_id_type=MESH
    )


class Spread:
    def __init__(self, buf, t, f, to, fo, sem, v=None, extra=None):
        self.buf, self.t, self.f, self.to, self.v, self.extra = buf, t, f, to, v, extra
        self.scatter, self.scatter_r, self.own, self.own_r, self.ag, self.ag_r, self.sib, self.sib_r = sem
        on = f == fo
        self.owner = (self.t == to) & on
        self.relay = (self.t != to) & on
        self.side = (self.t != to) & jnp.logical_not(on)
        self.owner_side = (self.t == to) & jnp.logical_not(on)

    def chunk(self, t):
        return self.buf.at[pl.ds(pl.multiple_of(t * 128, 128), 128), :]

    def c_scatter(self, k):
        p = peer(self.t, *OFFSETS[k])
        c = self.chunk(p)
        return remote(c, c, self.scatter.at[k], self.scatter_r, tm=p)

    def c_scatter_in(self):
        c = self.chunk(self.t)
        return remote(c, c, self.scatter.at[0], self.scatter_r, tm=self.to)

    def c_own(self, k):
        p = peer(self.t, *OFFSETS[k])
        c = self.chunk(self.t)
        return remote(c, c, self.own.at[k], self.own_r, tm=p)

    def c_own_in(self):
        c = self.chunk(self.to)
        return remote(c, c, self.own.at[0], self.own_r, tm=self.to)

    def c_ag(self, k):
        p = peer(self.t, *OFFSETS[k])
        c = self.chunk(self.t)
        return p, remote(c, c, self.ag.at[k], self.ag_r.at[k], tm=p)

    def c_ag_in(self, k):
        dy, dx = OFFSETS[k]
        p = peer(self.t, dy, 4 - dx)
        c = self.chunk(p)
        return p, remote(c, c, self.ag.at[k], self.ag_r.at[k], tm=p)

    def c_sib(self, k, p):
        c = self.chunk(p)
        return remote(c, c, self.sib.at[k], self.sib_r.at[k], feat=1 - self.f)

    def c_whole(self):
        return remote(self.buf, self.buf, self.sib.at[0], self.sib_r.at[0], feat=1 - self.f)

    def scatter_all(self, act):
        if self.v is None:
            for k in range(7):
                act(self.c_scatter(k))
        else:

            @pl.when(self.v != 0)
            def _():
                for k in range(7):
                    act(self.c_scatter(k))

    def pass_on(self, act):
        if self.v is not None:

            @pl.when(self.v == 1)
            def _():
                c = self.chunk(self.t)
                act(remote(c, c, self.extra, self.scatter_r, vox=0))

    def start(self):
        @pl.when(self.owner)
        def _():
            self.scatter_all(lambda c: c.start())
            for k in range(7):
                self.c_own(k).start()
            self.c_whole().start()

    def forward(self):
        @pl.when(self.relay)
        def _():
            self.c_scatter_in().wait_recv()
            self.pass_on(lambda c: c.start())
            for k in range(7):
                p, c = self.c_ag(k)

                @pl.when(p != self.to)
                def _():
                    c.start()

            self.c_sib(7, self.t).start()

    def collect(self):
        @pl.when(self.relay)
        def _():
            for k in range(7):
                p, c = self.c_ag_in(k)

                @pl.when(p != self.to)
                def _():
                    c.wait_recv()

                @pl.when(p == self.to)
                def _():
                    self.c_own_in().wait_recv()

                self.c_sib(k, p).start()

    def arrive(self):
        @pl.when(self.owner_side)
        def _():
            self.c_whole().wait_recv()

        @pl.when(self.side)
        def _():
            for k in range(7):
                dy, dx = OFFSETS[k]
                self.c_sib(k, peer(self.t, dy, 4 - dx)).wait_recv()
            self.c_sib(7, self.t).wait_recv()

    def finish(self):
        @pl.when(self.owner)
        def _():
            self.scatter_all(lambda c: c.wait_send())
            for k in range(7):
                self.c_own(k).wait_send()
            self.c_whole().wait_send()

        @pl.when(self.relay)
        def _():
            for k in range(7):
                p, c = self.c_ag(k)

                @pl.when(p != self.to)
                def _():
                    c.wait_send()

                q, _c = self.c_ag_in(k)
                self.c_sib(k, q).wait_send()
            self.c_sib(7, self.t).wait_send()
            self.pass_on(lambda c: c.wait_send())


def spread_sems():
    dma = pltpu.SemaphoreType.DMA
    return [dma((7,)), dma, dma((7,)), dma, dma((7,)), dma((7,)), dma((8,)), dma((8,))]


def gather_kernel(
    a_hbm, y_ref, lab_ref, w_hbm,
    at_ref, st_ref, grs_ref, grc_ref, gsc_ref, yall_ref, labs_ref, inv_ref,
    w_ref, a_ref, s_ref, c_ref, *sems,
):
    s_sem, c_sem, rest = sems[:8], sems[8:16], sems[16:]
    ysend, yrecv, bsend, brecv, lsend, lrecv, copy_sem, extra_sem, ready = rest
    t, f, v = lax.axis_index("tm"), lax.axis_index("feat"), lax.axis_index("vox")
    row = t * 2 + f
    to, fo = v // 4, (v // 2) % 2
    other = v != 0
    server = (v == 0) & (f == 1)
    owner_s, owner_c = row == 0, other & (t == to) & (f == fo)
    last_in = (v == 0) & (row == 0)
    barrier = pltpu.get_barrier_semaphore()

    def signal(**where):
        pl.semaphore_signal(barrier, inc=1, device_id=where, device_id_type=MESH)

    for offset in OFFSETS:
        signal(tm=peer(t, *offset))
    signal(feat=1 - f)

    helped = (v == 0) & (f == 0) & (t != 0)
    helper = (v == 1) & (f == 0) & (t != 0)

    @pl.when(helped)
    def _():
        signal(vox=1)

    first = jnp.where(t == 0, 16, 0)

    def client(i):
        return dict(tm=i // 2 % 8, feat=i % 2, vox=t * 4 + i // 16)

    @pl.when(server)
    def _():
        @pl.loop(first, 64)
        def _(i):
            signal(**client(i))

    get_s = pltpu.make_async_copy(a_hbm.at[:, pl.ds(0, CB)], s_ref, copy_sem.at[0])
    get_c = pltpu.make_async_copy(
        a_hbm.at[:, pl.ds(pl.multiple_of((v % 2) * CB, CB), CB)], c_ref, copy_sem.at[1]
    )
    get_y = pltpu.make_async_copy(
        y_ref, yall_ref.at[pl.ds(pl.multiple_of(t * 128, 128), 128), :], copy_sem.at[2]
    )
    get_lab = pltpu.make_async_copy(lab_ref, labs_ref, copy_sem.at[3])
    get_w = pltpu.make_async_copy(w_hbm, w_ref, copy_sem.at[4])
    get_a = pltpu.make_async_copy(a_hbm, a_ref, copy_sem.at[5])

    @pl.when(owner_s)
    def _():
        get_s.start()

    @pl.when(owner_c)
    def _():
        get_c.start()

    get_y.start()
    get_w.start()
    get_a.start()

    @pl.when(v == 0)
    def _():
        get_lab.start()
        get_lab.wait()

    @pl.when(owner_s)
    def _():
        get_s.wait()

    @pl.when(owner_c)
    def _():
        get_c.wait()

    get_y.wait()
    get_w.wait()

    def transpose():
        get_a.wait()
        at_ref[...] = a_ref[...].T

    @pl.when(jnp.logical_not(last_in))
    def _():
        transpose()

    @pl.when(v == 0)
    def _():
        pl.semaphore_wait(barrier, 8)

    @pl.when(helper)
    def _():
        pl.semaphore_wait(barrier, 10)

    @pl.when(other & jnp.logical_not(helper))
    def _():
        pl.semaphore_wait(barrier, 9)

    @pl.when(other)
    def _():
        pl.semaphore_signal(
            ready, inc=1, device_id={"tm": v // 4, "feat": 1, "vox": 0}, device_id_type=MESH
        )

    def c_lab(i):
        return remote(labs_ref, labs_ref, lsend.at[i], lrecv, **client(i))

    spread_s = Spread(s_ref, t, f, 0, 0, s_sem, v, extra_sem)
    spread_c = Spread(c_ref, t, f, to, fo, c_sem)

    def c_do(name):
        @pl.when(other)
        def _():
            getattr(spread_c, name)()

    spread_s.start()
    c_do("start")

    def yblock(q, g):
        return yall_ref.at[pl.ds(pl.multiple_of(q * 128 + g * 64, 64), 64), :]

    def source(k):
        dy, dx = OFFSETS[k]
        return peer(t, dy, 4 - dx)

    def c_y(k, b):
        return remote(b, b, ysend.at[k], yrecv.at[k], tm=peer(t, *OFFSETS[k]))

    def c_yout(k, b):
        return remote(b, b, bsend.at[k], brecv.at[k], feat=1 - f)

    def y_start(ks):
        for k in ks:
            c_y(k, yblock(t, f)).start()

    def y_collect(ks):
        for k in ks:
            b = yblock(source(k), f)
            c_y(k, b).wait_recv()
            c_yout(k, b).start()

    y_start((0, 2))

    @pl.when(last_in)
    def _():
        transpose()

    spread_s.forward()
    c_do("forward")
    y_start((3, 1, 4, 6, 5))

    spread_s.collect()
    spread_s.arrive()

    @pl.when(server & (t != 0))
    def _():
        pl.semaphore_wait(ready, 64)

    @pl.when(server & (t == 0))
    def _():
        pl.semaphore_wait(ready, 48)

    @pl.when(server)
    def _():
        @pl.loop(first, 64)
        def _(i):
            c_lab(i).start()

    @pl.when(other)
    def _():
        c_lab(0).wait_recv()

    s_all = s_ref[...]
    st_ref[...] = s_all.T
    gram = dot(st_ref[...], s_all) * (1.0 / TIME)
    eye = lax.broadcasted_iota(jnp.int32, (CB, CB), 0) == lax.broadcasted_iota(jnp.int32, (CB, CB), 1)
    matrices = []
    for r in range(2):
        pen = jnp.broadcast_to(penalty(w_ref, r, labs_ref[...]), (CB, CB))
        matrices.append(gram + jnp.where(eye, pen, 0.0))

    def between(panel):
        if panel == 0:
            c_do("collect")
        elif panel == 1:
            y_collect((0, 2, 3))
        elif panel == 2:
            y_collect((1, 4, 6, 5))

    inverse_factor(jnp.stack(matrices), inv_ref, between)
    grs_ref[...] = dot(at_ref[...], s_all) * (1.0 / TIME)
    c_do("arrive")

    @pl.when(v == 0)
    def _():
        c_ref[...] = s_ref[...]

    c_all = c_ref[...]
    grc_ref[...] = dot(at_ref[...], c_all) * (1.0 / TIME)
    gsc_ref[...] = dot(st_ref[...], c_all) * (1.0 / TIME)
    spread_s.finish()
    c_do("finish")

    for k in range(7):
        c_y(k, yblock(t, f)).wait_send()
        c_yout(k, yblock(source(k), f)).wait_send()
        c_yout(k, yblock(source(k), 1 - f)).wait_recv()

    @pl.when(server)
    def _():
        @pl.loop(first, 64)
        def _(i):
            c_lab(i).wait_send()


def in_hbm(*arrays):
    return [pltpu.with_memory_space_constraint(x, pltpu.HBM) for x in arrays]


def gather(a, y, lab, w):
    dma = pltpu.SemaphoreType.DMA
    vmem = pl.BlockSpec(memory_space=pltpu.VMEM)
    hbm = pl.BlockSpec(memory_space=pltpu.HBM)
    rows, voxels = a.shape[1], y.shape[1]
    return pl.pallas_call(
        gather_kernel,
        out_shape=[
            jax.ShapeDtypeStruct((rows, TIME), jnp.bfloat16),
            jax.ShapeDtypeStruct((CB, TIME), jnp.bfloat16),
            jax.ShapeDtypeStruct((rows, CB), jnp.float32),
            jax.ShapeDtypeStruct((rows, CB), jnp.float32),
            jax.ShapeDtypeStruct((CB, CB), jnp.float32),
            jax.ShapeDtypeStruct((TIME, voxels), jnp.bfloat16),
            jax.ShapeDtypeStruct((1, CB), jnp.int32),
            jax.ShapeDtypeStruct((2, CB, CB), jnp.float32),
        ],
        in_specs=[hbm] * 4,
        out_specs=[vmem] * 8,
        scratch_shapes=[
            pltpu.SMEM(w.shape, jnp.float32),
            pltpu.VMEM(a.shape, jnp.bfloat16),
            pltpu.VMEM((TIME, CB), jnp.bfloat16),
            pltpu.VMEM((TIME, CB), jnp.bfloat16),
        ]
        + spread_sems()
        + spread_sems()
        + [dma((7,)), dma((7,)), dma((7,)), dma((7,)), dma((64,)), dma, dma((6,))]
        + [dma, pltpu.SemaphoreType.REGULAR],
        compiler_params=pltpu.CompilerParams(
            collective_id=0, has_side_effects=True, vmem_limit_bytes=24 << 20
        ),
        name="gather",
    )(*in_hbm(a, y, lab, w))


PANEL = 32


def eliminate(t, base):
    q, height, n = t.shape
    lane8 = lax.broadcasted_iota(jnp.int32, (q, 8, n), 2)
    sub8 = lax.broadcasted_iota(jnp.int32, (q, 8, n), 1)
    out = []
    for step in range(height // 8):
        o = base + 8 * step
        block = t[:, :8, :]
        cols = [jnp.broadcast_to(block[:, :, o + p : o + p + 1], (q, 8, n)) for p in range(8)]
        inside = (lane8 >= o) & (lane8 < o + 8)
        block = jnp.where(inside, jnp.where(lane8 == o + sub8, 1.0, 0.0), block)
        invs, rrows, crows = [], [], []
        scale = jnp.zeros((q, 8, n), jnp.float32)
        for p in range(8):
            crow = {k: jnp.broadcast_to(cols[k][:, p : p + 1, :], (q, 8, n)) for k in range(p, 8)}
            rrow = jnp.broadcast_to(block[:, p : p + 1, :], (q, 8, n))
            inv = 1.0 / crow[p]
            scale = jnp.where(sub8 == p, lax.rsqrt(crow[p]), scale)
            factor = jnp.where(sub8 > p, cols[p] * inv, 0.0)
            block = block - factor * rrow
            for k in range(p + 1, 8):
                cols[k] = cols[k] - factor * crow[k]
            invs.append(inv)
            rrows.append(rrow)
            crows.append(crow)
        out.append(block * scale)
        rest = t.shape[1] - 8
        if rest:
            low = t[:, 8:, :].reshape(q, rest // 8, 8, n)
            cols = [
                jnp.broadcast_to(low[:, :, :, o + p : o + p + 1], (q, rest // 8, 8, n)) for p in range(8)
            ]
            lane = lax.broadcasted_iota(jnp.int32, low.shape, 3)
            low = jnp.where((lane >= o) & (lane < o + 8), 0.0, low)
            for p in range(8):
                factor = cols[p] * invs[p][:, None]
                low = low - factor * rrows[p][:, None]
                for k in range(p + 1, 8):
                    cols[k] = cols[k] - factor * crows[p][k][:, None]
            t = low.reshape(q, rest, n)
    return jnp.concatenate(out, axis=1)


def parts(x):
    high = x.astype(jnp.bfloat16)
    rest = x - high.astype(jnp.float32)
    mid = rest.astype(jnp.bfloat16)
    low = (rest - mid.astype(jnp.float32)).astype(jnp.bfloat16)
    return high, mid, low


def inverse_factor(t, out_ref, between):
    q, n, _ = t.shape
    lane = lax.broadcasted_iota(jnp.int32, (PANEL, n), 1)
    sub = lax.broadcasted_iota(jnp.int32, (PANEL, n), 0)
    for panel in range(n // PANEL):
        base, end = panel * PANEL, (panel + 1) * PANEL
        scaled = eliminate(t[:, :PANEL, :], base)
        for r in range(q):
            out_ref[r, base:end, :] = jnp.where(lane <= sub + base, scaled[r], 0.0)
        if end < n:
            rest = []
            for r in range(q):
                row = jnp.where((lane >= end) | (lane <= sub + base), scaled[r], 0.0)
                h, m, l = parts(row)
                update = tdot(
                    jnp.concatenate([h, h, h, m, m, l], 0), jnp.concatenate([h, m, l, h, m, h], 0)
                )[end:, :]
                low = t[r, PANEL:, :]
                lanes = lax.broadcasted_iota(jnp.int32, low.shape, 1)
                rest.append(jnp.where((lanes >= base) & (lanes < end), 0.0, low) - update)
            t = jnp.stack(rest)
            between(panel)


def penalty(w_ref, r, lab):
    total = jnp.zeros(lab.shape, jnp.float32)
    for g in range(GROUPS):
        total = jnp.where(lab == g, w_ref[r, g], total)
    return total


def tdot(a, b):
    return lax.dot_general(a, b, (((0,), (0,)), ((), ())), preferred_element_type=jnp.float32)


def stack_left(x):
    h, m, l = parts(x)
    return jnp.concatenate([h, h, h, m, m, l], axis=1)


def stack_right(x, axis):
    h, m, l = parts(x)
    return jnp.concatenate([h, m, l, h, m, h], axis=axis)


def dot(a, b):
    return jnp.dot(a, b, preferred_element_type=jnp.float32)


def dot_nt(a, b):
    return lax.dot_general(a, b, (((1,), (1,)), ((), ())), preferred_element_type=jnp.float32)


def solve_kernel(
    weights_hbm, choice_hbm, labc_hbm, at_ref, st_ref, grs_ref, grc_ref, gsc_ref, y_ref, labs_ref, inv_ref,
    trail_ref, sides_ref, weights_ref, choice_ref, labc_ref, sem,
):
    small = [
        pltpu.make_async_copy(weights_hbm, weights_ref, sem.at[0]),
        pltpu.make_async_copy(choice_hbm, choice_ref, sem.at[1]),
        pltpu.make_async_copy(labc_hbm, labc_ref, sem.at[2]),
    ]
    for copy in small:
        copy.start()
    t, f, v = lax.axis_index("tm"), lax.axis_index("feat"), lax.axis_index("vox")
    row = t * 2 + f
    rows, voxels = sides_ref.shape
    y = y_ref[...]
    sside = dot(st_ref[...], y) * (1.0 / math.sqrt(TIME))
    sside6 = stack_right(sside, 0)
    for copy in small:
        copy.wait()

    eye = lax.broadcasted_iota(jnp.int32, (CB, CB), 0) == lax.broadcasted_iota(jnp.int32, (CB, CB), 1)
    r_sub = lax.broadcasted_iota(jnp.int32, (rows, CB), 0) + row * rows
    r_lane = lax.broadcasted_iota(jnp.int32, (rows, CB), 1)
    group = lax.broadcasted_iota(jnp.int32, (1, voxels), 1) // GROUP
    ridge = jnp.zeros((1, voxels), jnp.int32)
    for g in range(voxels // GROUP):
        ridge = jnp.where(group == g, choice_ref[g], ridge)

    panels, solved = [], []
    for r in range(2):
        inv = inv_ref[r]
        left = stack_left(inv)
        pen_s = jnp.broadcast_to(penalty(weights_ref, r, labs_ref[...]), (rows, CB))
        pen_c = jnp.broadcast_to(penalty(weights_ref, r, labc_ref[...]), (rows, CB))
        grs_r = grs_ref[...] + jnp.where(r_sub == r_lane, pen_s, 0.0)
        gsc_r = gsc_ref[...] + jnp.where(eye & (v == 0), pen_c[:CB], 0.0)
        panel = stack_left(dot_nt(stack_left(grs_r), stack_right(inv, 1)))
        partner = dot(left, stack_right(gsc_r, 0))
        system = grc_ref[...] + jnp.where(r_sub == r_lane + v * CB, pen_c, 0.0)
        trail_ref[r] = system - dot(panel, stack_right(partner, 0))
        panels.append(panel)
        solved.append(jnp.where(ridge == r, dot(left, sside6), 0.0))
    update = dot(
        jnp.concatenate(panels, 1), jnp.concatenate([stack_right(solved[0], 0), stack_right(solved[1], 0)], 0)
    )
    sides_ref[...] = dot(at_ref[...], y) * (1.0 / math.sqrt(TIME)) - update

    @pl.when(row == 0)
    def _():
        sides_ref[0:CB, :] = solved[0] + solved[1]


def solve(weights, choice, labc, at, st, grs, grc, gsc, y, labs, inv):
    vmem = pl.BlockSpec(memory_space=pltpu.VMEM)
    hbm = pl.BlockSpec(memory_space=pltpu.HBM)
    rows, voxels = at.shape[0], y.shape[1]
    return pl.pallas_call(
        solve_kernel,
        out_shape=[
            jax.ShapeDtypeStruct((2, rows, CB), jnp.float32),
            jax.ShapeDtypeStruct((rows, voxels), jnp.float32),
        ],
        in_specs=[hbm] * 3 + [vmem] * 8,
        out_specs=[vmem] * 2,
        scratch_shapes=[
            pltpu.SMEM(weights.shape, jnp.float32),
            pltpu.SMEM(choice.shape, jnp.int32),
            pltpu.VMEM((1, CB), jnp.int32),
            pltpu.SemaphoreType.DMA((3,)),
        ],
        compiler_params=pltpu.CompilerParams(vmem_limit_bytes=32 << 20),
        name="solve",
    )(*in_hbm(weights, choice, labc), at, st, grs, grc, gsc, y, labs, inv)


def local(design, signals, label, weights, choice):
    lab = label.reshape(1, CB)
    at, st, grs, grc, gsc, y, labs, inv = gather(design, signals, lab, weights)
    return solve(weights, choice, lab, at, st, grs, grc, gsc, y, labs, inv)


def solution(mesh):
    return jax.shard_map(
        local,
        mesh=mesh,
        in_specs=(P(None, ("tm", "feat")), P("tm", "vox"), P("vox"), P(), P("vox")),
        out_specs=(P(None, ("tm", "feat"), "vox"), P(("tm", "feat"), "vox")),
        check_vma=False,
    )
```

```python
import math

import jax
import jax.numpy as jnp
from jax import lax
from jax.experimental import pallas as pl
from jax.experimental.pallas import tpu as pltpu
from jax.sharding import PartitionSpec as P

TIME = 1024
GROUPS = 4
CB = 128
GROUP = 64
OFFSETS = [(dy, dx) for dy in range(2) for dx in range(4)][1:]
MESH = pl.DeviceIdType.MESH


def peer(t, dy, dx):
    y, x = t // 4, t % 4
    return ((y + dy) % 2) * 4 + (x + dx) % 4


def remote(src, dst, send, recv, **where):
    return pltpu.make_async_remote_copy(
        src_ref=src, dst_ref=dst, send_sem=send, recv_sem=recv, device_id=where, device_id_type=MESH
    )


class Spread:
    def __init__(self, buf, t, f, to, fo, sem):
        self.buf, self.t, self.f, self.to = buf, t, f, to
        self.scatter, self.scatter_r, self.own, self.own_r, self.ag, self.ag_r, self.sib, self.sib_r = sem
        on = f == fo
        self.owner = (self.t == to) & on
        self.relay = (self.t != to) & on
        self.side = (self.t != to) & jnp.logical_not(on)
        self.owner_side = (self.t == to) & jnp.logical_not(on)

    def chunk(self, t):
        return self.buf.at[pl.ds(pl.multiple_of(t * 128, 128), 128), :]

    def c_scatter(self, k):
        p = peer(self.t, *OFFSETS[k])
        c = self.chunk(p)
        return remote(c, c, self.scatter.at[k], self.scatter_r, tm=p)

    def c_scatter_in(self):
        c = self.chunk(self.t)
        return remote(c, c, self.scatter.at[0], self.scatter_r, tm=self.to)

    def c_own(self, k):
        p = peer(self.t, *OFFSETS[k])
        c = self.chunk(self.t)
        return remote(c, c, self.own.at[k], self.own_r, tm=p)

    def c_own_in(self):
        c = self.chunk(self.to)
        return remote(c, c, self.own.at[0], self.own_r, tm=self.to)

    def c_ag(self, k):
        p = peer(self.t, *OFFSETS[k])
        c = self.chunk(self.t)
        return p, remote(c, c, self.ag.at[k], self.ag_r.at[k], tm=p)

    def c_ag_in(self, k):
        dy, dx = OFFSETS[k]
        p = peer(self.t, dy, 4 - dx)
        c = self.chunk(p)
        return p, remote(c, c, self.ag.at[k], self.ag_r.at[k], tm=p)

    def c_sib(self, k, p):
        c = self.chunk(p)
        return remote(c, c, self.sib.at[k], self.sib_r.at[k], feat=1 - self.f)

    def c_whole(self):
        return remote(self.buf, self.buf, self.sib.at[0], self.sib_r.at[0], feat=1 - self.f)

    def start(self):
        @pl.when(self.owner)
        def _():
            for k in range(7):
                self.c_scatter(k).start()
            for k in range(7):
                self.c_own(k).start()
            self.c_whole().start()

    def forward(self):
        @pl.when(self.relay)
        def _():
            self.c_scatter_in().wait_recv()
            for k in range(7):
                p, c = self.c_ag(k)

                @pl.when(p != self.to)
                def _():
                    c.start()

            self.c_sib(7, self.t).start()

    def collect(self):
        @pl.when(self.relay)
        def _():
            for k in range(7):
                p, c = self.c_ag_in(k)

                @pl.when(p != self.to)
                def _():
                    c.wait_recv()

                @pl.when(p == self.to)
                def _():
                    self.c_own_in().wait_recv()

                self.c_sib(k, p).start()

    def arrive(self):
        @pl.when(self.owner_side)
        def _():
            self.c_whole().wait_recv()

        @pl.when(self.side)
        def _():
            for k in range(7):
                dy, dx = OFFSETS[k]
                self.c_sib(k, peer(self.t, dy, 4 - dx)).wait_recv()
            self.c_sib(7, self.t).wait_recv()

    def finish(self):
        @pl.when(self.owner)
        def _():
            for k in range(7):
                self.c_scatter(k).wait_send()
                self.c_own(k).wait_send()
            self.c_whole().wait_send()

        @pl.when(self.relay)
        def _():
            for k in range(7):
                p, c = self.c_ag(k)

                @pl.when(p != self.to)
                def _():
                    c.wait_send()

                q, _c = self.c_ag_in(k)
                self.c_sib(k, q).wait_send()
            self.c_sib(7, self.t).wait_send()


def spread_sems():
    dma = pltpu.SemaphoreType.DMA
    return [dma((7,)), dma, dma((7,)), dma, dma((7,)), dma((7,)), dma((8,)), dma((8,))]


def gather_kernel(
    a_hbm, y_ref, lab_ref, w_hbm,
    at_ref, st_ref, grs_ref, grc_ref, gsc_ref, yall_ref, labs_ref, inv_ref,
    w_ref, a_ref, s_ref, c_ref, *sems,
):
    s_sem, c_sem, rest = sems[:8], sems[8:16], sems[16:]
    ysend, yrecv, bsend, brecv, lsend, lrecv, copy_sem, ready = rest
    t, f, v = lax.axis_index("tm"), lax.axis_index("feat"), lax.axis_index("vox")
    row = t * 2 + f
    to, fo = v // 4, (v // 2) % 2
    other = v != 0
    server = (v == 0) & (f == 1)
    owner_s, owner_c = row == 0, other & (t == to) & (f == fo)
    last_in = (v == 0) & (row == 0)
    barrier = pltpu.get_barrier_semaphore()

    def signal(**where):
        pl.semaphore_signal(barrier, inc=1, device_id=where, device_id_type=MESH)

    for offset in OFFSETS:
        signal(tm=peer(t, *offset))
    signal(feat=1 - f)

    first = jnp.where(t == 0, 16, 0)

    def client(i):
        return dict(tm=i // 2 % 8, feat=i % 2, vox=t * 4 + i // 16)

    @pl.when(server)
    def _():
        @pl.loop(first, 64)
        def _(i):
            signal(**client(i))

    get_s = pltpu.make_async_copy(a_hbm.at[:, pl.ds(0, CB)], s_ref, copy_sem.at[0])
    get_c = pltpu.make_async_copy(
        a_hbm.at[:, pl.ds(pl.multiple_of((v % 2) * CB, CB), CB)], c_ref, copy_sem.at[1]
    )
    get_y = pltpu.make_async_copy(
        y_ref, yall_ref.at[pl.ds(pl.multiple_of(t * 128, 128), 128), :], copy_sem.at[2]
    )
    get_lab = pltpu.make_async_copy(lab_ref, labs_ref, copy_sem.at[3])
    get_w = pltpu.make_async_copy(w_hbm, w_ref, copy_sem.at[4])
    get_a = pltpu.make_async_copy(a_hbm, a_ref, copy_sem.at[5])

    @pl.when(owner_s)
    def _():
        get_s.start()

    @pl.when(owner_c)
    def _():
        get_c.start()

    get_y.start()
    get_w.start()
    get_a.start()

    @pl.when(v == 0)
    def _():
        get_lab.start()
        get_lab.wait()

    @pl.when(owner_s)
    def _():
        get_s.wait()

    @pl.when(owner_c)
    def _():
        get_c.wait()

    get_y.wait()
    get_w.wait()

    def transpose():
        get_a.wait()
        at_ref[...] = a_ref[...].T

    @pl.when(jnp.logical_not(last_in))
    def _():
        transpose()

    @pl.when(v == 0)
    def _():
        pl.semaphore_wait(barrier, 8)

    @pl.when(other)
    def _():
        pl.semaphore_wait(barrier, 9)
        pl.semaphore_signal(
            ready, inc=1, device_id={"tm": v // 4, "feat": 1, "vox": 0}, device_id_type=MESH
        )

    def c_lab(i):
        return remote(labs_ref, labs_ref, lsend.at[i], lrecv, **client(i))

    spread_s = Spread(s_ref, t, f, 0, 0, s_sem)
    spread_c = Spread(c_ref, t, f, to, fo, c_sem)

    def c_do(name):
        @pl.when(other)
        def _():
            getattr(spread_c, name)()

    spread_s.start()
    c_do("start")

    def yblock(q, g):
        return yall_ref.at[pl.ds(pl.multiple_of(q * 128 + g * 64, 64), 64), :]

    def source(k):
        dy, dx = OFFSETS[k]
        return peer(t, dy, 4 - dx)

    def c_y(k, b):
        return remote(b, b, ysend.at[k], yrecv.at[k], tm=peer(t, *OFFSETS[k]))

    def c_yout(k, b):
        return remote(b, b, bsend.at[k], brecv.at[k], feat=1 - f)

    def y_start(ks):
        for k in ks:
            c_y(k, yblock(t, f)).start()

    def y_collect(ks):
        for k in ks:
            b = yblock(source(k), f)
            c_y(k, b).wait_recv()
            c_yout(k, b).start()

    @pl.when(last_in)
    def _():
        transpose()

    spread_s.forward()
    c_do("forward")
    y_start((0, 2, 3, 1, 4, 6, 5))

    @pl.when(server & (t != 0))
    def _():
        pl.semaphore_wait(ready, 64)

    @pl.when(server & (t == 0))
    def _():
        pl.semaphore_wait(ready, 48)

    @pl.when(server)
    def _():
        @pl.loop(first, 64)
        def _(i):
            c_lab(i).start()


    spread_s.collect()
    spread_s.arrive()

    @pl.when(other)
    def _():
        c_lab(0).wait_recv()

    s_all = s_ref[...]
    st_ref[...] = s_all.T
    gram = dot(st_ref[...], s_all) * (1.0 / TIME)
    eye = lax.broadcasted_iota(jnp.int32, (CB, CB), 0) == lax.broadcasted_iota(jnp.int32, (CB, CB), 1)
    matrices = []
    for r in range(2):
        pen = jnp.broadcast_to(penalty(w_ref, r, labs_ref[...]), (CB, CB))
        matrices.append(gram + jnp.where(eye, pen, 0.0))

    def between(panel):
        if panel == 0:
            c_do("collect")
        elif panel == 1:
            y_collect((0, 2, 3))
        elif panel == 2:
            y_collect((1, 4, 6, 5))

    inverse_factor(jnp.stack(matrices), inv_ref, between)
    grs_ref[...] = dot(at_ref[...], s_all) * (1.0 / TIME)
    c_do("arrive")

    @pl.when(v == 0)
    def _():
        c_ref[...] = s_ref[...]

    c_all = c_ref[...]
    grc_ref[...] = dot(at_ref[...], c_all) * (1.0 / TIME)
    gsc_ref[...] = dot(st_ref[...], c_all) * (1.0 / TIME)
    spread_s.finish()
    c_do("finish")

    for k in range(7):
        c_y(k, yblock(t, f)).wait_send()
        c_yout(k, yblock(source(k), f)).wait_send()
        c_yout(k, yblock(source(k), 1 - f)).wait_recv()

    @pl.when(server)
    def _():
        @pl.loop(first, 64)
        def _(i):
            c_lab(i).wait_send()


def in_hbm(*arrays):
    return [pltpu.with_memory_space_constraint(x, pltpu.HBM) for x in arrays]


def gather(a, y, lab, w):
    dma = pltpu.SemaphoreType.DMA
    vmem = pl.BlockSpec(memory_space=pltpu.VMEM)
    hbm = pl.BlockSpec(memory_space=pltpu.HBM)
    rows, voxels = a.shape[1], y.shape[1]
    return pl.pallas_call(
        gather_kernel,
        out_shape=[
            jax.ShapeDtypeStruct((rows, TIME), jnp.bfloat16),
            jax.ShapeDtypeStruct((CB, TIME), jnp.bfloat16),
            jax.ShapeDtypeStruct((rows, CB), jnp.float32),
            jax.ShapeDtypeStruct((rows, CB), jnp.float32),
            jax.ShapeDtypeStruct((CB, CB), jnp.float32),
            jax.ShapeDtypeStruct((TIME, voxels), jnp.bfloat16),
            jax.ShapeDtypeStruct((1, CB), jnp.int32),
            jax.ShapeDtypeStruct((2, CB, CB), jnp.float32),
        ],
        in_specs=[hbm] * 4,
        out_specs=[vmem] * 8,
        scratch_shapes=[
            pltpu.SMEM(w.shape, jnp.float32),
            pltpu.VMEM(a.shape, jnp.bfloat16),
            pltpu.VMEM((TIME, CB), jnp.bfloat16),
            pltpu.VMEM((TIME, CB), jnp.bfloat16),
        ]
        + spread_sems()
        + spread_sems()
        + [dma((7,)), dma((7,)), dma((7,)), dma((7,)), dma((64,)), dma, dma((6,))]
        + [pltpu.SemaphoreType.REGULAR],
        compiler_params=pltpu.CompilerParams(
            collective_id=0, has_side_effects=True, vmem_limit_bytes=24 << 20
        ),
        name="gather",
    )(*in_hbm(a, y, lab, w))


PANEL = 32


def eliminate(t, base):
    q, height, n = t.shape
    lane8 = lax.broadcasted_iota(jnp.int32, (q, 8, n), 2)
    sub8 = lax.broadcasted_iota(jnp.int32, (q, 8, n), 1)
    out = []
    for step in range(height // 8):
        o = base + 8 * step
        block = t[:, :8, :]
        cols = [jnp.broadcast_to(block[:, :, o + p : o + p + 1], (q, 8, n)) for p in range(8)]
        inside = (lane8 >= o) & (lane8 < o + 8)
        block = jnp.where(inside, jnp.where(lane8 == o + sub8, 1.0, 0.0), block)
        invs, rrows, crows = [], [], []
        scale = jnp.zeros((q, 8, n), jnp.float32)
        for p in range(8):
            crow = {k: jnp.broadcast_to(cols[k][:, p : p + 1, :], (q, 8, n)) for k in range(p, 8)}
            rrow = jnp.broadcast_to(block[:, p : p + 1, :], (q, 8, n))
            inv = 1.0 / crow[p]
            scale = jnp.where(sub8 == p, lax.rsqrt(crow[p]), scale)
            factor = jnp.where(sub8 > p, cols[p] * inv, 0.0)
            block = block - factor * rrow
            for k in range(p + 1, 8):
                cols[k] = cols[k] - factor * crow[k]
            invs.append(inv)
            rrows.append(rrow)
            crows.append(crow)
        out.append(block * scale)
        rest = t.shape[1] - 8
        if rest:
            low = t[:, 8:, :].reshape(q, rest // 8, 8, n)
            cols = [
                jnp.broadcast_to(low[:, :, :, o + p : o + p + 1], (q, rest // 8, 8, n)) for p in range(8)
            ]
            lane = lax.broadcasted_iota(jnp.int32, low.shape, 3)
            low = jnp.where((lane >= o) & (lane < o + 8), 0.0, low)
            for p in range(8):
                factor = cols[p] * invs[p][:, None]
                low = low - factor * rrows[p][:, None]
                for k in range(p + 1, 8):
                    cols[k] = cols[k] - factor * crows[p][k][:, None]
            t = low.reshape(q, rest, n)
    return jnp.concatenate(out, axis=1)


def parts(x):
    high = x.astype(jnp.bfloat16)
    rest = x - high.astype(jnp.float32)
    mid = rest.astype(jnp.bfloat16)
    low = (rest - mid.astype(jnp.float32)).astype(jnp.bfloat16)
    return high, mid, low


def inverse_factor(t, out_ref, between):
    q, n, _ = t.shape
    lane = lax.broadcasted_iota(jnp.int32, (PANEL, n), 1)
    sub = lax.broadcasted_iota(jnp.int32, (PANEL, n), 0)
    for panel in range(n // PANEL):
        base, end = panel * PANEL, (panel + 1) * PANEL
        scaled = eliminate(t[:, :PANEL, :], base)
        for r in range(q):
            out_ref[r, base:end, :] = jnp.where(lane <= sub + base, scaled[r], 0.0)
        if end < n:
            rest = []
            for r in range(q):
                row = jnp.where((lane >= end) | (lane <= sub + base), scaled[r], 0.0)
                h, m, l = parts(row)
                update = tdot(
                    jnp.concatenate([h, h, h, m, m, l], 0), jnp.concatenate([h, m, l, h, m, h], 0)
                )[end:, :]
                low = t[r, PANEL:, :]
                lanes = lax.broadcasted_iota(jnp.int32, low.shape, 1)
                rest.append(jnp.where((lanes >= base) & (lanes < end), 0.0, low) - update)
            t = jnp.stack(rest)
            between(panel)


def penalty(w_ref, r, lab):
    total = jnp.zeros(lab.shape, jnp.float32)
    for g in range(GROUPS):
        total = jnp.where(lab == g, w_ref[r, g], total)
    return total


def tdot(a, b):
    return lax.dot_general(a, b, (((0,), (0,)), ((), ())), preferred_element_type=jnp.float32)


def stack_left(x):
    h, m, l = parts(x)
    return jnp.concatenate([h, h, h, m, m, l], axis=1)


def stack_right(x, axis):
    h, m, l = parts(x)
    return jnp.concatenate([h, m, l, h, m, h], axis=axis)


def dot(a, b):
    return jnp.dot(a, b, preferred_element_type=jnp.float32)


def dot_nt(a, b):
    return lax.dot_general(a, b, (((1,), (1,)), ((), ())), preferred_element_type=jnp.float32)


def solve_kernel(
    weights_hbm, choice_hbm, labc_hbm, at_ref, st_ref, grs_ref, grc_ref, gsc_ref, y_ref, labs_ref, inv_ref,
    trail_ref, sides_ref, weights_ref, choice_ref, labc_ref, sem,
):
    small = [
        pltpu.make_async_copy(weights_hbm, weights_ref, sem.at[0]),
        pltpu.make_async_copy(choice_hbm, choice_ref, sem.at[1]),
        pltpu.make_async_copy(labc_hbm, labc_ref, sem.at[2]),
    ]
    for copy in small:
        copy.start()
    t, f, v = lax.axis_index("tm"), lax.axis_index("feat"), lax.axis_index("vox")
    row = t * 2 + f
    rows, voxels = sides_ref.shape
    y = y_ref[...]
    sside = dot(st_ref[...], y) * (1.0 / math.sqrt(TIME))
    sside6 = stack_right(sside, 0)
    for copy in small:
        copy.wait()

    eye = lax.broadcasted_iota(jnp.int32, (CB, CB), 0) == lax.broadcasted_iota(jnp.int32, (CB, CB), 1)
    r_sub = lax.broadcasted_iota(jnp.int32, (rows, CB), 0) + row * rows
    r_lane = lax.broadcasted_iota(jnp.int32, (rows, CB), 1)
    group = lax.broadcasted_iota(jnp.int32, (1, voxels), 1) // GROUP
    ridge = jnp.zeros((1, voxels), jnp.int32)
    for g in range(voxels // GROUP):
        ridge = jnp.where(group == g, choice_ref[g], ridge)

    panels, solved = [], []
    for r in range(2):
        inv = inv_ref[r]
        left = stack_left(inv)
        pen_s = jnp.broadcast_to(penalty(weights_ref, r, labs_ref[...]), (rows, CB))
        pen_c = jnp.broadcast_to(penalty(weights_ref, r, labc_ref[...]), (rows, CB))
        grs_r = grs_ref[...] + jnp.where(r_sub == r_lane, pen_s, 0.0)
        gsc_r = gsc_ref[...] + jnp.where(eye & (v == 0), pen_c[:CB], 0.0)
        panel = stack_left(dot_nt(stack_left(grs_r), stack_right(inv, 1)))
        partner = dot(left, stack_right(gsc_r, 0))
        system = grc_ref[...] + jnp.where(r_sub == r_lane + v * CB, pen_c, 0.0)
        trail_ref[r] = system - dot(panel, stack_right(partner, 0))
        panels.append(panel)
        solved.append(jnp.where(ridge == r, dot(left, sside6), 0.0))
    update = dot(
        jnp.concatenate(panels, 1), jnp.concatenate([stack_right(solved[0], 0), stack_right(solved[1], 0)], 0)
    )
    sides_ref[...] = dot(at_ref[...], y) * (1.0 / math.sqrt(TIME)) - update

    @pl.when(row == 0)
    def _():
        sides_ref[0:CB, :] = solved[0] + solved[1]


def solve(weights, choice, labc, at, st, grs, grc, gsc, y, labs, inv):
    vmem = pl.BlockSpec(memory_space=pltpu.VMEM)
    hbm = pl.BlockSpec(memory_space=pltpu.HBM)
    rows, voxels = at.shape[0], y.shape[1]
    return pl.pallas_call(
        solve_kernel,
        out_shape=[
            jax.ShapeDtypeStruct((2, rows, CB), jnp.float32),
            jax.ShapeDtypeStruct((rows, voxels), jnp.float32),
        ],
        in_specs=[hbm] * 3 + [vmem] * 8,
        out_specs=[vmem] * 2,
        scratch_shapes=[
            pltpu.SMEM(weights.shape, jnp.float32),
            pltpu.SMEM(choice.shape, jnp.int32),
            pltpu.VMEM((1, CB), jnp.int32),
            pltpu.SemaphoreType.DMA((3,)),
        ],
        compiler_params=pltpu.CompilerParams(vmem_limit_bytes=32 << 20),
        name="solve",
    )(*in_hbm(weights, choice, labc), at, st, grs, grc, gsc, y, labs, inv)


def local(design, signals, label, weights, choice):
    lab = label.reshape(1, CB)
    at, st, grs, grc, gsc, y, labs, inv = gather(design, signals, lab, weights)
    return solve(weights, choice, lab, at, st, grs, grc, gsc, y, labs, inv)


def solution(mesh):
    return jax.shard_map(
        local,
        mesh=mesh,
        in_specs=(P(None, ("tm", "feat")), P("tm", "vox"), P("vox"), P(), P("vox")),
        out_specs=(P(None, ("tm", "feat"), "vox"), P(("tm", "feat"), "vox")),
        check_vma=False,
    )
```

```python
import math

import jax
import jax.numpy as jnp
from jax import lax
from jax.experimental import pallas as pl
from jax.experimental.pallas import tpu as pltpu
from jax.sharding import PartitionSpec as P

TIME = 1024
GROUPS = 4
CB = 128
GROUP = 64
OFFSETS = [(dy, dx) for dy in range(2) for dx in range(4)][1:]
MESH = pl.DeviceIdType.MESH


def peer(t, dy, dx):
    y, x = t // 4, t % 4
    return ((y + dy) % 2) * 4 + (x + dx) % 4


def remote(src, dst, send, recv, **where):
    return pltpu.make_async_remote_copy(
        src_ref=src, dst_ref=dst, send_sem=send, recv_sem=recv, device_id=where, device_id_type=MESH
    )


class Spread:
    def __init__(self, buf, t, f, to, fo, sem):
        self.buf, self.t, self.f, self.to = buf, t, f, to
        self.scatter, self.scatter_r, self.own, self.own_r, self.ag, self.ag_r, self.sib, self.sib_r = sem
        on = f == fo
        self.owner = (self.t == to) & on
        self.relay = (self.t != to) & on
        self.side = (self.t != to) & jnp.logical_not(on)
        self.owner_side = (self.t == to) & jnp.logical_not(on)

    def chunk(self, t):
        return self.buf.at[pl.ds(pl.multiple_of(t * 128, 128), 128), :]

    def c_scatter(self, k):
        p = peer(self.t, *OFFSETS[k])
        c = self.chunk(p)
        return remote(c, c, self.scatter.at[k], self.scatter_r, tm=p)

    def c_scatter_in(self):
        c = self.chunk(self.t)
        return remote(c, c, self.scatter.at[0], self.scatter_r, tm=self.to)

    def c_own(self, k):
        p = peer(self.t, *OFFSETS[k])
        c = self.chunk(self.t)
        return remote(c, c, self.own.at[k], self.own_r, tm=p)

    def c_own_in(self):
        c = self.chunk(self.to)
        return remote(c, c, self.own.at[0], self.own_r, tm=self.to)

    def c_ag(self, k):
        p = peer(self.t, *OFFSETS[k])
        c = self.chunk(self.t)
        return p, remote(c, c, self.ag.at[k], self.ag_r.at[k], tm=p)

    def c_ag_in(self, k):
        dy, dx = OFFSETS[k]
        p = peer(self.t, dy, 4 - dx)
        c = self.chunk(p)
        return p, remote(c, c, self.ag.at[k], self.ag_r.at[k], tm=p)

    def c_sib(self, k, p):
        c = self.chunk(p)
        return remote(c, c, self.sib.at[k], self.sib_r.at[k], feat=1 - self.f)

    def c_whole(self):
        return remote(self.buf, self.buf, self.sib.at[0], self.sib_r.at[0], feat=1 - self.f)

    def start(self):
        @pl.when(self.owner)
        def _():
            for k in range(7):
                self.c_scatter(k).start()
            for k in range(7):
                self.c_own(k).start()
            self.c_whole().start()

    def forward(self):
        @pl.when(self.relay)
        def _():
            self.c_scatter_in().wait_recv()
            for k in range(7):
                p, c = self.c_ag(k)

                @pl.when(p != self.to)
                def _():
                    c.start()

            self.c_sib(7, self.t).start()

    def collect(self):
        @pl.when(self.relay)
        def _():
            for k in range(7):
                p, c = self.c_ag_in(k)

                @pl.when(p != self.to)
                def _():
                    c.wait_recv()

                @pl.when(p == self.to)
                def _():
                    self.c_own_in().wait_recv()

                self.c_sib(k, p).start()

    def arrive(self):
        @pl.when(self.owner_side)
        def _():
            self.c_whole().wait_recv()

        @pl.when(self.side)
        def _():
            for k in range(7):
                dy, dx = OFFSETS[k]
                self.c_sib(k, peer(self.t, dy, 4 - dx)).wait_recv()
            self.c_sib(7, self.t).wait_recv()

    def finish(self):
        @pl.when(self.owner)
        def _():
            for k in range(7):
                self.c_scatter(k).wait_send()
                self.c_own(k).wait_send()
            self.c_whole().wait_send()

        @pl.when(self.relay)
        def _():
            for k in range(7):
                p, c = self.c_ag(k)

                @pl.when(p != self.to)
                def _():
                    c.wait_send()

                q, _c = self.c_ag_in(k)
                self.c_sib(k, q).wait_send()
            self.c_sib(7, self.t).wait_send()


def spread_sems():
    dma = pltpu.SemaphoreType.DMA
    return [dma((7,)), dma, dma((7,)), dma, dma((7,)), dma((7,)), dma((8,)), dma((8,))]


def gather_kernel(
    a_hbm, y_ref, lab_ref, w_hbm,
    at_ref, st_ref, grs_ref, grc_ref, gsc_ref, yall_ref, labs_ref, inv_ref,
    w_ref, a_ref, s_ref, c_ref, *sems,
):
    s_sem, c_sem, rest = sems[:8], sems[8:16], sems[16:]
    ysend, yrecv, bsend, brecv, lsend, lrecv, copy_sem, ready = rest
    t, f, v = lax.axis_index("tm"), lax.axis_index("feat"), lax.axis_index("vox")
    row = t * 2 + f
    to, fo = v // 4, (v // 2) % 2
    other = v != 0
    server = (v == 0) & (f == 1)
    owner_s, owner_c = row == 0, other & (t == to) & (f == fo)
    last_in = (v == 0) & (row == 0)
    barrier = pltpu.get_barrier_semaphore()

    def signal(**where):
        pl.semaphore_signal(barrier, inc=1, device_id=where, device_id_type=MESH)

    for offset in OFFSETS:
        signal(tm=peer(t, *offset))
    signal(feat=1 - f)

    first = jnp.where(t == 0, 16, 0)

    def client(i):
        return dict(tm=i // 2 % 8, feat=i % 2, vox=t * 4 + i // 16)

    @pl.when(server)
    def _():
        @pl.loop(first, 64)
        def _(i):
            signal(**client(i))

    get_s = pltpu.make_async_copy(a_hbm.at[:, pl.ds(0, CB)], s_ref, copy_sem.at[0])
    get_c = pltpu.make_async_copy(
        a_hbm.at[:, pl.ds(pl.multiple_of((v % 2) * CB, CB), CB)], c_ref, copy_sem.at[1]
    )
    get_y = pltpu.make_async_copy(
        y_ref, yall_ref.at[pl.ds(pl.multiple_of(t * 128, 128), 128), :], copy_sem.at[2]
    )
    get_lab = pltpu.make_async_copy(lab_ref, labs_ref, copy_sem.at[3])
    get_w = pltpu.make_async_copy(w_hbm, w_ref, copy_sem.at[4])
    get_a = pltpu.make_async_copy(a_hbm, a_ref, copy_sem.at[5])

    @pl.when(owner_s)
    def _():
        get_s.start()

    @pl.when(owner_c)
    def _():
        get_c.start()

    get_y.start()
    get_w.start()
    get_a.start()

    @pl.when(v == 0)
    def _():
        get_lab.start()
        get_lab.wait()

    @pl.when(owner_s)
    def _():
        get_s.wait()

    @pl.when(owner_c)
    def _():
        get_c.wait()

    get_y.wait()
    get_w.wait()

    def transpose():
        get_a.wait()
        at_ref[...] = a_ref[...].T

    @pl.when(jnp.logical_not(last_in))
    def _():
        transpose()

    @pl.when(v == 0)
    def _():
        pl.semaphore_wait(barrier, 8)

    @pl.when(other)
    def _():
        pl.semaphore_wait(barrier, 9)
        pl.semaphore_signal(
            ready, inc=1, device_id={"tm": v // 4, "feat": 1, "vox": 0}, device_id_type=MESH
        )

    def c_lab(i):
        return remote(labs_ref, labs_ref, lsend.at[i], lrecv, **client(i))

    spread_s = Spread(s_ref, t, f, 0, 0, s_sem)
    spread_c = Spread(c_ref, t, f, to, fo, c_sem)

    def c_do(name):
        @pl.when(other)
        def _():
            getattr(spread_c, name)()

    spread_s.start()
    c_do("start")

    def yblock(q, g):
        return yall_ref.at[pl.ds(pl.multiple_of(q * 128 + g * 64, 64), 64), :]

    def source(k):
        dy, dx = OFFSETS[k]
        return peer(t, dy, 4 - dx)

    def c_y(k, b):
        return remote(b, b, ysend.at[k], yrecv.at[k], tm=peer(t, *OFFSETS[k]))

    def c_yout(k, b):
        return remote(b, b, bsend.at[k], brecv.at[k], feat=1 - f)

    def y_start(ks):
        for k in ks:
            c_y(k, yblock(t, f)).start()

    def y_collect(ks):
        for k in ks:
            b = yblock(source(k), f)
            c_y(k, b).wait_recv()
            c_yout(k, b).start()

    @pl.when(last_in)
    def _():
        transpose()

    spread_s.forward()
    c_do("forward")
    y_start((0, 2, 3, 1, 4, 6, 5))

    @pl.when(server & (t != 0))
    def _():
        pl.semaphore_wait(ready, 64)

    @pl.when(server & (t == 0))
    def _():
        pl.semaphore_wait(ready, 48)

    @pl.when(server)
    def _():
        @pl.loop(first, 64)
        def _(i):
            c_lab(i).start()


    spread_s.collect()
    spread_s.arrive()

    @pl.when(other)
    def _():
        c_lab(0).wait_recv()

    s_all = s_ref[...]
    st_ref[...] = s_all.T
    gram = dot(st_ref[...], s_all) * (1.0 / TIME)
    eye = lax.broadcasted_iota(jnp.int32, (CB, CB), 0) == lax.broadcasted_iota(jnp.int32, (CB, CB), 1)
    matrices = []
    for r in range(2):
        pen = jnp.broadcast_to(penalty(w_ref, r, labs_ref[...]), (CB, CB))
        matrices.append(gram + jnp.where(eye, pen, 0.0))

    def between(panel):
        if panel == 0:
            c_do("collect")
        elif panel == 1:
            y_collect((0, 2, 3))
        elif panel == 2:
            y_collect((1, 4, 6, 5))

    inverse_factor(jnp.stack(matrices), inv_ref, between)
    grs = dot(at_ref[...], s_all) * (1.0 / TIME)
    grs_ref[...] = grs
    c_do("arrive")

    @pl.when(v == 0)
    def _():
        grc_ref[...] = grs
        gsc_ref[...] = gram

    @pl.when(other)
    def _():
        c_all = c_ref[...]
        grc_ref[...] = dot(at_ref[...], c_all) * (1.0 / TIME)
        gsc_ref[...] = dot(st_ref[...], c_all) * (1.0 / TIME)

    spread_s.finish()
    c_do("finish")

    for k in range(7):
        c_y(k, yblock(t, f)).wait_send()
        c_yout(k, yblock(source(k), f)).wait_send()
        c_yout(k, yblock(source(k), 1 - f)).wait_recv()

    @pl.when(server)
    def _():
        @pl.loop(first, 64)
        def _(i):
            c_lab(i).wait_send()


def in_hbm(*arrays):
    return [pltpu.with_memory_space_constraint(x, pltpu.HBM) for x in arrays]


def gather(a, y, lab, w):
    dma = pltpu.SemaphoreType.DMA
    vmem = pl.BlockSpec(memory_space=pltpu.VMEM)
    hbm = pl.BlockSpec(memory_space=pltpu.HBM)
    rows, voxels = a.shape[1], y.shape[1]
    return pl.pallas_call(
        gather_kernel,
        out_shape=[
            jax.ShapeDtypeStruct((rows, TIME), jnp.bfloat16),
            jax.ShapeDtypeStruct((CB, TIME), jnp.bfloat16),
            jax.ShapeDtypeStruct((rows, CB), jnp.float32),
            jax.ShapeDtypeStruct((rows, CB), jnp.float32),
            jax.ShapeDtypeStruct((CB, CB), jnp.float32),
            jax.ShapeDtypeStruct((TIME, voxels), jnp.bfloat16),
            jax.ShapeDtypeStruct((1, CB), jnp.int32),
            jax.ShapeDtypeStruct((2, CB, CB), jnp.float32),
        ],
        in_specs=[hbm] * 4,
        out_specs=[vmem] * 8,
        scratch_shapes=[
            pltpu.SMEM(w.shape, jnp.float32),
            pltpu.VMEM(a.shape, jnp.bfloat16),
            pltpu.VMEM((TIME, CB), jnp.bfloat16),
            pltpu.VMEM((TIME, CB), jnp.bfloat16),
        ]
        + spread_sems()
        + spread_sems()
        + [dma((7,)), dma((7,)), dma((7,)), dma((7,)), dma((64,)), dma, dma((6,))]
        + [pltpu.SemaphoreType.REGULAR],
        compiler_params=pltpu.CompilerParams(
            collective_id=0, has_side_effects=True, vmem_limit_bytes=24 << 20
        ),
        name="gather",
    )(*in_hbm(a, y, lab, w))


PANEL = 32


def eliminate(t, base):
    q, height, n = t.shape
    lane8 = lax.broadcasted_iota(jnp.int32, (q, 8, n), 2)
    sub8 = lax.broadcasted_iota(jnp.int32, (q, 8, n), 1)
    out = []
    for step in range(height // 8):
        o = base + 8 * step
        block = t[:, :8, :]
        cols = [jnp.broadcast_to(block[:, :, o + p : o + p + 1], (q, 8, n)) for p in range(8)]
        inside = (lane8 >= o) & (lane8 < o + 8)
        block = jnp.where(inside, jnp.where(lane8 == o + sub8, 1.0, 0.0), block)
        invs, rrows, crows = [], [], []
        scale = jnp.zeros((q, 8, n), jnp.float32)
        for p in range(8):
            crow = {k: jnp.broadcast_to(cols[k][:, p : p + 1, :], (q, 8, n)) for k in range(p, 8)}
            rrow = jnp.broadcast_to(block[:, p : p + 1, :], (q, 8, n))
            inv = 1.0 / crow[p]
            scale = jnp.where(sub8 == p, lax.rsqrt(crow[p]), scale)
            factor = jnp.where(sub8 > p, cols[p] * inv, 0.0)
            block = block - factor * rrow
            for k in range(p + 1, 8):
                cols[k] = cols[k] - factor * crow[k]
            invs.append(inv)
            rrows.append(rrow)
            crows.append(crow)
        out.append(block * scale)
        rest = t.shape[1] - 8
        if rest:
            low = t[:, 8:, :].reshape(q, rest // 8, 8, n)
            cols = [
                jnp.broadcast_to(low[:, :, :, o + p : o + p + 1], (q, rest // 8, 8, n)) for p in range(8)
            ]
            lane = lax.broadcasted_iota(jnp.int32, low.shape, 3)
            low = jnp.where((lane >= o) & (lane < o + 8), 0.0, low)
            for p in range(8):
                factor = cols[p] * invs[p][:, None]
                low = low - factor * rrows[p][:, None]
                for k in range(p + 1, 8):
                    cols[k] = cols[k] - factor * crows[p][k][:, None]
            t = low.reshape(q, rest, n)
    return jnp.concatenate(out, axis=1)


def parts(x):
    high = x.astype(jnp.bfloat16)
    rest = x - high.astype(jnp.float32)
    mid = rest.astype(jnp.bfloat16)
    low = (rest - mid.astype(jnp.float32)).astype(jnp.bfloat16)
    return high, mid, low


def inverse_factor(t, out_ref, between):
    q, n, _ = t.shape
    lane = lax.broadcasted_iota(jnp.int32, (PANEL, n), 1)
    sub = lax.broadcasted_iota(jnp.int32, (PANEL, n), 0)
    for panel in range(n // PANEL):
        base, end = panel * PANEL, (panel + 1) * PANEL
        scaled = eliminate(t[:, :PANEL, :], base)
        for r in range(q):
            out_ref[r, base:end, :] = jnp.where(lane <= sub + base, scaled[r], 0.0)
        if end < n:
            rest = []
            for r in range(q):
                row = jnp.where((lane >= end) | (lane <= sub + base), scaled[r], 0.0)
                h, m, l = parts(row)
                update = tdot(
                    jnp.concatenate([h, h, h, m, m, l], 0), jnp.concatenate([h, m, l, h, m, h], 0)
                )[end:, :]
                low = t[r, PANEL:, :]
                lanes = lax.broadcasted_iota(jnp.int32, low.shape, 1)
                rest.append(jnp.where((lanes >= base) & (lanes < end), 0.0, low) - update)
            t = jnp.stack(rest)
            between(panel)


def penalty(w_ref, r, lab):
    total = jnp.zeros(lab.shape, jnp.float32)
    for g in range(GROUPS):
        total = jnp.where(lab == g, w_ref[r, g], total)
    return total


def tdot(a, b):
    return lax.dot_general(a, b, (((0,), (0,)), ((), ())), preferred_element_type=jnp.float32)


def stack_left(x):
    h, m, l = parts(x)
    return jnp.concatenate([h, h, h, m, m, l], axis=1)


def stack_right(x, axis):
    h, m, l = parts(x)
    return jnp.concatenate([h, m, l, h, m, h], axis=axis)


def dot(a, b):
    return jnp.dot(a, b, preferred_element_type=jnp.float32)


def dot_nt(a, b):
    return lax.dot_general(a, b, (((1,), (1,)), ((), ())), preferred_element_type=jnp.float32)


def solve_kernel(
    weights_hbm, choice_hbm, labc_hbm, at_ref, st_ref, grs_ref, grc_ref, gsc_ref, y_ref, labs_ref, inv_ref,
    trail_ref, sides_ref, weights_ref, choice_ref, labc_ref, sem,
):
    small = [
        pltpu.make_async_copy(weights_hbm, weights_ref, sem.at[0]),
        pltpu.make_async_copy(choice_hbm, choice_ref, sem.at[1]),
        pltpu.make_async_copy(labc_hbm, labc_ref, sem.at[2]),
    ]
    for copy in small:
        copy.start()
    t, f, v = lax.axis_index("tm"), lax.axis_index("feat"), lax.axis_index("vox")
    row = t * 2 + f
    rows, voxels = sides_ref.shape
    y = y_ref[...]
    sside = dot(st_ref[...], y) * (1.0 / math.sqrt(TIME))
    sside6 = stack_right(sside, 0)
    for copy in small:
        copy.wait()

    eye = lax.broadcasted_iota(jnp.int32, (CB, CB), 0) == lax.broadcasted_iota(jnp.int32, (CB, CB), 1)
    r_sub = lax.broadcasted_iota(jnp.int32, (rows, CB), 0) + row * rows
    r_lane = lax.broadcasted_iota(jnp.int32, (rows, CB), 1)
    group = lax.broadcasted_iota(jnp.int32, (1, voxels), 1) // GROUP
    ridge = jnp.zeros((1, voxels), jnp.int32)
    for g in range(voxels // GROUP):
        ridge = jnp.where(group == g, choice_ref[g], ridge)

    panels, solved = [], []
    for r in range(2):
        inv = inv_ref[r]
        left = stack_left(inv)
        pen_s = jnp.broadcast_to(penalty(weights_ref, r, labs_ref[...]), (rows, CB))
        pen_c = jnp.broadcast_to(penalty(weights_ref, r, labc_ref[...]), (rows, CB))
        grs_r = grs_ref[...] + jnp.where(r_sub == r_lane, pen_s, 0.0)
        gsc_r = gsc_ref[...] + jnp.where(eye & (v == 0), pen_c[:CB], 0.0)
        panel = stack_left(dot_nt(stack_left(grs_r), stack_right(inv, 1)))
        partner = dot(left, stack_right(gsc_r, 0))
        system = grc_ref[...] + jnp.where(r_sub == r_lane + v * CB, pen_c, 0.0)
        trail_ref[r] = system - dot(panel, stack_right(partner, 0))
        panels.append(panel)
        solved.append(jnp.where(ridge == r, dot(left, sside6), 0.0))
    update = dot(
        jnp.concatenate(panels, 1), jnp.concatenate([stack_right(solved[0], 0), stack_right(solved[1], 0)], 0)
    )
    sides_ref[...] = dot(at_ref[...], y) * (1.0 / math.sqrt(TIME)) - update

    @pl.when(row == 0)
    def _():
        sides_ref[0:CB, :] = solved[0] + solved[1]


def solve(weights, choice, labc, at, st, grs, grc, gsc, y, labs, inv):
    vmem = pl.BlockSpec(memory_space=pltpu.VMEM)
    hbm = pl.BlockSpec(memory_space=pltpu.HBM)
    rows, voxels = at.shape[0], y.shape[1]
    return pl.pallas_call(
        solve_kernel,
        out_shape=[
            jax.ShapeDtypeStruct((2, rows, CB), jnp.float32),
            jax.ShapeDtypeStruct((rows, voxels), jnp.float32),
        ],
        in_specs=[hbm] * 3 + [vmem] * 8,
        out_specs=[vmem] * 2,
        scratch_shapes=[
            pltpu.SMEM(weights.shape, jnp.float32),
            pltpu.SMEM(choice.shape, jnp.int32),
            pltpu.VMEM((1, CB), jnp.int32),
            pltpu.SemaphoreType.DMA((3,)),
        ],
        compiler_params=pltpu.CompilerParams(vmem_limit_bytes=32 << 20),
        name="solve",
    )(*in_hbm(weights, choice, labc), at, st, grs, grc, gsc, y, labs, inv)


def local(design, signals, label, weights, choice):
    lab = label.reshape(1, CB)
    at, st, grs, grc, gsc, y, labs, inv = gather(design, signals, lab, weights)
    return solve(weights, choice, lab, at, st, grs, grc, gsc, y, labs, inv)


def solution(mesh):
    return jax.shard_map(
        local,
        mesh=mesh,
        in_specs=(P(None, ("tm", "feat")), P("tm", "vox"), P("vox"), P(), P("vox")),
        out_specs=(P(None, ("tm", "feat"), "vox"), P(("tm", "feat"), "vox")),
        check_vma=False,
    )
```

```python
import math

import jax
import jax.numpy as jnp
from jax import lax
from jax.experimental import pallas as pl
from jax.experimental.pallas import tpu as pltpu
from jax.sharding import PartitionSpec as P

TIME = 1024
GROUPS = 4
CB = 128
GROUP = 64
OFFSETS = [(dy, dx) for dy in range(2) for dx in range(4)][1:]
MESH = pl.DeviceIdType.MESH


def peer(t, dy, dx):
    y, x = t // 4, t % 4
    return ((y + dy) % 2) * 4 + (x + dx) % 4


def remote(src, dst, send, recv, **where):
    return pltpu.make_async_remote_copy(
        src_ref=src, dst_ref=dst, send_sem=send, recv_sem=recv, device_id=where, device_id_type=MESH
    )


class Spread:
    def __init__(self, buf, t, f, to, fo, sem):
        self.buf, self.t, self.f, self.to = buf, t, f, to
        self.scatter, self.scatter_r, self.own, self.own_r, self.ag, self.ag_r, self.sib, self.sib_r = sem
        on = f == fo
        self.owner = (self.t == to) & on
        self.relay = (self.t != to) & on
        self.side = (self.t != to) & jnp.logical_not(on)
        self.owner_side = (self.t == to) & jnp.logical_not(on)

    def chunk(self, t):
        return self.buf.at[pl.ds(pl.multiple_of(t * 128, 128), 128), :]

    def c_scatter(self, k):
        p = peer(self.t, *OFFSETS[k])
        c = self.chunk(p)
        return remote(c, c, self.scatter.at[k], self.scatter_r, tm=p)

    def c_scatter_in(self):
        c = self.chunk(self.t)
        return remote(c, c, self.scatter.at[0], self.scatter_r, tm=self.to)

    def c_own(self, k):
        p = peer(self.t, *OFFSETS[k])
        c = self.chunk(self.t)
        return remote(c, c, self.own.at[k], self.own_r, tm=p)

    def c_own_in(self):
        c = self.chunk(self.to)
        return remote(c, c, self.own.at[0], self.own_r, tm=self.to)

    def c_ag(self, k):
        p = peer(self.t, *OFFSETS[k])
        c = self.chunk(self.t)
        return p, remote(c, c, self.ag.at[k], self.ag_r.at[k], tm=p)

    def c_ag_in(self, k):
        dy, dx = OFFSETS[k]
        p = peer(self.t, dy, 4 - dx)
        c = self.chunk(p)
        return p, remote(c, c, self.ag.at[k], self.ag_r.at[k], tm=p)

    def c_sib(self, k, p):
        c = self.chunk(p)
        return remote(c, c, self.sib.at[k], self.sib_r.at[k], feat=1 - self.f)

    def c_whole(self):
        return remote(self.buf, self.buf, self.sib.at[0], self.sib_r.at[0], feat=1 - self.f)

    def scatter_from(self, source):
        for k in range(7):
            p = peer(self.t, *OFFSETS[k])
            rows = source.at[pl.ds(pl.multiple_of(p * 128, 128), 128), pl.ds(0, CB)]
            remote(rows, self.chunk(p), self.scatter.at[k], self.scatter_r, tm=p).start()

    def start(self, scattered):
        @pl.when(self.owner & jnp.logical_not(scattered))
        def _():
            for k in range(7):
                self.c_scatter(k).start()

        @pl.when(self.owner)
        def _():
            for k in range(7):
                self.c_own(k).start()
            self.c_whole().start()

    def forward(self):
        @pl.when(self.relay)
        def _():
            self.c_scatter_in().wait_recv()
            for k in range(7):
                p, c = self.c_ag(k)

                @pl.when(p != self.to)
                def _():
                    c.start()

            self.c_sib(7, self.t).start()

    def collect(self):
        @pl.when(self.relay)
        def _():
            for k in range(7):
                p, c = self.c_ag_in(k)

                @pl.when(p != self.to)
                def _():
                    c.wait_recv()

                @pl.when(p == self.to)
                def _():
                    self.c_own_in().wait_recv()

                self.c_sib(k, p).start()

    def arrive(self):
        @pl.when(self.owner_side)
        def _():
            self.c_whole().wait_recv()

        @pl.when(self.side)
        def _():
            for k in range(7):
                dy, dx = OFFSETS[k]
                self.c_sib(k, peer(self.t, dy, 4 - dx)).wait_recv()
            self.c_sib(7, self.t).wait_recv()

    def finish(self):
        @pl.when(self.owner)
        def _():
            for k in range(7):
                self.c_scatter(k).wait_send()
                self.c_own(k).wait_send()
            self.c_whole().wait_send()

        @pl.when(self.relay)
        def _():
            for k in range(7):
                p, c = self.c_ag(k)

                @pl.when(p != self.to)
                def _():
                    c.wait_send()

                q, _c = self.c_ag_in(k)
                self.c_sib(k, q).wait_send()
            self.c_sib(7, self.t).wait_send()


def spread_sems():
    dma = pltpu.SemaphoreType.DMA
    return [dma((7,)), dma, dma((7,)), dma, dma((7,)), dma((7,)), dma((8,)), dma((8,))]


def gather_kernel(
    a_hbm, y_ref, lab_ref, w_hbm,
    at_ref, st_ref, grs_ref, grc_ref, gsc_ref, yall_ref, labs_ref, inv_ref,
    w_ref, a_ref, s_ref, c_ref, *sems,
):
    s_sem, c_sem, rest = sems[:8], sems[8:16], sems[16:]
    ysend, yrecv, bsend, brecv, lsend, lrecv, copy_sem, ready = rest
    t, f, v = lax.axis_index("tm"), lax.axis_index("feat"), lax.axis_index("vox")
    row = t * 2 + f
    to, fo = v // 4, (v // 2) % 2
    other = v != 0
    server = (v == 0) & (f == 1)
    owner_s, owner_c = row == 0, other & (t == to) & (f == fo)
    last_in = (v == 0) & (row == 0)
    barrier = pltpu.get_barrier_semaphore()

    def signal(**where):
        pl.semaphore_signal(barrier, inc=1, device_id=where, device_id_type=MESH)

    for offset in OFFSETS:
        signal(tm=peer(t, *offset))
    signal(feat=1 - f)

    first = jnp.where(t == 0, 16, 0)

    def client(i):
        return dict(tm=i // 2 % 8, feat=i % 2, vox=t * 4 + i // 16)

    @pl.when(server)
    def _():
        @pl.loop(first, 64)
        def _(i):
            signal(**client(i))

    get_s = pltpu.make_async_copy(a_hbm.at[:, pl.ds(0, CB)], s_ref, copy_sem.at[0])
    get_c = pltpu.make_async_copy(
        a_hbm.at[:, pl.ds(pl.multiple_of((v % 2) * CB, CB), CB)], c_ref, copy_sem.at[1]
    )
    get_y = pltpu.make_async_copy(
        y_ref, yall_ref.at[pl.ds(pl.multiple_of(t * 128, 128), 128), :], copy_sem.at[2]
    )
    get_lab = pltpu.make_async_copy(lab_ref, labs_ref, copy_sem.at[3])
    get_w = pltpu.make_async_copy(w_hbm, w_ref, copy_sem.at[4])
    get_a = pltpu.make_async_copy(a_hbm, a_ref, copy_sem.at[5])

    @pl.when(owner_s)
    def _():
        get_s.start()

    @pl.when(owner_c)
    def _():
        get_c.start()

    spread_s = Spread(s_ref, t, f, 0, 0, s_sem)
    spread_c = Spread(c_ref, t, f, to, fo, c_sem)

    @pl.when(last_in)
    def _():
        pl.semaphore_wait(barrier, 8)
        spread_s.scatter_from(a_hbm)

    get_y.start()
    get_w.start()
    get_a.start()

    @pl.when(v == 0)
    def _():
        get_lab.start()
        get_lab.wait()

    @pl.when(owner_s)
    def _():
        get_s.wait()

    @pl.when(owner_c)
    def _():
        get_c.wait()

    get_y.wait()
    get_w.wait()

    def transpose():
        get_a.wait()
        at_ref[...] = a_ref[...].T

    @pl.when(jnp.logical_not(last_in))
    def _():
        transpose()

    @pl.when((v == 0) & jnp.logical_not(last_in))
    def _():
        pl.semaphore_wait(barrier, 8)

    @pl.when(other)
    def _():
        pl.semaphore_wait(barrier, 9)
        pl.semaphore_signal(
            ready, inc=1, device_id={"tm": v // 4, "feat": 1, "vox": 0}, device_id_type=MESH
        )

    def c_lab(i):
        return remote(labs_ref, labs_ref, lsend.at[i], lrecv, **client(i))


    def c_do(name, *args):
        @pl.when(other)
        def _():
            getattr(spread_c, name)(*args)

    spread_s.start(last_in)
    c_do("start", False)

    def yblock(q, g):
        return yall_ref.at[pl.ds(pl.multiple_of(q * 128 + g * 64, 64), 64), :]

    def source(k):
        dy, dx = OFFSETS[k]
        return peer(t, dy, 4 - dx)

    def c_y(k, b):
        return remote(b, b, ysend.at[k], yrecv.at[k], tm=peer(t, *OFFSETS[k]))

    def c_yout(k, b):
        return remote(b, b, bsend.at[k], brecv.at[k], feat=1 - f)

    def y_start(ks):
        for k in ks:
            c_y(k, yblock(t, f)).start()

    def y_collect(ks):
        for k in ks:
            b = yblock(source(k), f)
            c_y(k, b).wait_recv()
            c_yout(k, b).start()

    @pl.when(last_in)
    def _():
        transpose()

    spread_s.forward()
    c_do("forward")
    y_start((0, 2, 3, 1, 4, 6, 5))

    @pl.when(server & (t != 0))
    def _():
        pl.semaphore_wait(ready, 64)

    @pl.when(server & (t == 0))
    def _():
        pl.semaphore_wait(ready, 48)

    @pl.when(server)
    def _():
        @pl.loop(first, 64)
        def _(i):
            c_lab(i).start()


    spread_s.collect()
    spread_s.arrive()

    @pl.when(other)
    def _():
        c_lab(0).wait_recv()

    s_all = s_ref[...]
    st_ref[...] = s_all.T
    gram = dot(st_ref[...], s_all) * (1.0 / TIME)
    eye = lax.broadcasted_iota(jnp.int32, (CB, CB), 0) == lax.broadcasted_iota(jnp.int32, (CB, CB), 1)
    matrices = []
    for r in range(2):
        pen = jnp.broadcast_to(penalty(w_ref, r, labs_ref[...]), (CB, CB))
        matrices.append(gram + jnp.where(eye, pen, 0.0))

    def between(panel):
        if panel == 0:
            c_do("collect")
        elif panel == 1:
            y_collect((0, 2, 3))
        elif panel == 2:
            y_collect((1, 4, 6, 5))

    inverse_factor(jnp.stack(matrices), inv_ref, between)
    grs = dot(at_ref[...], s_all) * (1.0 / TIME)
    grs_ref[...] = grs
    c_do("arrive")

    @pl.when(v == 0)
    def _():
        grc_ref[...] = grs
        gsc_ref[...] = gram

    @pl.when(other)
    def _():
        c_all = c_ref[...]
        grc_ref[...] = dot(at_ref[...], c_all) * (1.0 / TIME)
        gsc_ref[...] = dot(st_ref[...], c_all) * (1.0 / TIME)

    spread_s.finish()
    c_do("finish")

    for k in range(7):
        c_y(k, yblock(t, f)).wait_send()
        c_yout(k, yblock(source(k), f)).wait_send()
        c_yout(k, yblock(source(k), 1 - f)).wait_recv()

    @pl.when(server)
    def _():
        @pl.loop(first, 64)
        def _(i):
            c_lab(i).wait_send()


def in_hbm(*arrays):
    return [pltpu.with_memory_space_constraint(x, pltpu.HBM) for x in arrays]


def gather(a, y, lab, w):
    dma = pltpu.SemaphoreType.DMA
    vmem = pl.BlockSpec(memory_space=pltpu.VMEM)
    hbm = pl.BlockSpec(memory_space=pltpu.HBM)
    rows, voxels = a.shape[1], y.shape[1]
    return pl.pallas_call(
        gather_kernel,
        out_shape=[
            jax.ShapeDtypeStruct((rows, TIME), jnp.bfloat16),
            jax.ShapeDtypeStruct((CB, TIME), jnp.bfloat16),
            jax.ShapeDtypeStruct((rows, CB), jnp.float32),
            jax.ShapeDtypeStruct((rows, CB), jnp.float32),
            jax.ShapeDtypeStruct((CB, CB), jnp.float32),
            jax.ShapeDtypeStruct((TIME, voxels), jnp.bfloat16),
            jax.ShapeDtypeStruct((1, CB), jnp.int32),
            jax.ShapeDtypeStruct((2, CB, CB), jnp.float32),
        ],
        in_specs=[hbm] * 4,
        out_specs=[vmem] * 8,
        scratch_shapes=[
            pltpu.SMEM(w.shape, jnp.float32),
            pltpu.VMEM(a.shape, jnp.bfloat16),
            pltpu.VMEM((TIME, CB), jnp.bfloat16),
            pltpu.VMEM((TIME, CB), jnp.bfloat16),
        ]
        + spread_sems()
        + spread_sems()
        + [dma((7,)), dma((7,)), dma((7,)), dma((7,)), dma((64,)), dma, dma((6,))]
        + [pltpu.SemaphoreType.REGULAR],
        compiler_params=pltpu.CompilerParams(
            collective_id=0, has_side_effects=True, vmem_limit_bytes=24 << 20
        ),
        name="gather",
    )(*in_hbm(a, y, lab, w))


PANEL = 32


def eliminate(t, base):
    q, height, n = t.shape
    lane8 = lax.broadcasted_iota(jnp.int32, (q, 8, n), 2)
    sub8 = lax.broadcasted_iota(jnp.int32, (q, 8, n), 1)
    out = []
    for step in range(height // 8):
        o = base + 8 * step
        block = t[:, :8, :]
        cols = [jnp.broadcast_to(block[:, :, o + p : o + p + 1], (q, 8, n)) for p in range(8)]
        inside = (lane8 >= o) & (lane8 < o + 8)
        block = jnp.where(inside, jnp.where(lane8 == o + sub8, 1.0, 0.0), block)
        invs, rrows, crows = [], [], []
        scale = jnp.zeros((q, 8, n), jnp.float32)
        for p in range(8):
            crow = {k: jnp.broadcast_to(cols[k][:, p : p + 1, :], (q, 8, n)) for k in range(p, 8)}
            rrow = jnp.broadcast_to(block[:, p : p + 1, :], (q, 8, n))
            inv = 1.0 / crow[p]
            scale = jnp.where(sub8 == p, lax.rsqrt(crow[p]), scale)
            factor = jnp.where(sub8 > p, cols[p] * inv, 0.0)
            block = block - factor * rrow
            for k in range(p + 1, 8):
                cols[k] = cols[k] - factor * crow[k]
            invs.append(inv)
            rrows.append(rrow)
            crows.append(crow)
        out.append(block * scale)
        rest = t.shape[1] - 8
        if rest:
            low = t[:, 8:, :].reshape(q, rest // 8, 8, n)
            cols = [
                jnp.broadcast_to(low[:, :, :, o + p : o + p + 1], (q, rest // 8, 8, n)) for p in range(8)
            ]
            lane = lax.broadcasted_iota(jnp.int32, low.shape, 3)
            low = jnp.where((lane >= o) & (lane < o + 8), 0.0, low)
            for p in range(8):
                factor = cols[p] * invs[p][:, None]
                low = low - factor * rrows[p][:, None]
                for k in range(p + 1, 8):
                    cols[k] = cols[k] - factor * crows[p][k][:, None]
            t = low.reshape(q, rest, n)
    return jnp.concatenate(out, axis=1)


def parts(x):
    high = x.astype(jnp.bfloat16)
    rest = x - high.astype(jnp.float32)
    mid = rest.astype(jnp.bfloat16)
    low = (rest - mid.astype(jnp.float32)).astype(jnp.bfloat16)
    return high, mid, low


def inverse_factor(t, out_ref, between):
    q, n, _ = t.shape
    lane = lax.broadcasted_iota(jnp.int32, (PANEL, n), 1)
    sub = lax.broadcasted_iota(jnp.int32, (PANEL, n), 0)
    for panel in range(n // PANEL):
        base, end = panel * PANEL, (panel + 1) * PANEL
        scaled = eliminate(t[:, :PANEL, :], base)
        for r in range(q):
            out_ref[r, base:end, :] = jnp.where(lane <= sub + base, scaled[r], 0.0)
        if end < n:
            rest = []
            for r in range(q):
                row = jnp.where((lane >= end) | (lane <= sub + base), scaled[r], 0.0)
                h, m, l = parts(row)
                update = tdot(
                    jnp.concatenate([h, h, h, m, m, l], 0), jnp.concatenate([h, m, l, h, m, h], 0)
                )[end:, :]
                low = t[r, PANEL:, :]
                lanes = lax.broadcasted_iota(jnp.int32, low.shape, 1)
                rest.append(jnp.where((lanes >= base) & (lanes < end), 0.0, low) - update)
            t = jnp.stack(rest)
            between(panel)


def penalty(w_ref, r, lab):
    total = jnp.zeros(lab.shape, jnp.float32)
    for g in range(GROUPS):
        total = jnp.where(lab == g, w_ref[r, g], total)
    return total


def tdot(a, b):
    return lax.dot_general(a, b, (((0,), (0,)), ((), ())), preferred_element_type=jnp.float32)


def stack_left(x):
    h, m, l = parts(x)
    return jnp.concatenate([h, h, h, m, m, l], axis=1)


def stack_right(x, axis):
    h, m, l = parts(x)
    return jnp.concatenate([h, m, l, h, m, h], axis=axis)


def dot(a, b):
    return jnp.dot(a, b, preferred_element_type=jnp.float32)


def dot_nt(a, b):
    return lax.dot_general(a, b, (((1,), (1,)), ((), ())), preferred_element_type=jnp.float32)


def solve_kernel(
    weights_hbm, choice_hbm, labc_hbm, at_ref, st_ref, grs_ref, grc_ref, gsc_ref, y_ref, labs_ref, inv_ref,
    trail_ref, sides_ref, weights_ref, choice_ref, labc_ref, sem,
):
    small = [
        pltpu.make_async_copy(weights_hbm, weights_ref, sem.at[0]),
        pltpu.make_async_copy(choice_hbm, choice_ref, sem.at[1]),
        pltpu.make_async_copy(labc_hbm, labc_ref, sem.at[2]),
    ]
    for copy in small:
        copy.start()
    t, f, v = lax.axis_index("tm"), lax.axis_index("feat"), lax.axis_index("vox")
    row = t * 2 + f
    rows, voxels = sides_ref.shape
    y = y_ref[...]
    sside = dot(st_ref[...], y) * (1.0 / math.sqrt(TIME))
    sside6 = stack_right(sside, 0)
    for copy in small:
        copy.wait()

    eye = lax.broadcasted_iota(jnp.int32, (CB, CB), 0) == lax.broadcasted_iota(jnp.int32, (CB, CB), 1)
    r_sub = lax.broadcasted_iota(jnp.int32, (rows, CB), 0) + row * rows
    r_lane = lax.broadcasted_iota(jnp.int32, (rows, CB), 1)
    group = lax.broadcasted_iota(jnp.int32, (1, voxels), 1) // GROUP
    ridge = jnp.zeros((1, voxels), jnp.int32)
    for g in range(voxels // GROUP):
        ridge = jnp.where(group == g, choice_ref[g], ridge)

    panels, solved = [], []
    for r in range(2):
        inv = inv_ref[r]
        left = stack_left(inv)
        pen_s = jnp.broadcast_to(penalty(weights_ref, r, labs_ref[...]), (rows, CB))
        pen_c = jnp.broadcast_to(penalty(weights_ref, r, labc_ref[...]), (rows, CB))
        grs_r = grs_ref[...] + jnp.where(r_sub == r_lane, pen_s, 0.0)
        gsc_r = gsc_ref[...] + jnp.where(eye & (v == 0), pen_c[:CB], 0.0)
        panel = stack_left(dot_nt(stack_left(grs_r), stack_right(inv, 1)))
        partner = dot(left, stack_right(gsc_r, 0))
        system = grc_ref[...] + jnp.where(r_sub == r_lane + v * CB, pen_c, 0.0)
        trail_ref[r] = system - dot(panel, stack_right(partner, 0))
        panels.append(panel)
        solved.append(jnp.where(ridge == r, dot(left, sside6), 0.0))
    update = dot(
        jnp.concatenate(panels, 1), jnp.concatenate([stack_right(solved[0], 0), stack_right(solved[1], 0)], 0)
    )
    sides_ref[...] = dot(at_ref[...], y) * (1.0 / math.sqrt(TIME)) - update

    @pl.when(row == 0)
    def _():
        sides_ref[0:CB, :] = solved[0] + solved[1]


def solve(weights, choice, labc, at, st, grs, grc, gsc, y, labs, inv):
    vmem = pl.BlockSpec(memory_space=pltpu.VMEM)
    hbm = pl.BlockSpec(memory_space=pltpu.HBM)
    rows, voxels = at.shape[0], y.shape[1]
    return pl.pallas_call(
        solve_kernel,
        out_shape=[
            jax.ShapeDtypeStruct((2, rows, CB), jnp.float32),
            jax.ShapeDtypeStruct((rows, voxels), jnp.float32),
        ],
        in_specs=[hbm] * 3 + [vmem] * 8,
        out_specs=[vmem] * 2,
        scratch_shapes=[
            pltpu.SMEM(weights.shape, jnp.float32),
            pltpu.SMEM(choice.shape, jnp.int32),
            pltpu.VMEM((1, CB), jnp.int32),
            pltpu.SemaphoreType.DMA((3,)),
        ],
        compiler_params=pltpu.CompilerParams(vmem_limit_bytes=32 << 20),
        name="solve",
    )(*in_hbm(weights, choice, labc), at, st, grs, grc, gsc, y, labs, inv)


def local(design, signals, label, weights, choice):
    lab = label.reshape(1, CB)
    at, st, grs, grc, gsc, y, labs, inv = gather(design, signals, lab, weights)
    return solve(weights, choice, lab, at, st, grs, grc, gsc, y, labs, inv)


def solution(mesh):
    return jax.shard_map(
        local,
        mesh=mesh,
        in_specs=(P(None, ("tm", "feat")), P("tm", "vox"), P("vox"), P(), P("vox")),
        out_specs=(P(None, ("tm", "feat"), "vox"), P(("tm", "feat"), "vox")),
        check_vma=False,
    )
```
